32 devices in a mesh: ep: 8 (over z, y), fs: 4 (over x, core).
Axes of the slice: x: 2, y: 2, z: 4, core: 2. Of those that a mesh axis runs over, the one named last changes fastest.
Arguments:
- tokens: bfloat16 [8192, 768], P(('ep', 'fs')), may hold values from -6 to 6
- cotangent: bfloat16 [8192, 768], P(('ep', 'fs')), may hold values from -6 to 6
- routes: int32 [8192, 2], P(('ep', 'fs')), may hold values from 0 to 15, all different within a row; in each aligned block of 256 rows (0 to 255, 256 to 511, ...) at most 48 rows name the same one
- priority: int32 [8192], P(('ep', 'fs')), may hold values 0 or 1
- gain_attn: bfloat16 [768], P('fs'), may hold values from 0.25 to 1.75
- w_query: bfloat16 [768, 768], P('fs'), may hold values from -0.21875 to 0.21875
- w_key: bfloat16 [768, 768], P('fs'), may hold values from -0.21875 to 0.21875
- w_value: bfloat16 [768, 768], P('fs'), may hold values from -0.21875 to 0.21875
- w_out: bfloat16 [768, 768], P('fs'), may hold values from -0.875 to 0.875
- gain_ffn: bfloat16 [768], P('fs'), may hold values from 0.25 to 1.75
- w_shared_gate: bfloat16 [768, 2048], P('fs'), may hold values from -0.21875 to 0.21875
- w_shared_up: bfloat16 [768, 2048], P('fs'), may hold values from -0.21875 to 0.21875
- w_shared_down: bfloat16 [2048, 768], P('fs'), may hold values from -0.125 to 0.125
- w_router: bfloat16 [768, 16], P('fs'), may hold values from -0.15625 to 0.15625
- w_expert_gate: bfloat16 [768, 32768], P(None, ('ep', 'fs')), may hold values from -0.21875 to 0.21875
- w_expert_up: bfloat16 [768, 32768], P(None, ('ep', 'fs')), may hold values from -0.21875 to 0.21875
- w_expert_down: bfloat16 [32768, 768], P(('ep', 'fs')), may hold values from -0.125 to 0.125
Outputs:
- output: bfloat16 [8192, 768], P(('ep', 'fs'))
- grad_tokens: float32 [8192, 768], P(('ep', 'fs'))
- grad_gain_attn: float32 [768], P('fs')
- grad_w_query: float32 [768, 768], P('fs')
- grad_w_key: float32 [768, 768], P('fs')
- grad_w_value: float32 [768, 768], P('fs')
- grad_w_out: float32 [768, 768], P('fs')
- grad_gain_ffn: float32 [768], P('fs')
- grad_w_shared_gate: float32 [768, 2048], P('fs')
- grad_w_shared_up: float32 [768, 2048], P('fs')
- grad_w_shared_down: float32 [2048, 768], P('fs')
- grad_w_router: float32 [768, 16], P('fs')
- grad_w_expert_gate: float32 [768, 32768], P(None, ('ep', 'fs'))
- grad_w_expert_up: float32 [768, 32768], P(None, ('ep', 'fs'))
- grad_w_expert_down: float32 [32768, 768], P(('ep', 'fs'))
The draws below stay inside these ranges and needn't reach their ends.
Inputs may be any that keep to these rules, and one draw needn't show every extreme that they name: The two routes of a token differ; among the 256 tokens of one device no expert is named by more than 48 tokens, and in some device's tokens one is named by exactly 48. Route priority[t] of token t is its first choice.
All inputs are finite; a program needn't handle non-finite values. No bound on the sum of `priority` on one device may be relied on, other than what follows from the above.
Results may differ from the reference program's by a relative error of at most 0.02.
Values may be sent and summed in bfloat16 or wider, within the bound.
No kernel may reach another device: no remote copies, remote signals or barrier semaphores. Data moves between devices by JAX's collectives and lax.ppermute only.
A program may use at most 192 MiB of HBM per device.

```python
import math
import jax
import jax.numpy as jnp
import numpy as np
from jax import lax

D = 768
HEADS = 12
HEAD_DIM = 64
FF = 2048
EXPERTS = 16
EH = 2048
TOP = 2
TOK_DEV = 256
LENGTH = 1024
TOKENS = 8192
MOST = 48
CAP = 1280


def place_ends(array, stream_key, least, high):
    longest = array.shape.index(max(array.shape))
    spots = []
    for shift in (0, 1):
        where = [jax.random.randint(jax.random.fold_in(stream_key, axis), (), 0, length) for axis, length in enumerate(array.shape)]
        where[longest] = (where[longest] + shift) % array.shape[longest]
        spots.append(tuple(where))
    return array.at[spots[0]].set(least).at[spots[1]].set(high)


def block_levels(key, shape, cuts, least, largest):
    gain = 1.0
    for axis_at, parts in cuts:
        steps = jax.random.uniform(jax.random.fold_in(jax.random.fold_in(key, 6), axis_at), (parts,), jnp.float32, least / len(cuts), largest / len(cuts))
        gain = gain * jnp.repeat(jnp.exp(steps), shape[axis_at] // parts).reshape((-1,) + (1,) * (len(shape) - 1 - axis_at))
    return gain


def assign_block(stream_key, own, number, rows, amount, top, bound, slope):
    order = jax.random.permutation(stream_key, amount)
    packed, usual = portions_of(amount, rows * top, bound, slope, True), portions_of(amount, rows * top, bound, slope, False)
    places = jnp.arange(amount)

    def named(tallies, rotation):
        used = int((tallies > 0).sum())
        fixed = max(1, used // 4)
        passed = fixed + (places - fixed + rotation * (used - fixed)) % max(1, amount - fixed)
        return jnp.zeros((amount,), jnp.int32).at[order[jnp.where(places < fixed, places, passed)]].set(jnp.asarray(tallies, jnp.int32))

    tallies = jnp.where(number % 4 == 0, named(packed, number // 4), named(usual, number - number // 4 - 1))
    mixed = jax.random.permutation(jax.random.fold_in(own, 3), amount)
    giver, sink = mixed[0:amount // 2 * 2:2], mixed[1:amount // 2 * 2:2]
    slack = jnp.minimum(tallies[giver] - 1, bound - tallies[sink]) // 2
    slack = jnp.where((giver == order[0]) | (sink == order[0]) | (tallies[sink] == 0), 0, jnp.maximum(slack, 0))
    passed = jax.random.randint(jax.random.fold_in(own, 4), (amount // 2,), 0, 1 << 20) % (slack + 1)
    tallies = tallies.at[giver].add(-passed).at[sink].add(passed)
    items = jnp.searchsorted(jnp.cumsum(tallies), jnp.arange(rows * top), side="right").astype(jnp.int32)
    listing = items.reshape(top, rows).T
    listing = listing[jax.random.permutation(jax.random.fold_in(own, 1), rows)]
    rotation = jax.random.randint(jax.random.fold_in(own, 2), (rows, 1), 0, top)
    return jnp.take_along_axis(listing, (jnp.arange(top)[None, :] + rotation) % top, axis=1)


def portions_of(number_of, total, reach, slope, full):
    loads = [(1 << 20) // math.isqrt(grade ** slope) + 1 for grade in range(1, number_of + 1)]
    largest = reach if full else min(reach, max(-(-total // number_of), total * loads[0] // sum(loads)))
    least = 1 if total - largest >= number_of - 1 else 0
    holding, rest = [largest] + [least] * (number_of - 1), total - largest - least * (number_of - 1)
    while rest > 0:
        free = [i for i in range(1, number_of) if holding[i] < largest] or [i for i in range(1, number_of) if holding[i] < reach]
        pool, left = sum([loads[i] for i in free]), rest
        for i in free:
            addition = min(reach - holding[i], max(1, left * loads[i] // pool), rest)
            holding[i] = holding[i] + addition
            rest = rest - addition
    return np.array(holding)


def gaussian(key, dims, width, reach, cuts=(), kind=jnp.bfloat16):
    result = jax.random.normal(key, dims, jnp.float32) * width
    if len(cuts) > 0:
        result = block_levels(key, dims, cuts, -0.22, 0.18) * result
    return jnp.clip(result, min=-reach, max=reach).astype(kind)


def setup_inputs(seed: int = 0) -> dict:
    keys = jax.random.split(jax.random.key(seed), 18)
    tokens = gaussian(keys[0], (TOKENS, D), 1.0, 6.0, ((0, 32),))
    cotangent = gaussian(keys[1], (TOKENS, D), 1.0, 6.0, ((0, 32),))
    routes_keys = jax.random.split(jax.random.fold_in(keys[2], 1), TOKENS // TOK_DEV)
    routes_turns = jax.random.permutation(jax.random.fold_in(keys[2], 3), TOKENS // TOK_DEV)
    routes = jax.vmap(lambda own, number: assign_block(jax.random.fold_in(keys[2], 2), own, number, TOK_DEV, EXPERTS, TOP, MOST, 1))(routes_keys, routes_turns).reshape((TOKENS, TOP))
    priority = place_ends((jax.random.randint(keys[3], (TOKENS,), 0, 2) < 1).astype(jnp.int32), jax.random.fold_in(keys[3], 1), 0, 1)
    gain_attn = jnp.clip(1.0 + 0.15 * jax.random.normal(keys[4], (D,), jnp.float32), 0.25, 1.75).astype(jnp.bfloat16)
    w_query = gaussian(keys[5], (D, D), D ** -0.5, 0.21875, ((0, 4),))
    w_key = gaussian(keys[6], (D, D), D ** -0.5, 0.21875, ((0, 4),))
    w_value = gaussian(keys[7], (D, D), D ** -0.5, 0.21875, ((0, 4),))
    w_out = gaussian(keys[8], (D, D), (D // 16) ** -0.5, 0.875, ((0, 4),))
    gain_ffn = jnp.clip(1.0 + 0.15 * jax.random.normal(keys[9], (D,), jnp.float32), 0.25, 1.75).astype(jnp.bfloat16)
    w_shared_gate = gaussian(keys[10], (D, FF), D ** -0.5, 0.21875, ((0, 4),))
    w_shared_up = gaussian(keys[11], (D, FF), D ** -0.5, 0.21875, ((0, 4),))
    w_shared_down = gaussian(keys[12], (FF, D), FF ** -0.5, 0.125, ((0, 4),))
    w_router = gaussian(keys[13], (D, EXPERTS), (2 * D) ** -0.5, 0.15625, ((0, 4),))
    w_expert_gate = gaussian(keys[14], (D, EXPERTS * EH), D ** -0.5, 0.21875, ((1, 32),))
    w_expert_up = gaussian(keys[15], (D, EXPERTS * EH), D ** -0.5, 0.21875, ((1, 32),))
    w_expert_down = gaussian(keys[16], (EXPERTS * EH, D), EH ** -0.5, 0.125, ((0, 32),))
    return dict(tokens=tokens, cotangent=cotangent, routes=routes, priority=priority, gain_attn=gain_attn, w_query=w_query, w_key=w_key, w_value=w_value, w_out=w_out, gain_ffn=gain_ffn, w_shared_gate=w_shared_gate, w_shared_up=w_shared_up, w_shared_down=w_shared_down, w_router=w_router, w_expert_gate=w_expert_gate, w_expert_up=w_expert_up, w_expert_down=w_expert_down)


EPS = 1e-06
SCALE = 0.125
NEG = -1e+30

@jax.custom_vjp
def low(v):
    return lax.optimization_barrier(v.astype(jnp.bfloat16)).astype(jnp.float32)

@jax.custom_vjp
def low_back(v):
    return v

def low_keep(v):
    return (low(v), None)

def low_pass(kept, grad):
    return (grad,)

def back_keep(v):
    return (v, None)

def back_low(kept, grad):
    return (low(grad),)
low.defvjp(low_keep, low_pass)
low_back.defvjp(back_keep, back_low)

def matmul(left_op, right_op):
    return jnp.dot(left_op, right_op, precision=lax.Precision.HIGHEST, preferred_element_type=jnp.float32)

def rms_scale(values, gain_vec):
    return values * lax.rsqrt(lax.optimization_barrier(jnp.mean(values * values, -1, keepdims=True)) + EPS) * gain_vec

def rope_tables(positions, half_size):
    freq = jnp.exp(-jnp.log(10000.0) * jnp.arange(half_size).astype(jnp.float32) / half_size)
    angle = positions.astype(jnp.float32)[:, None] * freq[None, :]
    return (jnp.cos(angle), jnp.sin(angle))

def rotate(values, cosine, sine_tab):
    half_size = values.shape[-1] // 2
    first_half, second_half = (values[..., :half_size], values[..., half_size:])
    cosine, sine_tab = (cosine[:, None, :], sine_tab[:, None, :])
    return jnp.concatenate([first_half * cosine - second_half * sine_tab, second_half * cosine + first_half * sine_tab], -1)

def silu_of(values):
    return values * jax.nn.sigmoid(values)

def attend_sequence(seq_block):
    query, keys_all, values_all = seq_block
    length_here = query.shape[0]
    scores = low_back(jnp.einsum('qhd,khd->hqk', query, keys_all, precision=lax.Precision.HIGHEST, preferred_element_type=jnp.float32) * SCALE)
    causal = jnp.arange(length_here)[:, None] >= jnp.arange(length_here)[None, :]
    scores = jnp.where(causal[None], scores, NEG)
    exp_scores = jnp.exp(scores - lax.optimization_barrier(jnp.max(scores, -1, keepdims=True)))
    weights = low(exp_scores / lax.optimization_barrier(jnp.sum(exp_scores, -1, keepdims=True)))
    return jnp.einsum('hqk,khd->qhd', weights, values_all, precision=lax.Precision.HIGHEST, preferred_element_type=jnp.float32)

def routing_tables(routes, priority):
    expert_iota = jnp.arange(EXPERTS).astype(jnp.int32)
    classes = jnp.stack([priority, 1 - priority], 1).astype(jnp.int32)
    route_hits = (routes[:, :, None] == expert_iota).astype(jnp.int32)
    per_class = jnp.stack([lax.optimization_barrier(jnp.sum(route_hits * (classes == class_id)[:, :, None].astype(jnp.int32), 1)).astype(jnp.int32) for class_id in (0, 1)])
    before = (jnp.cumsum(per_class, 1) - per_class).astype(jnp.int32)
    offset = jnp.stack([jnp.zeros((EXPERTS,), jnp.int32), lax.optimization_barrier(jnp.sum(per_class[0], 0)).astype(jnp.int32)])
    global_table = before + offset[:, None, :]
    picked = jnp.where((classes == 0)[:, :, None], global_table[0][:, None, :], global_table[1][:, None, :])
    position = lax.optimization_barrier(jnp.sum(picked * route_hits, -1)).astype(jnp.int32)
    kept_mask = position < CAP
    slot_pos = jnp.where(kept_mask, position, CAP).astype(jnp.int32)
    token_ids = jnp.broadcast_to(jnp.arange(TOKENS).astype(jnp.int32)[:, None], (TOKENS, 2))
    pair_ids = jnp.arange(2 * TOKENS).astype(jnp.int32).reshape(TOKENS, 2)
    token_table = jnp.full((EXPERTS, CAP), TOKENS, jnp.int32).at[routes, slot_pos].set(token_ids, mode='drop')
    pair_table = jnp.full((EXPERTS, CAP), 2 * TOKENS, jnp.int32).at[routes, slot_pos].set(pair_ids, mode='drop')
    return (token_table, pair_table, kept_mask.astype(jnp.float32))

def layer(inputs, params, routes, token_table, pair_table, kept_mask):
    gain_attn, w_query, w_key, w_value, w_out, gain_ffn, w_shared_gate, w_shared_up, w_shared_down, w_router, w_expert_gate, w_expert_up, w_expert_down = params
    attn_in = low(rms_scale(inputs, gain_attn))
    cosine, sine_tab = rope_tables(jnp.arange(TOKENS) % LENGTH, HEAD_DIM // 2)
    head_shape = (TOKENS, HEADS, HEAD_DIM)
    query = low(rotate(low_back(matmul(attn_in, w_query)).reshape(head_shape), cosine, sine_tab))
    keys_all = low(rotate(low_back(matmul(attn_in, w_key)).reshape(head_shape), cosine, sine_tab))
    values_all = low(low_back(matmul(attn_in, w_value))).reshape(head_shape)
    seq_shape = (TOKENS // LENGTH, LENGTH, HEADS, HEAD_DIM)
    attended = lax.map(jax.checkpoint(attend_sequence), (query.reshape(seq_shape), keys_all.reshape(seq_shape), values_all.reshape(seq_shape)))
    attended = low(low_back(attended.reshape(TOKENS, D)))
    residual = inputs + low_back(matmul(attended, w_out))
    ffn_in = low(rms_scale(residual, gain_ffn))
    shared_gate = low_back(matmul(ffn_in, w_shared_gate))
    shared_up = low_back(matmul(ffn_in, w_shared_up))
    shared_out = matmul(low(silu_of(shared_gate) * shared_up), w_shared_down)
    logits = low_back(matmul(ffn_in, w_router))
    chosen = jnp.take_along_axis(logits, routes, 1)
    chosen_exp = jnp.exp(chosen - lax.optimization_barrier(jnp.max(chosen, -1, keepdims=True)))
    gates = chosen_exp / lax.optimization_barrier(jnp.sum(chosen_exp, -1, keepdims=True))
    pair_weight = jnp.concatenate([(gates * kept_mask).reshape(-1), jnp.zeros((1,), jnp.float32)])
    rows_pad = jnp.concatenate([ffn_in, jnp.zeros((1, D), jnp.float32)])
    gate_all = w_expert_gate.reshape(D, EXPERTS, EH).transpose(1, 0, 2)
    up_all = w_expert_up.reshape(D, EXPERTS, EH).transpose(1, 0, 2)
    down_all = w_expert_down.reshape(EXPERTS, EH, D)

    def one_expert(pieces):
        token_ids, pair_ids, gate_mat, up_mat, down_mat = pieces
        row_block = rows_pad[token_ids]
        gate_val = low_back(matmul(row_block, gate_mat))
        up_val = low_back(matmul(row_block, up_mat))
        out_rows = low_back(matmul(low(silu_of(gate_val) * up_val), down_mat))
        return pair_weight[pair_ids][:, None] * out_rows
    stacked = lax.map(jax.checkpoint(one_expert), (token_table, pair_table, gate_all, up_all, down_all))
    mixed = jnp.zeros((TOKENS + 1, D), jnp.float32).at[token_table.reshape(-1)].add(stacked.reshape(-1, D))
    return residual + shared_out + mixed[:TOKENS]

def reference(tokens, cotangent, routes, priority, gain_attn, w_query, w_key, w_value, w_out, gain_ffn, w_shared_gate, w_shared_up, w_shared_down, w_router, w_expert_gate, w_expert_up, w_expert_down):
    token_table, pair_table, kept_mask = routing_tables(routes, priority)
    params = tuple((piece.astype(jnp.float32) for piece in (gain_attn, w_query, w_key, w_value, w_out, gain_ffn, w_shared_gate, w_shared_up, w_shared_down, w_router, w_expert_gate, w_expert_up, w_expert_down)))
    inputs = tokens.astype(jnp.float32)

    def closed(input_vals, param_vals):
        return layer(input_vals, param_vals, routes, token_table, pair_table, kept_mask)
    output, pullback = jax.vjp(closed, inputs, params)
    grad_inputs, grad_params = pullback(cotangent.astype(jnp.float32))
    return (output.astype(jnp.bfloat16), grad_inputs, grad_params[0], grad_params[1], grad_params[2], grad_params[3], grad_params[4], grad_params[5], grad_params[6], grad_params[7], grad_params[8], grad_params[9], grad_params[10], grad_params[11], grad_params[12])
```

```python
import jax
import jax.numpy as jnp
from jax import lax
from jax.sharding import Mesh
from jax.sharding import PartitionSpec as P

HEADS = 12
EXPERTS = 16
MOST = 48

EPS = 1e-06
SCALE = 0.125
NEG = -1e30
LOW = jnp.bfloat16
WIDE = jnp.float32
ALL = ("ep", "fx", "fc")
SEQ = ("fx", "fc")
SWAP = [(0, 1), (1, 0)]


def matmul(left_op, right_op):
    return jnp.dot(left_op, right_op, preferred_element_type=WIDE)


def contract_rows(left_op, right_op):
    return lax.dot_general(left_op, right_op, (((0,), (0,)), ((), ())), preferred_element_type=WIDE)


def contract_cols(left_op, right_op):
    return lax.dot_general(left_op, right_op, (((1,), (1,)), ((), ())), preferred_element_type=WIDE)


def rms_forward(values, gain_vec):
    inverse = lax.rsqrt(jnp.mean(values * values, -1, keepdims=True) + EPS)
    return (values * inverse * gain_vec, inverse)


def rms_backward(upstream, values, inverse, gain_vec):
    scaled = upstream * gain_vec
    return inverse * scaled - values * inverse**3 * jnp.mean(scaled * values, -1, keepdims=True)


def rope_tables(positions, half_size):
    freq = jnp.exp(-jnp.log(10000.0) * jnp.arange(half_size).astype(WIDE) / half_size)
    angle = positions.astype(WIDE)[:, None] * freq[None, :]
    return (jnp.cos(angle), jnp.sin(angle))


def rotate(values, cosine, sine_tab):
    half_size = values.shape[-1] // 2
    first_half, second_half = (values[..., :half_size], values[..., half_size:])
    cosine, sine_tab = (cosine[:, None, :], sine_tab[:, None, :])
    return jnp.concatenate(
        [
            first_half * cosine - second_half * sine_tab,
            second_half * cosine + first_half * sine_tab,
        ],
        -1,
    )


def silu_grad(gate_val):
    sigma = jax.nn.sigmoid(gate_val)
    return (gate_val * sigma, sigma * (1.0 + gate_val * (1.0 - sigma)))


def ordered(own, other, index, axis=0):
    lead = jnp.concatenate([jnp.expand_dims(own, axis), jnp.expand_dims(other, axis)], axis)
    swapped = jnp.concatenate([jnp.expand_dims(other, axis), jnp.expand_dims(own, axis)], axis)
    return jnp.where(index == 0, lead, swapped)


def gather_seq(block):
    far = lax.ppermute(block, "fx", SWAP)
    pair = ordered(block, far, lax.axis_index("fx"))
    near = lax.ppermute(pair, "fc", SWAP)
    quad = ordered(pair, near, lax.axis_index("fc"), 1)
    return quad.reshape((4 * block.shape[0],) + block.shape[1:])


def scatter_seq(total):
    rows = total.shape[0] // 4
    cut = total.reshape((2, 2, rows) + total.shape[1:])
    core, side = (lax.axis_index("fc"), lax.axis_index("fx"))
    keep = lax.dynamic_index_in_dim(cut, core, 1, keepdims=False)
    give = lax.dynamic_index_in_dim(cut, 1 - core, 1, keepdims=False)
    keep = keep + lax.ppermute(give.astype(LOW), "fc", SWAP).astype(WIDE)
    mine = lax.dynamic_index_in_dim(keep, side, 0, keepdims=False)
    give = lax.dynamic_index_in_dim(keep, 1 - side, 0, keepdims=False)
    return mine + lax.ppermute(give.astype(LOW), "fx", SWAP).astype(WIDE)


def exchange(blocks, axes):
    return lax.all_to_all(blocks, axes, split_axis=0, concat_axis=0, tiled=True)


def spread_whole(vector, axes, count):
    return exchange(jnp.broadcast_to(vector[None], (count,) + vector.shape), axes)


def experts_chip(rows_sent, grads_sent, slot_weight, weg, weu, wed):
    width = rows_sent.shape[1]
    axes = ("ep", "fx")
    got_grads = exchange(grads_sent.reshape(EXPERTS, MOST, width), axes).reshape(-1, width)
    gate_mat = jnp.concatenate([weg, lax.ppermute(weg, "fc", SWAP)], 1)
    up_mat = jnp.concatenate([weu, lax.ppermute(weu, "fc", SWAP)], 1)
    down_mat = jnp.concatenate([wed, lax.ppermute(wed, "fc", SWAP)], 0)
    hidden = weg.shape[1]
    grad_hidden = contract_cols(got_grads, down_mat)
    got_weight = exchange(slot_weight.reshape(EXPERTS, MOST), axes).reshape(-1, 1)
    own_rows = exchange(rows_sent.reshape(EXPERTS, MOST, width), axes).reshape(-1, width)
    gate_val = matmul(own_rows, gate_mat)
    up_val = matmul(own_rows, up_mat)
    silu_val, slope_val = silu_grad(gate_val)
    hidden_wide = silu_val * up_val
    hidden_val = hidden_wide.astype(LOW)
    row_dot = jnp.sum(hidden_val.astype(WIDE) * grad_hidden, -1)
    scaled = got_weight * grad_hidden
    grad_gate = (scaled * up_val * slope_val).astype(LOW)
    grad_up = (scaled * silu_val).astype(LOW)
    din_rows = contract_cols(grad_gate, gate_mat) + contract_cols(grad_up, up_mat)
    back_din = exchange(din_rows.astype(LOW).reshape(EXPERTS, MOST, width), axes)
    back_dot = exchange(row_dot.reshape(EXPERTS, MOST), axes)
    out_rows = matmul(hidden_val, down_mat)
    back_out = exchange(out_rows.astype(LOW).reshape(EXPERTS, MOST, width), axes)
    own_grads = (got_weight * got_grads.astype(WIDE)).astype(LOW)

    def finish(full, axis):
        own = lax.slice_in_dim(full, 0, hidden, axis=axis)
        peer = lax.slice_in_dim(full, hidden, 2 * hidden, axis=axis)
        return own + lax.ppermute(peer.astype(LOW), "fc", SWAP).astype(WIDE)

    gate_g = finish(contract_rows(own_rows, grad_gate), 1)
    up_g = finish(contract_rows(own_rows, grad_up), 1)
    down_g = finish(contract_rows(hidden_val, own_grads), 0)
    return (
        back_out.reshape(-1, width),
        back_din.reshape(-1, width),
        back_dot.reshape(-1),
        gate_g,
        up_g,
        down_g,
    )


def experts_spread(rows_sent, grads_sent, slot_weight, weg, weu, wed):
    ep_count = lax.axis_size("ep")
    width = rows_sent.shape[1]
    local_count = max(1, EXPERTS // ep_count)
    replicas = max(1, ep_count // EXPERTS)
    groups = EXPERTS // local_count
    gate_cols, up_cols, down_rows = (
        lax.all_gather(weg, SEQ, axis=1, tiled=True),
        lax.all_gather(weu, SEQ, axis=1, tiled=True),
        lax.all_gather(wed, SEQ, axis=0, tiled=True),
    )
    hidden_part = gate_cols.shape[1] // local_count
    gate_local = gate_cols.reshape(width, local_count, hidden_part).transpose(1, 0, 2)
    up_local = up_cols.reshape(width, local_count, hidden_part).transpose(1, 0, 2)
    down_local = down_rows.reshape(local_count, hidden_part, width)

    def spread(buffer):
        last = buffer.shape[-1]
        wide = buffer.reshape(groups, 1, local_count * MOST, last)
        wide = jnp.broadcast_to(wide, (groups, replicas, local_count * MOST, last))
        return exchange(wide.reshape(ep_count, local_count * MOST, last), "ep")

    def collect(buffer):
        last = buffer.shape[-1]
        return jnp.sum(
            exchange(buffer, "ep").astype(WIDE).reshape(groups, replicas, local_count * MOST, last),
            1,
        ).reshape(EXPERTS * MOST, last)

    def owner_layout(received):
        last = received.shape[-1]
        return (
            received.reshape(ep_count, local_count, MOST, last)
            .transpose(1, 0, 2, 3)
            .reshape(local_count, ep_count * MOST, last)
        )

    def source_layout(owned):
        last = owned.shape[-1]
        return (
            owned.reshape(local_count, ep_count, MOST, last)
            .transpose(1, 0, 2, 3)
            .reshape(ep_count, local_count * MOST, last)
        )

    def batched(spec, left_op, right_op):
        return jnp.einsum(spec, left_op, right_op, preferred_element_type=WIDE)

    own_rows = owner_layout(spread(rows_sent))
    got_grads = owner_layout(spread(grads_sent))
    got_weight = owner_layout(spread(slot_weight[:, None]))
    gate_val = batched("lrd,ldh->lrh", own_rows, gate_local)
    up_val = batched("lrd,ldh->lrh", own_rows, up_local)
    silu_val, slope_val = silu_grad(gate_val)
    hidden_val = (silu_val * up_val).astype(LOW)
    out_rows = batched("lrh,lhd->lrd", hidden_val, down_local)
    back_out = collect(source_layout(out_rows.astype(LOW)))
    grad_hidden = batched("lrd,lhd->lrh", got_grads, down_local)
    row_dot = jnp.sum(hidden_val.astype(WIDE) * grad_hidden, -1, keepdims=True)
    back_dot = collect(source_layout(row_dot))
    scaled = got_weight * grad_hidden
    own_grads = (got_weight * got_grads.astype(WIDE)).astype(LOW)
    grad_gate = (scaled * up_val * slope_val).astype(LOW)
    grad_up = (scaled * silu_val).astype(LOW)
    din_rows = batched("lrh,ldh->lrd", grad_gate, gate_local)
    din_rows = din_rows + batched("lrh,ldh->lrd", grad_up, up_local)
    back_din = collect(source_layout(din_rows.astype(LOW)))
    grad_gate_w = batched("lrd,lrh->ldh", own_rows, grad_gate)
    grad_up_w = batched("lrd,lrh->ldh", own_rows, grad_up)
    grad_down_w = batched("lrh,lrd->lhd", hidden_val, own_grads)

    def share(full, axis):
        return lax.psum_scatter(
            full.astype(LOW), SEQ, scatter_dimension=axis, tiled=True
        ).astype(WIDE)

    return (
        back_out,
        back_din,
        back_dot[:, 0],
        share(grad_gate_w.transpose(1, 0, 2).reshape(width, local_count * hidden_part), 1),
        share(grad_up_w.transpose(1, 0, 2).reshape(width, local_count * hidden_part), 1),
        share(grad_down_w.reshape(local_count * hidden_part, width), 0),
    )


def shards(
    tokens,
    cotangent,
    routes,
    priority,
    gain_attn,
    w_query,
    w_key,
    w_value,
    w_out,
    gain_ffn,
    w_shared_gate,
    w_shared_up,
    w_shared_down,
    w_router,
    w_expert_gate,
    w_expert_up,
    w_expert_down,
):
    tok_rows, width = tokens.shape
    rows_w = w_query.shape[0]
    fs_count = lax.axis_size("fx") * lax.axis_size("fc")
    ep_count = lax.axis_size("ep")
    devices = ep_count * fs_count
    seq_len = tok_rows * fs_count
    head_count = HEADS // fs_count
    head_size = width // HEADS
    fs_index = lax.axis_index("fx") * lax.axis_size("fc") + lax.axis_index("fc")
    my_rank = lax.axis_index("ep") * fs_count + fs_index

    x_all = gather_seq(tokens)
    qkv_cut = jnp.stack([w_query, w_key, w_value]).reshape(3, rows_w, fs_count, rows_w)
    qkv_got = exchange(qkv_cut.transpose(2, 0, 1, 3), SEQ)
    qkv_mat = qkv_got.transpose(1, 0, 2, 3).reshape(3, width, rows_w)
    small = jnp.concatenate([gain_attn[None], gain_ffn[None], w_router.T], 0)
    small_all = gather_seq(small[None]).transpose(1, 0, 2).reshape(2 + EXPERTS, width)
    gain_one, gain_two, router_t = (small_all[0], small_all[1], small_all[2:])
    dy_all = gather_seq(cotangent)
    out_mat = gather_seq(w_out)
    ff_part = w_shared_gate.shape[1] // fs_count
    up_cut = jnp.stack([w_shared_gate, w_shared_up]).reshape(2, rows_w, fs_count, ff_part)
    up_got = exchange(up_cut.transpose(2, 0, 1, 3), SEQ)
    shared_mat = up_got.transpose(1, 0, 2, 3).reshape(2, width, ff_part)
    sgate_mat, sup_mat = (shared_mat[0], shared_mat[1])

    expert_iota = jnp.arange(EXPERTS)
    classes = jnp.stack([priority, 1 - priority], 1)
    route_hits = (routes[:, :, None] == expert_iota).astype(jnp.int32)
    per_class = jnp.stack(
        [
            jnp.sum(route_hits * (classes == class_id)[:, :, None].astype(jnp.int32), 1)
            for class_id in (0, 1)
        ]
    )
    counts = jnp.sum(per_class, 1)
    all_counts = spread_whole(counts, ALL, devices)
    lower = (jnp.arange(tok_rows)[:, None] > jnp.arange(tok_rows)[None, :]).astype(LOW)
    flat_class = per_class.transpose(1, 0, 2).reshape(tok_rows, 2 * EXPERTS)
    before = (
        matmul(lower, flat_class.astype(LOW))
        .astype(jnp.int32)
        .reshape(tok_rows, 2, EXPERTS)
        .transpose(1, 0, 2)
    )
    earlier = (jnp.arange(devices) < my_rank).astype(jnp.int32)
    ahead = jnp.sum(all_counts * earlier[:, None, None], 0)
    zero_row = jnp.zeros((EXPERTS,), jnp.int32)
    global_table = (
        before + (ahead + jnp.stack([zero_row, jnp.sum(all_counts[:, 0, :], 0)]))[:, None, :]
    )
    local_table = before + jnp.stack([zero_row, counts[0]])[:, None, :]

    def pair_value(class_table):
        picked = jnp.where(
            (classes == 0)[:, :, None], class_table[0][:, None, :], class_table[1][:, None, :]
        )
        return jnp.sum(picked * route_hits, -1)

    capacity = 5 * tok_rows * devices // 32
    kept_mask = (pair_value(global_table) < capacity).astype(WIDE)
    flat_slot = routes * MOST + pair_value(local_table)
    slot_iota = jnp.arange(EXPERTS * MOST)
    slot_hit = flat_slot[:, :, None] == slot_iota
    slot_hit_low = slot_hit.astype(LOW)
    dispatch = slot_hit_low[:, 0] + slot_hit_low[:, 1]
    grads_sent = contract_rows(dispatch, cotangent).astype(LOW)

    x_float = x_all.astype(WIDE)
    normed_one, inverse_one = rms_forward(x_float, gain_one)
    attn_input = normed_one.astype(LOW)
    cosine, sine_tab = rope_tables(jnp.arange(seq_len), head_size // 2)
    head_shape = (seq_len, head_count, head_size)
    query_rot = rotate(matmul(attn_input, qkv_mat[0]).reshape(head_shape), cosine, sine_tab)
    key_rot = rotate(matmul(attn_input, qkv_mat[1]).reshape(head_shape), cosine, sine_tab)
    query_heads = query_rot.astype(LOW).transpose(1, 0, 2)
    key_heads = key_rot.astype(LOW).transpose(1, 0, 2)
    value_heads = (
        matmul(attn_input, qkv_mat[2]).astype(LOW).reshape(head_shape).transpose(1, 0, 2)
    )
    causal = jnp.arange(seq_len)[:, None] >= jnp.arange(seq_len)[None, :]

    def head_forward(query_head, key_head, value_head):
        scores = jnp.where(causal, contract_cols(query_head, key_head) * SCALE, NEG)
        row_max = jnp.max(scores, -1, keepdims=True)
        exp_scores = jnp.exp(scores - row_max)
        row_total = jnp.sum(exp_scores, -1, keepdims=True)
        weights = (exp_scores / row_total).astype(LOW)
        return (matmul(weights, value_head).astype(LOW), row_max + jnp.log(row_total))

    fwd = [head_forward(query_heads[h], key_heads[h], value_heads[h]) for h in range(head_count)]
    attended_own = jnp.concatenate([piece[0] for piece in fwd], -1)
    attended_got = exchange(attended_own.reshape(fs_count, tok_rows, rows_w), SEQ)
    attended_low = attended_got.transpose(1, 0, 2).reshape(tok_rows, width)

    residual = tokens.astype(WIDE) + matmul(attended_low, out_mat)
    normed_two, inverse_two = rms_forward(residual, gain_two)
    ffn_input = normed_two.astype(LOW)
    logits = contract_cols(ffn_input, router_t)
    chosen = jnp.sum(route_hits.astype(WIDE) * logits[:, None, :], -1)
    chosen_exp = jnp.exp(chosen - jnp.max(chosen, -1, keepdims=True))
    gates = chosen_exp / jnp.sum(chosen_exp, -1, keepdims=True)
    pair_weight = gates * kept_mask
    slot_weight = jnp.sum(jnp.where(slot_hit, pair_weight[:, :, None], 0.0), (0, 1))
    rows_sent = contract_rows(dispatch, ffn_input).astype(LOW)

    pair_of_cores = EXPERTS == ep_count * lax.axis_size("fx")
    experts = experts_chip if pair_of_cores else experts_spread
    slot_out, slot_din, slot_dot, expert_gate_g, expert_up_g, expert_down_g = experts(
        rows_sent, grads_sent, slot_weight, w_expert_gate, w_expert_up, w_expert_down
    )

    ffn_all = gather_seq(ffn_input)
    shared_gate = matmul(ffn_all, sgate_mat)
    shared_up = matmul(ffn_all, sup_mat)
    shared_silu, shared_slope = silu_grad(shared_gate)
    shared_hidden = (shared_silu * shared_up).astype(LOW)
    grad_shidden = contract_cols(dy_all, w_shared_down)
    grad_sgate = (grad_shidden * shared_up * shared_slope).astype(LOW)
    grad_sup = (grad_shidden * shared_silu).astype(LOW)
    shared_din = scatter_seq(contract_cols(grad_sgate, sgate_mat) + contract_cols(grad_sup, sup_mat))
    shared_out = scatter_seq(matmul(shared_hidden, w_shared_down))
    grad_sdown = contract_rows(shared_hidden, dy_all)
    grad_sgate_w = contract_rows(ffn_all, grad_sgate)
    grad_sup_w = contract_rows(ffn_all, grad_sup)
    turned = jnp.stack([grad_sgate_w, grad_sup_w]).astype(LOW)
    turned = exchange(turned.reshape(2, fs_count, rows_w, ff_part).transpose(1, 0, 2, 3), SEQ)
    turned = turned.transpose(1, 2, 0, 3).reshape(2, rows_w, fs_count * ff_part)

    slot_out_low = slot_out.astype(LOW)
    mixed = sum(
        pair_weight[:, j : j + 1] * matmul(slot_hit_low[:, j], slot_out_low) for j in (0, 1)
    )
    output = (residual + shared_out + mixed).astype(LOW)
    grad_weight = jnp.sum(jnp.where(slot_hit, slot_dot, 0.0), -1) * kept_mask
    grad_chosen = gates * (grad_weight - jnp.sum(gates * grad_weight, -1, keepdims=True))
    grad_logits = jnp.sum(route_hits.astype(WIDE) * grad_chosen[:, :, None], 1).astype(LOW)
    grad_ffn = (
        shared_din + matmul(grad_logits, router_t) + matmul(dispatch, slot_din.astype(LOW))
    )
    grad_resid = cotangent.astype(WIDE) + rms_backward(grad_ffn, residual, inverse_two, gain_two)
    grad_branch = grad_resid.astype(LOW)
    gain_part = jnp.sum(grad_ffn * residual * inverse_two, 0)
    branch_all = gather_seq(grad_branch)
    grad_att = contract_cols(branch_all, w_out).astype(LOW)
    grad_out_w = contract_rows(attended_own, branch_all)
    router_part = contract_rows(grad_logits, ffn_input)

    grad_heads = grad_att.reshape(head_shape).transpose(1, 0, 2)

    def head_backward(query_head, key_head, value_head, grad_head, lse_head):
        scores = jnp.where(causal, contract_cols(query_head, key_head) * SCALE, NEG)
        probs = jnp.exp(scores - lse_head)
        grad_probs = contract_cols(grad_head, value_head)
        inner = jnp.sum(probs * grad_probs, -1, keepdims=True)
        grad_scores = (probs * (grad_probs - inner)).astype(LOW)
        grad_query = matmul(grad_scores, key_head) * SCALE
        grad_keys = contract_rows(grad_scores, query_head) * SCALE
        grad_values = contract_rows(probs.astype(LOW), grad_head)
        return (grad_query, grad_keys, grad_values)

    bwd = [
        head_backward(query_heads[h], key_heads[h], value_heads[h], grad_heads[h], fwd[h][1])
        for h in range(head_count)
    ]
    stack3 = [jnp.stack([piece[i] for piece in bwd], 1) for i in range(3)]
    d_query = rotate(stack3[0], cosine, -sine_tab).reshape(seq_len, rows_w).astype(LOW)
    d_keys = rotate(stack3[1], cosine, -sine_tab).reshape(seq_len, rows_w).astype(LOW)
    d_values = stack3[2].reshape(seq_len, rows_w).astype(LOW)
    d_qkv = (d_query, d_keys, d_values)
    grads_qkv = jnp.stack([contract_rows(attn_input, d_one) for d_one in d_qkv]).astype(LOW)
    grad_in = scatter_seq(sum(contract_cols(d_qkv[i], qkv_mat[i]) for i in range(3)))
    own_float = tokens.astype(WIDE)
    own_inverse = lax.rsqrt(jnp.mean(own_float * own_float, -1, keepdims=True) + EPS)
    grad_tokens = grad_resid + rms_backward(grad_in, own_float, own_inverse, gain_one)

    dense = lax.psum(
        (turned, grad_sdown.astype(LOW), grad_out_w.astype(LOW)), "ep"
    )
    sum_sgate_w, sum_sup_w = (dense[0][0].astype(WIDE), dense[0][1].astype(WIDE))
    sum_sdown, sum_out_w = (dense[1].astype(WIDE), dense[2].astype(WIDE))
    small_sum = lax.psum(jnp.concatenate([gain_part[None], router_part], 0), ALL)
    small_own = lax.dynamic_slice_in_dim(small_sum, fs_index * rows_w, rows_w, 1)
    sum_gain_two, sum_router = (small_own[0], small_own[1:].T)
    strip = rows_w // ep_count
    qkv_blocks = grads_qkv.reshape(3, fs_count, ep_count, strip, rows_w).transpose(2, 1, 0, 3, 4)
    qkv_parts = exchange(qkv_blocks.reshape(devices, 3, strip, rows_w), ALL)
    qkv_parts = qkv_parts.reshape(ep_count, fs_count, 3, strip, rows_w).astype(WIDE)
    qkv_sum = jnp.sum(qkv_parts, 0).transpose(1, 2, 0, 3).reshape(3, strip, width).astype(LOW)
    qkv_whole = spread_whole(qkv_sum, "ep", ep_count)
    qkv_whole = qkv_whole.transpose(1, 0, 2, 3).reshape(3, rows_w, width).astype(WIDE)
    sum_gain_one = (
        sum(
            jnp.sum(qkv_whole[i] * mat.astype(WIDE), -1)
            for i, mat in enumerate((w_query, w_key, w_value))
        )
        / gain_attn.astype(WIDE)
    )
    return (
        output,
        grad_tokens,
        sum_gain_one,
        qkv_whole[0],
        qkv_whole[1],
        qkv_whole[2],
        sum_out_w,
        sum_gain_two,
        sum_sgate_w,
        sum_sup_w,
        sum_sdown,
        sum_router,
        expert_gate_g,
        expert_up_g,
        expert_down_g,
    )


def solution(mesh):
    ep_count, fs_count = mesh.devices.shape
    cut_mesh = Mesh(mesh.devices.reshape(ep_count, fs_count // 2, 2), ALL)
    tok = P(ALL, None)
    row = P(SEQ, None)
    return jax.shard_map(
        shards,
        mesh=cut_mesh,
        in_specs=(
            tok,
            tok,
            tok,
            P(ALL),
            P(SEQ),
            row,
            row,
            row,
            row,
            P(SEQ),
            row,
            row,
            row,
            row,
            P(None, ALL),
            P(None, ALL),
            tok,
        ),
        out_specs=(
            tok,
            tok,
            P(SEQ),
            row,
            row,
            row,
            row,
            P(SEQ),
            row,
            row,
            row,
            row,
            P(None, ALL),
            P(None, ALL),
            tok,
        ),
        check_vma=False,
    )
```

```python
import jax
import jax.numpy as jnp
import numpy as np
from jax import lax
from jax.experimental import pallas as pl
from jax.experimental.pallas import tpu as pltpu
from jax.sharding import Mesh
from jax.sharding import PartitionSpec as P

HEADS = 12
EXPERTS = 16
MOST = 48
EXTRA = 2 * EXPERTS

EPS = 1e-06
NEG = -1e30
LOW = jnp.bfloat16
WIDE = jnp.float32
ALL = ("ep", "fx", "fc")
SEQ = ("fx", "fc")
SWAP = [(0, 1), (1, 0)]
VMEM = pl.BlockSpec(memory_space=pltpu.VMEM)
SMEM = pl.BlockSpec(memory_space=pltpu.SMEM)


def matmul(left_op, right_op):
    return jnp.dot(left_op, right_op, preferred_element_type=WIDE)


def contract_rows(left_op, right_op):
    return lax.dot_general(left_op, right_op, (((0,), (0,)), ((), ())), preferred_element_type=WIDE)


def contract_cols(left_op, right_op):
    return lax.dot_general(left_op, right_op, (((1,), (1,)), ((), ())), preferred_element_type=WIDE)


def inverse_rms(values):
    return lax.rsqrt(jnp.mean(values * values, -1, keepdims=True) + EPS)


def rms_backward(upstream, values, inverse, gain_vec):
    scaled = upstream * gain_vec
    return inverse * scaled - values * inverse**3 * jnp.mean(scaled * values, -1, keepdims=True)


def silu_grad(gate_val):
    sigma = jax.nn.sigmoid(gate_val)
    return (gate_val * sigma, sigma * (1.0 + gate_val * (1.0 - sigma)))


def far_of(block):
    return lax.ppermute(block, "fx", SWAP)


def near_of(block):
    return lax.ppermute(block, "fc", SWAP)


def after(value, *others):
    return lax.optimization_barrier((value, *others))[0]


def exchange(blocks, axes):
    return lax.all_to_all(blocks, axes, split_axis=0, concat_axis=0, tiled=True)


def halve(parts):
    index = lax.axis_index("ep")
    count = parts.shape[0]
    size = count
    while size > 1:
        bit = count // size
        cut = parts.reshape((size // 2, 2) + parts.shape[1:])
        mine = lax.rem(index // bit, 2)
        give = lax.dynamic_index_in_dim(cut, 1 - mine, 1, keepdims=False)
        keep = lax.dynamic_index_in_dim(cut, mine, 1, keepdims=False)
        got = lax.ppermute(give, "ep", [(i, i ^ bit) for i in range(count)])
        parts = (keep.astype(WIDE) + got.astype(WIDE)).astype(LOW)
        size //= 2
    return parts[0]


def shape_of(dims, kind):
    return jax.ShapeDtypeStruct(dims, kind)


def run_kernel(body, outs, args, specs=None, out_specs=None, scratch=(), grid=None, flops=0, move=0):
    options = {} if grid is None else {"grid": grid}
    return pl.pallas_call(
        body,
        out_shape=outs,
        in_specs=specs if specs is not None else [VMEM] * len(args),
        out_specs=out_specs if out_specs is not None else [VMEM] * len(outs),
        scratch_shapes=list(scratch),
        compiler_params=pltpu.CompilerParams(vmem_limit_bytes=52 * 2**20),
        cost_estimate=pl.CostEstimate(flops=flops, bytes_accessed=move, transcendentals=0),
        **options,
    )(*args)


def pick_rows(first_iota, second_iota, source):
    return (first_iota == source(second_iota)).astype(LOW)


def rope_constants(length, half):
    freq = np.exp(-np.log(np.float32(10000.0)) * np.arange(half, dtype=np.float32) / np.float32(half))
    angle = np.arange(length, dtype=np.float32)[:, None] * freq.astype(np.float32)[None, :]
    cosine, sine = (np.cos(angle), np.sin(angle))
    return (
        np.concatenate([cosine, cosine, sine, sine], 1).astype(np.float32),
        np.concatenate([cosine] * 4, 1).astype(np.float32),
        np.concatenate([sine, -sine, sine, -sine], 1).astype(np.float32),
    )


def attention_forward(ids, x_parts, w_parts, table):
    full, width = x_parts[0].shape
    rows = full - EXTRA
    block = w_parts[0].shape[1]
    length = 4 * rows
    heads = block // 64
    size = heads * 128

    def body(ids_ref, *refs):
        x_refs, w_refs, table_ref = (refs[:4], refs[4:8], refs[8])
        ain_ref, own_ref, q_ref, k_ref, v_ref, lse_ref = refs[9:15]
        att_refs, small_ref = (refs[15:19], refs[19])
        att_scr = refs[20]
        first = lax.broadcasted_iota(jnp.int32, (block, width), 0)
        lane = lax.broadcasted_iota(jnp.int32, (block, width), 1)
        small = jnp.zeros((EXTRA, width), WIDE)
        for k in range(4):
            place = jnp.where(lane == first + ids_ref[1 + k] * block, 1.0, 0.0).astype(LOW)
            small = small + matmul(x_refs[k][rows:, :block], place)
        small_ref[...] = small.astype(LOW)
        gain = small[EXPERTS : EXPERTS + 1, :]
        for k in range(4):
            place = ids_ref[1 + k]
            piece = x_refs[k][:rows, :].astype(WIDE)
            ain_ref[pl.ds(place * rows, rows), :] = (piece * inverse_rms(piece) * gain).astype(LOW)
            for m in range(3):
                own_ref[m, pl.ds(place * block, block), :] = w_refs[k][m]
        first = lax.broadcasted_iota(jnp.int32, (block, size), 0)
        lane = lax.broadcasted_iota(jnp.int32, (block, size), 1)
        head, inner = (lane // 128, lane % 128)
        low = inner % 64
        swapped = jnp.where(low < 32, low + 32, low - 32)
        source = 64 * head + jnp.where(inner < 64, low, swapped)
        sign = jnp.where((inner >= 64) & (low < 32), -1.0, 1.0)
        turn = jnp.where(first == source, sign, 0.0).astype(LOW)
        keep = (inner // 64 == head % 2) & (first == 64 * head + low)
        place_v = jnp.where(keep, 1.0, 0.0).astype(LOW)
        w_q = matmul(own_ref[0], turn).astype(LOW)
        w_k = matmul(own_ref[1], turn).astype(LOW)
        w_v = matmul(own_ref[2], place_v).astype(LOW)
        half = lax.broadcasted_iota(jnp.int32, (rows, 128), 1) < 64
        for i in range(4):
            span = slice(i * rows, (i + 1) * rows)
            ain = ain_ref[span, :]
            y_q, y_k, y_v = (matmul(ain, w_q), matmul(ain, w_k), matmul(ain, w_v))
            tab = table_ref[span, :]
            for h in range(heads):
                cols = slice(128 * h, 128 * h + 128)
                turned = y_q[:, cols] * tab
                turned = (turned + pltpu.roll(turned, 64, 1)).astype(LOW).astype(WIDE)
                q_ref[h, span, :] = jnp.where(half, turned * 0.125, 0.0).astype(LOW)
                turned = y_k[:, cols] * tab
                k_ref[h, span, :] = (turned + pltpu.roll(turned, 64, 1)).astype(LOW)
                v_ref[h, span, :] = y_v[:, cols].astype(LOW)
        tri = lax.broadcasted_iota(jnp.int32, (rows, rows), 0) >= lax.broadcasted_iota(
            jnp.int32, (rows, rows), 1
        )
        for i in range(4):
            span = slice(i * rows, (i + 1) * rows)
            done = slice(0, i * rows)
            tiles = []
            for h in range(heads):
                query = q_ref[h, span, :]
                diag = jnp.where(tri, contract_cols(query, k_ref[h, span, :]), NEG)
                top = jnp.max(diag, -1, keepdims=True)
                if i:
                    past = contract_cols(query, k_ref[h, done, :])
                    top = jnp.maximum(top, jnp.max(past, -1, keepdims=True))
                diag = jnp.exp(diag - top)
                total = jnp.sum(diag, -1, keepdims=True)
                if i:
                    past = jnp.exp(past - top)
                    total = total + jnp.sum(past, -1, keepdims=True)
                scale = 1.0 / total
                out = matmul((diag * scale).astype(LOW), v_ref[h, span, :])
                if i:
                    out = out + matmul((past * scale).astype(LOW), v_ref[h, done, :])
                lse_ref[h, span, :] = top + jnp.log(total)
                tiles.append(out)
            for t in range((heads + 1) // 2):
                pair = tiles[2 * t] + (tiles[2 * t + 1] if 2 * t + 1 < heads else 0.0)
                wide = min(128, block - 128 * t)
                att_scr[span, 128 * t : 128 * t + wide] = pair[:, :wide].astype(LOW)
        for k in range(4):
            att_refs[k][...] = att_scr[pl.ds(ids_ref[1 + k] * rows, rows), :]

    outs = (
        [shape_of((length, width), LOW), shape_of((3, width, block), LOW)]
        + [shape_of((heads, length, 128), LOW)] * 3
        + [shape_of((heads, length, 1), WIDE)]
        + [shape_of((rows, block), LOW)] * 4
        + [shape_of((EXTRA, width), LOW)]
    )
    args = [ids, *x_parts, *w_parts, table]
    got = run_kernel(
        body,
        outs,
        args,
        specs=[SMEM] + [VMEM] * (len(args) - 1),
        scratch=[pltpu.VMEM((length, block), LOW)],
        flops=8 * 10**9,
        move=12 * 10**6,
    )
    return (got[0], got[1], got[2:5], got[5], got[6:10], got[10])


def after_attention(att_parts, out_parts, tokens, small, dispatch):
    rows, width = tokens.shape

    def body(*refs):
        att_refs, out_refs = (refs[:4], refs[4:8])
        tok_ref, small_ref, disp_ref, res_ref, ffn_ref, sent_ref = refs[8:]
        total = tok_ref[...].astype(WIDE)
        for k in range(4):
            total = total + matmul(att_refs[k][...], out_refs[k][...])
        res_ref[...] = total
        gain = small_ref[EXPERTS + 1 : EXPERTS + 2, :].astype(WIDE)
        ffn = (total * inverse_rms(total) * gain).astype(LOW)
        ffn_ref[...] = ffn
        sent_ref[...] = contract_rows(disp_ref[...], ffn).astype(LOW)

    slots = dispatch.shape[1]
    outs = [shape_of((rows, width), WIDE), shape_of((rows, width), LOW), shape_of((slots, width), LOW)]
    args = [*att_parts, *out_parts, tokens, small, dispatch]
    return run_kernel(body, outs, args, flops=6 * 10**8, move=4 * 10**6)


def shared_branch(ids, ffn_parts, dy_parts, w_parts, down, chunks):
    rows, width = ffn_parts[0].shape
    block, hidden = w_parts[0].shape[1:]

    def body(ids_ref, *refs):
        ffn_refs, dy_refs, w_refs = (refs[:4], refs[4:8], refs[8:12])
        down_ref = refs[12]
        mine_ref, near_ref, mid_ref = refs[13:16]
        grad_refs = refs[16:-3]
        w_scr, g_scr, d_scr = refs[-3:]
        for k in range(4):
            for m in range(2):
                w_scr[m, pl.ds(ids_ref[1 + k] * block, block), :] = w_refs[k][m]
        for k in range(4):
            ffn, dy = (ffn_refs[k][...], dy_refs[k][...])
            gate, up = (matmul(ffn, w_scr[0]), matmul(ffn, w_scr[1]))
            silu, slope = silu_grad(gate)
            hid = (silu * up).astype(LOW)
            back = contract_cols(dy, down_ref[...])
            d_gate = (back * up * slope).astype(LOW)
            d_up = (back * silu).astype(LOW)
            din = (contract_cols(d_gate, w_scr[0]) + contract_cols(d_up, w_scr[1])).astype(LOW)
            out = matmul(hid, down_ref[...]).astype(LOW)
            if k % 2 == 0:
                target = mine_ref if k == 0 else mid_ref
                target[0], target[1] = (din, out)
            else:
                near_ref[k // 2, 0], near_ref[k // 2, 1] = (din, out)
            parts = (contract_rows(ffn, d_gate), contract_rows(ffn, d_up), contract_rows(hid, dy))
            if k == 0:
                g_scr[0], g_scr[1], d_scr[...] = parts
            else:
                g_scr[0] += parts[0]
                g_scr[1] += parts[1]
                d_scr[...] += parts[2]
        if chunks:
            per = chunks // 2
            cut, line = (block // per, hidden // chunks)
            for r in range(chunks):
                part = ids_ref[6] ^ r
                target = grad_refs[r % 2]
                which, low = (part // per, part % per)
                for k in range(4):
                    start = ids_ref[1 + k] * block + low * cut
                    target[r // 2, k * cut : (k + 1) * cut, :] = g_scr[
                        which, pl.ds(pl.multiple_of(start, 16), cut), :
                    ].astype(LOW)
                start = pl.multiple_of(part * line, 16)
                piece = d_scr[pl.ds(start, line), :].astype(LOW)
                base = 4 * cut
                target[r // 2, base : base + line, :] = piece[:, :hidden]
                target[r // 2, base + line :, : hidden // 2] = piece[: line // 2, hidden:]
                target[r // 2, base + line :, hidden // 2 :] = piece[line // 2 :, hidden:]
        else:
            for k in range(4):
                for m in range(2):
                    grad_refs[k][m] = g_scr[m, pl.ds(ids_ref[1 + k] * block, block), :].astype(LOW)
            grad_refs[4][...] = d_scr[...].astype(LOW)

    if chunks:
        lines = 4 * block * 2 // chunks + 3 * hidden // chunks // 2
        grad_outs = [shape_of((chunks // 2, lines, hidden), LOW)] * 2
    else:
        grad_outs = [shape_of((2, block, hidden), LOW)] * 4 + [shape_of((hidden, width), LOW)]
    outs = [
        shape_of((2, rows, width), LOW),
        shape_of((2, 2, rows, width), LOW),
        shape_of((2, rows, width), LOW),
    ] + grad_outs
    args = [ids, *ffn_parts, *dy_parts, *w_parts, down]
    got = run_kernel(
        body,
        outs,
        args,
        specs=[SMEM] + [VMEM] * (len(args) - 1),
        scratch=[
            pltpu.VMEM((2, width, hidden), LOW),
            pltpu.VMEM((2, width, hidden), WIDE),
            pltpu.VMEM((hidden, width), WIDE),
        ],
        flops=7 * 10**9,
        move=14 * 10**6,
    )
    return (got[0:3], got[3:])


def place_shared(ids, groups, block, width):
    per_group, lines, hidden = groups[0].shape
    chunks = per_group * len(groups)
    per = chunks // 2
    cut, line = (block // per, hidden // chunks)
    order = (0, 4, 2, 6, 1, 5, 3, 7)

    def body(ids_ref, *refs):
        up_ref, down_ref = refs[-2:]
        for n in range(chunks):
            part = ids_ref[6] ^ order[n]
            which, low = (part // per, part % per)
            piece = refs[n // per_group][n % per_group].astype(WIDE)
            for k in range(4):
                lane = pl.multiple_of(ids_ref[1 + k] * hidden, 128)
                up_ref[which, pl.ds(low * cut, cut), pl.ds(lane, hidden)] = piece[
                    k * cut : (k + 1) * cut, :
                ]
            base = 4 * cut
            start = pl.multiple_of(part * line, 16)
            down_ref[pl.ds(start, line), :hidden] = piece[base : base + line, :]
            tail = piece[base + line :, :]
            down_ref[pl.ds(start, line // 2), hidden:] = tail[:, : hidden // 2]
            down_ref[pl.ds(start + line // 2, line // 2), hidden:] = tail[:, hidden // 2 :]

    return run_kernel(
        body,
        [shape_of((2, block, 4 * hidden), WIDE), shape_of((hidden, width), WIDE)],
        [ids, *groups],
        specs=[SMEM] + [VMEM] * len(groups),
        move=8 * 10**6,
    )


def expert_main(ids, rows_in, dy_in, mats, other, router_t):
    count, width = rows_in.shape
    own_hidden = mats[0].shape[1]
    tile = 512
    steps = 2 * own_hidden // tile
    half = steps // 2
    chunk = 256

    def body(ids_ref, rows_ref, dy_ref, *refs):
        own, peer = (refs[0:3], refs[3:6])
        other_ref, router_ref = refs[6:8]
        din_ref, hid_ref, dg_ref, du_ref, dyw_ref, w_ref, part_ref = refs[8:15]
        acc, dot_scr = refs[15:17]
        step = pl.program_id(0)
        expert = ids_ref[5]

        @pl.when(step == 0)
        def start():
            for r in range(0, count, chunk):
                span = slice(r, r + chunk)
                logits = contract_cols(rows_ref[span, :], router_ref[...])
                lane = lax.broadcasted_iota(jnp.int32, logits.shape, 1)
                mine = jnp.sum(jnp.where(lane == expert, logits, 0.0), -1, keepdims=True)
                rest = jnp.sum(jnp.where(lane == other_ref[span, :], logits, 0.0), -1, keepdims=True)
                weight = jax.nn.sigmoid(mine - rest)
                w_ref[span, :] = weight
                dyw_ref[span, :] = (weight * dy_ref[span, :].astype(WIDE)).astype(LOW)
                dot_scr[span, :] = jnp.zeros((chunk, 1), WIDE)
                acc[span, :] = jnp.zeros((chunk, width), WIDE)

        def work(gate_ref, up_ref, down_ref):
            for r in range(0, count, chunk):
                span = slice(r, r + chunk)
                rows = rows_ref[span, :]
                gate, up = (matmul(rows, gate_ref[...]), matmul(rows, up_ref[...]))
                back = contract_cols(dy_ref[span, :], down_ref[...])
                silu, slope = silu_grad(gate)
                hid = (silu * up).astype(LOW)
                hid_ref[span, :] = hid
                dot_scr[span, :] += jnp.sum(hid.astype(WIDE) * back, -1, keepdims=True)
                scaled = w_ref[span, :] * back
                d_gate = (scaled * up * slope).astype(LOW)
                d_up = (scaled * silu).astype(LOW)
                dg_ref[span, :] = d_gate
                du_ref[span, :] = d_up
                acc[span, :] += contract_cols(d_gate, gate_ref[...]) + contract_cols(
                    d_up, up_ref[...]
                )

        @pl.when(step < half)
        def first():
            work(*own)

        @pl.when(step >= half)
        def second():
            work(*peer)

        @pl.when(step == steps - 1)
        def finish():
            for r in range(0, count, chunk):
                span = slice(r, r + chunk)
                weight = w_ref[span, :]
                amount = weight * (1.0 - weight) * dot_scr[span, :]
                lane = lax.broadcasted_iota(jnp.int32, (chunk, EXTRA), 1)
                signs = jnp.where(lane == expert, 1.0, 0.0) - jnp.where(
                    lane == other_ref[span, :], 1.0, 0.0
                )
                d_logit = (amount * signs).astype(LOW)
                din_ref[span, :] = (acc[span, :] + matmul(d_logit, router_ref[...])).astype(LOW)
                part = contract_rows(d_logit, rows_ref[span, :])
                part_ref[...] = part if r == 0 else part_ref[...] + part

    def fixed(dims):
        return pl.BlockSpec(dims, lambda j: (0,) * len(dims))

    def near(j):
        return jnp.minimum(j, half - 1)

    def late(j):
        return jnp.maximum(j - half, 0)

    cols = (width, tile)
    specs = [SMEM, fixed((count, width)), fixed((count, width))]
    for place in (near, late):
        specs += [
            pl.BlockSpec(cols, lambda j, place=place: (0, place(j))),
            pl.BlockSpec(cols, lambda j, place=place: (0, place(j))),
            pl.BlockSpec((tile, width), lambda j, place=place: (place(j), 0)),
        ]
    specs += [fixed((count, 1)), fixed(router_t.shape)]
    tiles = pl.BlockSpec((count, tile), lambda j: (0, j))
    outs = (
        [shape_of((count, width), LOW)]
        + [shape_of((count, 2 * own_hidden), LOW)] * 3
        + [shape_of((count, width), LOW), shape_of((count, 1), WIDE), shape_of(router_t.shape, WIDE)]
    )
    out_specs = [
        fixed((count, width)),
        tiles,
        tiles,
        tiles,
        fixed((count, width)),
        fixed((count, 1)),
        fixed(router_t.shape),
    ]
    return run_kernel(
        body,
        outs,
        [ids, rows_in, dy_in, *mats, other, router_t],
        specs=specs,
        out_specs=out_specs,
        scratch=[pltpu.VMEM((count, width), WIDE), pltpu.VMEM((count, 1), WIDE)],
        grid=(steps,),
        flops=12 * 10**9,
        move=22 * 10**6,
    )


def expert_out(hid, weight, down_own, down_peer):
    count, hidden = hid.shape
    width = down_own.shape[1]
    half = hidden // 2
    chunk = 256

    def body(hid_ref, w_ref, own_ref, peer_ref, out_ref):
        for r in range(0, count, chunk):
            span = slice(r, r + chunk)
            total = matmul(hid_ref[span, :half], own_ref[...])
            total = total + matmul(hid_ref[span, half:], peer_ref[...])
            out_ref[span, :] = (w_ref[span, :] * total).astype(LOW)

    return run_kernel(
        body,
        [shape_of((count, width), LOW)],
        [hid, weight, down_own, down_peer],
        flops=2 * 10**9,
        move=8 * 10**6,
    )[0]


def expert_weight_grads(rows_in, dyw, hid, d_gate, d_up, peer, add=None):
    count, width = rows_in.shape
    half = hid.shape[1] // 2
    tile = 512
    steps = half // tile
    offset = steps if peer else 0
    kind = LOW if add is None else WIDE

    def body(rows_ref, dyw_ref, hid_ref, dg_ref, du_ref, *refs):
        outs = refs[-3:]
        grads = (
            contract_rows(rows_ref[...], dg_ref[...]),
            contract_rows(rows_ref[...], du_ref[...]),
            contract_rows(hid_ref[...], dyw_ref[...]),
        )
        for i in range(3):
            value = grads[i] if add is None else grads[i] + refs[i][...].astype(WIDE)
            outs[i][...] = value.astype(kind)

    def fixed(dims):
        return pl.BlockSpec(dims, lambda j: (0,) * len(dims))

    tiles = pl.BlockSpec((count, tile), lambda j: (0, j + offset))
    cols = pl.BlockSpec((width, tile), lambda j: (0, j))
    lines = pl.BlockSpec((tile, width), lambda j: (j, 0))
    specs = [fixed((count, width)), fixed((count, width)), tiles, tiles, tiles]
    extra = [] if add is None else list(add)
    return run_kernel(
        body,
        [shape_of((width, half), kind), shape_of((width, half), kind), shape_of((half, width), kind)],
        [rows_in, dyw, hid, d_gate, d_up, *extra],
        specs=specs + ([] if add is None else [cols, cols, lines]),
        out_specs=[cols, cols, lines],
        grid=(steps,),
        flops=37 * 10**8,
        move=14 * 10**6,
    )


def back_at_tokens(fold, back_din, dispatch, residual, small, cotangent, router_part):
    rows, width = residual.shape

    def body(one_ref, two_ref, last_ref, back_ref, disp_ref, res_ref, small_ref, dy_ref, part_ref, dres_ref, br_ref):
        d_ffn = one_ref[0].astype(WIDE) + two_ref[0, 0].astype(WIDE) + last_ref[0].astype(WIDE)
        d_ffn = d_ffn + matmul(disp_ref[...], back_ref[...])
        residual_val = res_ref[...]
        inverse = inverse_rms(residual_val)
        gain = small_ref[EXPERTS + 1 : EXPERTS + 2, :].astype(WIDE)
        d_res = dy_ref[...].astype(WIDE) + rms_backward(d_ffn, residual_val, inverse, gain)
        dres_ref[...] = d_res
        br_ref[0:rows, :] = d_res.astype(LOW)
        gain_part = jnp.sum(d_ffn * residual_val * inverse, 0, keepdims=True)
        line = lax.broadcasted_iota(jnp.int32, (EXTRA, width), 0)
        extra = jnp.where(line == EXPERTS, gain_part, part_ref[...])
        br_ref[rows:, :] = extra.astype(LOW)

    return run_kernel(
        body,
        [shape_of((rows, width), WIDE), shape_of((rows + EXTRA, width), LOW)],
        [*fold, back_din, dispatch, residual, small, cotangent, router_part],
        flops=3 * 10**8,
        move=5 * 10**6,
    )


def finish_output(residual, fold, back_out, dispatch):
    rows, width = residual.shape

    def body(res_ref, one_ref, two_ref, last_ref, back_ref, disp_ref, out_ref):
        total = res_ref[...] + one_ref[1].astype(WIDE) + two_ref[0, 1].astype(WIDE)
        total = total + last_ref[1].astype(WIDE)
        out_ref[...] = (total + matmul(disp_ref[...], back_ref[...])).astype(LOW)

    return run_kernel(
        body,
        [shape_of((rows, width), LOW)],
        [residual, *fold, back_out, dispatch],
        flops=3 * 10**8,
        move=4 * 10**6,
    )[0]


def attention_backward(ids, branch, w_out, queries, keys, values, lse, ain, tables):
    heads, length, _ = queries.shape
    rows = length // 4
    block, width = w_out.shape
    tiles = (heads + 1) // 2

    def body(ids_ref, *refs):
        br_refs = refs[:4]
        wo_ref, q_ref, k_ref, v_ref, lse_ref, ain_ref, cc_ref, ss_ref = refs[4:12]
        d_ref, g_ref = refs[12:14]
        da_scr, dk_scr, dv_scr = refs[14:17]
        zero = jnp.zeros((rows, 128), WIDE)
        for k in range(4):
            d_att = contract_cols(br_refs[k][0:rows, :], wo_ref[...]).astype(LOW)
            place = ids_ref[1 + k] * rows
            for t in range(tiles):
                wide = min(128, block - 128 * t)
                if wide < 128:
                    da_scr[t, pl.ds(place, rows), :] = zero.astype(LOW)
                da_scr[t, pl.ds(place, rows), 0:wide] = d_att[:, 128 * t : 128 * t + wide]
        half = lax.broadcasted_iota(jnp.int32, (rows, 128), 1) < 64
        tri = lax.broadcasted_iota(jnp.int32, (rows, rows), 0) >= lax.broadcasted_iota(
            jnp.int32, (rows, rows), 1
        )

        def place_tile(m, span, h, value):
            t = h // 2
            wide = min(128, block - 128 * t)
            if h % 2 == 0:
                d_ref[m, span, 128 * t : 128 * t + wide] = value[:, :wide].astype(LOW)
            else:
                kept = d_ref[m, span, 128 * t : 128 * t + 128].astype(WIDE)
                d_ref[m, span, 128 * t : 128 * t + 128] = jnp.where(half, kept, value).astype(LOW)

        def unturn(value, span):
            return value * cc_ref[span, :] + pltpu.roll(value, 32, 1) * ss_ref[span, :]

        for h in range(heads):
            for i in range(4):
                span = slice(i * rows, (i + 1) * rows)
                done = slice(0, i * rows)
                query = q_ref[h, span, :]
                d_att = da_scr[h // 2, span, :]
                level = lse_ref[h, span, :]
                diag = contract_cols(query, k_ref[h, span, :]) - level
                diag = jnp.exp(jnp.where(tri, diag, NEG))
                d_diag = contract_cols(d_att, v_ref[h, span, :])
                inner = jnp.sum(diag * d_diag, -1, keepdims=True)
                if i:
                    past = jnp.exp(contract_cols(query, k_ref[h, done, :]) - level)
                    d_past = contract_cols(d_att, v_ref[h, done, :])
                    inner = inner + jnp.sum(past * d_past, -1, keepdims=True)
                d_diag = (diag * (d_diag - inner)).astype(LOW)
                d_query = matmul(d_diag, k_ref[h, span, :])
                dk_scr[span, :] = contract_rows(d_diag, query)
                dv_scr[span, :] = contract_rows(diag.astype(LOW), d_att)
                if i:
                    d_past = (past * (d_past - inner)).astype(LOW)
                    d_query = d_query + matmul(d_past, k_ref[h, done, :])
                    dk_scr[done, :] += contract_rows(d_past, query)
                    dv_scr[done, :] += contract_rows(past.astype(LOW), d_att)
                place_tile(0, span, h, unturn(d_query * 0.125, span))
            for i in range(4):
                span = slice(i * rows, (i + 1) * rows)
                d_key = dk_scr[span, :]
                place_tile(1, span, h, unturn(d_key + pltpu.roll(d_key, 64, 1), span))
                place_tile(2, span, h, dv_scr[span, :])
        for m in range(3):
            g_ref[m] = contract_rows(ain_ref[...], d_ref[m]).astype(LOW)

    args = [ids, *branch, w_out, queries, keys, values, lse, ain, *tables]
    return run_kernel(
        body,
        [shape_of((3, length, block), LOW), shape_of((3, width, block), LOW)],
        args,
        specs=[SMEM] + [VMEM] * (len(args) - 1),
        scratch=[
            pltpu.VMEM((tiles, length, 128), LOW),
            pltpu.VMEM((length, 128), WIDE),
            pltpu.VMEM((length, 128), WIDE),
        ],
        flops=16 * 10**9,
        move=12 * 10**6,
    )


def late_grads(ids, d_qkv, own_mats, att_parts, branch):
    length, block = d_qkv.shape[1:]
    rows = length // 4
    width = own_mats.shape[1]
    extra = branch[0].shape[0] - rows

    def body(ids_ref, d_ref, w_ref, *refs):
        att_refs, br_refs = (refs[:4], refs[4:8])
        mine_ref, near_ref, mid_ref, gout_ref = refs[8:12]
        for k in range(4):
            span = pl.ds(ids_ref[1 + k] * rows, rows)
            total = contract_cols(d_ref[0, span, :], w_ref[0])
            for m in range(1, 3):
                total = total + contract_cols(d_ref[m, span, :], w_ref[m])
            if k % 2 == 0:
                target = mine_ref if k == 0 else mid_ref
                target[...] = total.astype(LOW)
            else:
                near_ref[k // 2] = total.astype(LOW)
        gout = contract_rows(att_refs[0][...], br_refs[0][0:rows, :])
        small = br_refs[0][rows:, :].astype(WIDE)
        for k in range(1, 4):
            gout = gout + contract_rows(att_refs[k][...], br_refs[k][0:rows, :])
            small = small + br_refs[k][rows:, :].astype(WIDE)
        gout_ref[0:block, :] = gout.astype(LOW)
        gout_ref[block:, :] = small.astype(LOW)

    args = [ids, d_qkv, own_mats, *att_parts, *branch]
    got = run_kernel(
        body,
        [
            shape_of((rows, width), LOW),
            shape_of((2, rows, width), LOW),
            shape_of((rows, width), LOW),
            shape_of((block + extra, width), LOW),
        ],
        args,
        specs=[SMEM] + [VMEM] * (len(args) - 1),
        flops=12 * 10**8,
        move=7 * 10**6,
    )
    return (got[:3], got[3])


def experts_chip(ids, rows_sent, got_dy, other, small, weights, peers):
    width = rows_sent.shape[1]
    axes = ("ep", "fx")
    own_rows = exchange(rows_sent.reshape(EXPERTS, MOST, width), axes).reshape(-1, width)
    din, hid, d_gate, d_up, dyw, weight, part = expert_main(
        ids, own_rows, got_dy, [*weights, *peers], other, small
    )
    back_din = exchange(din.reshape(EXPERTS, MOST, width), axes).reshape(-1, width)

    def middle(start):
        out = expert_out(after(hid, start), weight, weights[2], peers[2])
        given = expert_weight_grads(after(own_rows, out), dyw, hid, d_gate, d_up, True)
        return (out, [near_of(piece) for piece in given])

    def outward(out):
        return exchange(out.reshape(EXPERTS, MOST, width), axes).reshape(-1, width)

    def finish(start, received):
        return expert_weight_grads(
            after(own_rows, start), dyw, hid, d_gate, d_up, False, received
        )

    return (back_din, part, din, middle, outward, finish)


def experts_spread(rows_sent, grads_sent, other, router_t, weights):
    ep_count = lax.axis_size("ep")
    weg, weu, wed = weights
    width = rows_sent.shape[1]
    local_count = max(1, EXPERTS // ep_count)
    replicas = max(1, ep_count // EXPERTS)
    groups = EXPERTS // local_count
    gate_cols, up_cols, down_rows = (
        lax.all_gather(weg, SEQ, axis=1, tiled=True),
        lax.all_gather(weu, SEQ, axis=1, tiled=True),
        lax.all_gather(wed, SEQ, axis=0, tiled=True),
    )
    hidden_part = gate_cols.shape[1] // local_count
    gate_local = gate_cols.reshape(width, local_count, hidden_part).transpose(1, 0, 2)
    up_local = up_cols.reshape(width, local_count, hidden_part).transpose(1, 0, 2)
    down_local = down_rows.reshape(local_count, hidden_part, width)

    def spread(buffer):
        last = buffer.shape[-1]
        wide = buffer.reshape(groups, 1, local_count * MOST, last)
        wide = jnp.broadcast_to(wide, (groups, replicas, local_count * MOST, last))
        return exchange(wide.reshape(ep_count, local_count * MOST, last), "ep")

    def collect(buffer):
        last = buffer.shape[-1]
        return jnp.sum(
            exchange(buffer, "ep").astype(WIDE).reshape(groups, replicas, local_count * MOST, last),
            1,
        ).reshape(EXPERTS * MOST, last)

    def owner_layout(received):
        last = received.shape[-1]
        return (
            received.reshape(ep_count, local_count, MOST, last)
            .transpose(1, 0, 2, 3)
            .reshape(local_count, ep_count * MOST, last)
        )

    def source_layout(owned):
        last = owned.shape[-1]
        return (
            owned.reshape(local_count, ep_count, MOST, last)
            .transpose(1, 0, 2, 3)
            .reshape(ep_count, local_count * MOST, last)
        )

    def batched(spec, left_op, right_op):
        return jnp.einsum(spec, left_op, right_op, preferred_element_type=WIDE)

    own_rows = owner_layout(spread(rows_sent))
    got_grads = owner_layout(spread(grads_sent))
    got_other = owner_layout(spread(other[:, None]))
    first = lax.axis_index("ep") // replicas * local_count
    mine = first + jnp.arange(local_count)[:, None, None]
    lane = jnp.arange(EXPERTS)
    logits = batched("lrd,ed->lre", own_rows, router_t)
    hit_mine, hit_other = ((lane == mine).astype(WIDE), (lane == got_other).astype(WIDE))
    got_weight = jax.nn.sigmoid(jnp.sum(logits * (hit_mine - hit_other), -1, keepdims=True))
    gate_val = batched("lrd,ldh->lrh", own_rows, gate_local)
    up_val = batched("lrd,ldh->lrh", own_rows, up_local)
    silu_val, slope_val = silu_grad(gate_val)
    hidden_val = (silu_val * up_val).astype(LOW)
    out_rows = batched("lrh,lhd->lrd", hidden_val, down_local)
    back_out = collect(source_layout((got_weight * out_rows).astype(LOW)))
    grad_hidden = batched("lrd,lhd->lrh", got_grads, down_local)
    row_dot = jnp.sum(hidden_val.astype(WIDE) * grad_hidden, -1, keepdims=True)
    amount = got_weight * (1.0 - got_weight) * row_dot
    d_logits = (amount * (hit_mine - hit_other)).astype(LOW)
    part = jnp.sum(batched("lre,lrd->led", d_logits, own_rows), 0)
    scaled = got_weight * grad_hidden
    own_grads = (got_weight * got_grads.astype(WIDE)).astype(LOW)
    grad_gate = (scaled * up_val * slope_val).astype(LOW)
    grad_up = (scaled * silu_val).astype(LOW)
    din_rows = batched("lrh,ldh->lrd", grad_gate, gate_local)
    din_rows = din_rows + batched("lrh,ldh->lrd", grad_up, up_local)
    din_rows = din_rows + batched("lre,ed->lrd", d_logits, router_t)
    back_din = collect(source_layout(din_rows.astype(LOW)))
    grad_gate_w = batched("lrd,lrh->ldh", own_rows, grad_gate)
    grad_up_w = batched("lrd,lrh->ldh", own_rows, grad_up)
    grad_down_w = batched("lrh,lrd->lhd", hidden_val, own_grads)

    def share(full, axis):
        return lax.psum_scatter(
            full.astype(LOW), SEQ, scatter_dimension=axis, tiled=True
        ).astype(WIDE)

    return (
        back_out.astype(LOW),
        back_din.astype(LOW),
        jnp.pad(part, ((0, EXTRA - EXPERTS), (0, 0))),
        lambda start: (
            share(grad_gate_w.transpose(1, 0, 2).reshape(width, local_count * hidden_part), 1),
            share(grad_up_w.transpose(1, 0, 2).reshape(width, local_count * hidden_part), 1),
            share(grad_down_w.reshape(local_count * hidden_part, width), 0),
        ),
    )


def shards(
    tokens,
    cotangent,
    routes,
    priority,
    gain_attn,
    w_query,
    w_key,
    w_value,
    w_out,
    gain_ffn,
    w_shared_gate,
    w_shared_up,
    w_shared_down,
    w_router,
    w_expert_gate,
    w_expert_up,
    w_expert_down,
):
    tok_rows, width = tokens.shape
    rows_w = w_query.shape[0]
    fs_count = lax.axis_size("fx") * lax.axis_size("fc")
    ep_count = lax.axis_size("ep")
    devices = ep_count * fs_count
    seq_len = tok_rows * fs_count
    head_size = width // HEADS
    side, core = (lax.axis_index("fx"), lax.axis_index("fc"))
    fs_index = side * lax.axis_size("fc") + core
    my_rank = lax.axis_index("ep") * fs_count + fs_index
    my_expert = lax.axis_index("ep") * lax.axis_size("fx") + side
    ids = [core] + [fs_index ^ k for k in range(4)] + [my_expert, lax.axis_index("ep")]
    ids = jnp.stack(ids).astype(jnp.int32)

    small_own = jnp.concatenate([w_router.T, gain_attn[None], gain_ffn[None]], 0)
    small_own = jnp.pad(small_own, ((0, EXTRA - EXPERTS - 2), (0, width - rows_w)))
    pack = jnp.concatenate([tokens, small_own])
    pack_far = far_of(pack)
    qkv_stack = jnp.stack([w_query, w_key, w_value])
    qkv_cut = [
        lax.dynamic_slice_in_dim(qkv_stack, (fs_index ^ k) * rows_w, rows_w, 2) for k in range(4)
    ]

    def to_place(parts):
        got = [
            lax.ppermute(parts[k], SEQ, [(i, i ^ k) for i in range(fs_count)]) for k in (2, 3, 1)
        ]
        return (parts[0], got[2], got[0], got[1])

    w_parts = to_place(qkv_cut)
    x_parts = (pack, near_of(pack), pack_far, near_of(pack_far))

    lane = jnp.arange(2 * EXPERTS)
    classes = jnp.stack([priority, 1 - priority], 1)
    named = routes + EXPERTS * classes
    hits = [(named[:, j : j + 1] == lane).astype(WIDE) for j in (0, 1)]
    both = hits[0] + hits[1]
    lower = (jnp.arange(tok_rows)[:, None] > jnp.arange(tok_rows)[None, :]).astype(LOW)
    before = matmul(lower, both.astype(LOW))
    counts = jnp.sum(both, 0)
    zero_row = jnp.zeros((EXPERTS,), WIDE)
    local_table = before + jnp.concatenate([zero_row, counts[:EXPERTS]])
    slot_iota = jnp.arange(EXPERTS * MOST)
    slot_hit = []
    for j in (0, 1):
        rank = jnp.sum(local_table * hits[j], -1).astype(jnp.int32)
        slot_hit.append(((routes[:, j] * MOST + rank)[:, None] == slot_iota).astype(LOW))
    dispatch = slot_hit[0] + slot_hit[1]
    others = jnp.stack([routes[:, 1], routes[:, 0]]).astype(LOW)
    other_sent = matmul(others[0:1], slot_hit[0]) + matmul(others[1:2], slot_hit[1])
    other_sent = other_sent.reshape(EXPERTS, MOST)
    pair_of_cores = EXPERTS == ep_count * lax.axis_size("fx")
    if pair_of_cores:
        tiny = jnp.concatenate(
            [jnp.broadcast_to(counts[None], (EXPERTS, 2 * EXPERTS)), other_sent], 1
        )
        tiny = jnp.pad(tiny, ((0, 0), (0, 128 - tiny.shape[1]))).astype(jnp.int32)
        tiny = jnp.broadcast_to(tiny[:, None], (EXPERTS, 2, 128)).reshape(devices, 1, 128)
        tiny_got = exchange(tiny, ALL)
        dy_sent = contract_rows(dispatch, cotangent).astype(LOW)
        dy_sent = after(dy_sent, tiny_got, pack_far, *w_parts[2:])
        got_dy = exchange(dy_sent.reshape(EXPERTS, MOST, width), ("ep", "fx"))
        got_dy = got_dy.reshape(-1, width)
        all_counts = tiny_got[:, 0, : 2 * EXPERTS].astype(WIDE)
        other = lax.dynamic_index_in_dim(tiny_got.reshape(EXPERTS, 2, 128), core, 1, keepdims=False)
        other = other[:, 2 * EXPERTS : 2 * EXPERTS + MOST].reshape(EXPERTS * MOST, 1)
    else:
        spread_counts = jnp.broadcast_to(counts.astype(jnp.int32), (devices, 2 * EXPERTS))
        all_counts = exchange(spread_counts, ALL).astype(WIDE)
    earlier = (jnp.arange(devices) < my_rank).astype(WIDE)
    base = jnp.sum(all_counts * earlier[:, None], 0)
    base = base + jnp.concatenate([zero_row, jnp.sum(all_counts[:, :EXPERTS], 0)])
    capacity = 5 * tok_rows * devices // 32
    kept = [(jnp.sum((before + base) * hits[j], -1) < capacity).astype(LOW) for j in (0, 1)]
    dispatch_kept = slot_hit[0] * kept[0][:, None] + slot_hit[1] * kept[1][:, None]

    forward_table, cos_table, sin_table = rope_constants(seq_len, head_size // 2)
    ain, own_mats, (queries, keys, values), lse, att_own, small = attention_forward(
        ids, x_parts, w_parts, jnp.asarray(forward_table)
    )
    out_far = far_of(after(w_out, pack_far, *w_parts[2:]))
    out_parts = (w_out, near_of(after(w_out, pack_far)), out_far, near_of(out_far))
    att_parts = to_place(att_own)
    residual, ffn_input, rows_sent = after_attention(
        att_parts, out_parts, tokens, small, dispatch_kept
    )

    ffn_far = far_of(ffn_input)
    dy_far = far_of(after(cotangent, ffn_far))
    up_stack = jnp.stack([w_shared_gate, w_shared_up])
    ff_part = w_shared_gate.shape[1] // fs_count
    up_own = lax.dynamic_slice_in_dim(up_stack, side * 2 * ff_part, 2 * ff_part, 2)
    up_give = lax.dynamic_slice_in_dim(up_stack, (1 - side) * 2 * ff_part, 2 * ff_part, 2)
    up_far = far_of(after(up_give, dy_far))

    def core_cut(piece, which):
        return lax.dynamic_slice_in_dim(piece, which * ff_part, ff_part, 2)

    up_parts = (
        core_cut(up_own, core),
        near_of(after(core_cut(up_own, 1 - core), ffn_far)),
        core_cut(up_far, core),
        near_of(core_cut(up_far, 1 - core)),
    )
    dy_parts = (cotangent, near_of(after(cotangent, ffn_far)), dy_far, near_of(dy_far))
    ffn_parts = (ffn_input, near_of(ffn_input), ffn_far, near_of(ffn_far))

    def fold(parts):
        mine, give, mid = parts
        got = near_of(give)
        return (mine, got, far_of((mid.astype(WIDE) + got[1].astype(WIDE)).astype(LOW)))

    def shared(start):
        sums, grads = shared_branch(
            ids,
            (after(ffn_parts[0], start), *ffn_parts[1:]),
            dy_parts,
            up_parts,
            w_shared_down,
            ep_count if pair_of_cores else 0,
        )
        return (fold(sums), grads, sums[0])

    def ep_step(block, bit):
        return lax.ppermute(block, "ep", [(i, i ^ bit) for i in range(ep_count)])

    def added(first, second):
        return (first.astype(WIDE) + second.astype(WIDE)).astype(LOW)

    weights = (w_expert_gate, w_expert_up, w_expert_down)
    if pair_of_cores:
        peers = [near_of(after(piece, out_far)) for piece in weights]
        back_din, router_part, din_sent, middle, outward, last = experts_chip(
            ids, rows_sent, got_dy, other, small, weights, peers
        )
        folded, (grads_keep, grads_give), shared_done = shared(din_sent)
        grads_got = ep_step(grads_give, 1)
        expert_out_rows, received = middle(shared_done)
    else:
        dy_sent = contract_rows(dispatch, cotangent).astype(LOW)
        back_out, back_din, router_part, expert_grads = experts_spread(
            rows_sent, dy_sent, other_sent.reshape(-1), small[:EXPERTS], weights
        )
        folded, grads_rest, _ = shared(back_din)

    grad_resid, branch = back_at_tokens(
        folded, back_din, dispatch, residual, small, cotangent, router_part
    )
    branch_far = far_of(branch)
    branch_parts = (branch, near_of(branch), branch_far, near_of(branch_far))
    if pair_of_cores:
        back_out = outward(after(expert_out_rows, branch))
        half = added(grads_keep, after(grads_got, branch))
        half_got = ep_step(half[1::2], 2)
        quarter = added(half[0::2], after(half_got, branch_parts[3]))
        quarter_got = ep_step(quarter[1:2], 4)
    output = finish_output(residual, folded, back_out, dispatch)

    d_qkv, grads_qkv = attention_backward(
        ids, branch_parts, w_out, queries, keys, values, lse, ain, (cos_table, sin_table)
    )
    din_parts, grad_out_w = late_grads(ids, d_qkv, own_mats, att_own, branch_parts)
    in_fold = fold(din_parts)
    own_float = tokens.astype(WIDE)
    grad_in = in_fold[0].astype(WIDE) + in_fold[1][0].astype(WIDE) + in_fold[2].astype(WIDE)
    gain_one = small[EXPERTS : EXPERTS + 1].astype(WIDE)
    grad_tokens = grad_resid + rms_backward(grad_in, own_float, inverse_rms(own_float), gain_one)

    strip = rows_w // ep_count
    grads_qkv = after(grads_qkv, back_out)
    qkv_blocks = grads_qkv.reshape(3, fs_count, ep_count, strip, rows_w).transpose(2, 1, 0, 3, 4)
    qkv_got = exchange(qkv_blocks.reshape(devices, 3, strip, rows_w), ALL)
    qkv_got = qkv_got.reshape(ep_count, fs_count, 3, strip, rows_w).astype(WIDE)
    qkv_sum = jnp.sum(qkv_got, 0).transpose(1, 2, 0, 3).reshape(3 * strip, width).astype(LOW)
    small_part = lax.dynamic_slice_in_dim(grad_out_w[rows_w:], fs_index * rows_w, rows_w, 1)
    if pair_of_cores:
        lines = EXTRA * rows_w // (ep_count * width)
        parts = jnp.concatenate(
            [
                grad_out_w[:rows_w].reshape(ep_count, strip, width),
                small_part.reshape(ep_count, lines, width),
            ],
            1,
        )
        out_sum = halve(parts)
    else:
        lines = 0
        out_whole = lax.psum((grad_out_w[:rows_w], small_part), "ep")
        out_sum = jnp.zeros((0, width), LOW)
    sums = jnp.concatenate([qkv_sum, out_sum])
    sums = exchange(jnp.broadcast_to(sums[None], (ep_count,) + sums.shape), "ep").astype(WIDE)
    qkv_all = sums[:, : 3 * strip].reshape(ep_count, 3, strip, width)
    qkv_all = qkv_all.transpose(1, 0, 2, 3).reshape(3, rows_w, width)
    if pair_of_cores:
        sum_out_w = sums[:, 3 * strip : 4 * strip].reshape(rows_w, width)
        sum_small = sums[:, 4 * strip :].reshape(EXTRA, rows_w)
    else:
        sum_out_w, sum_small = (piece.astype(WIDE) for piece in out_whole)
    sum_gain_one = (
        sum(
            jnp.sum(qkv_all[i] * mat.astype(WIDE), -1)
            for i, mat in enumerate((w_query, w_key, w_value))
        )
        / gain_attn.astype(WIDE)
    )
    sum_router, sum_gain_two = (sum_small[:EXPERTS].T, sum_small[EXPERTS])
    if pair_of_cores:
        expert_grads = last(qkv_blocks, received)
        own_chunk = added(quarter[0:1], after(quarter_got, grads_qkv))
        cut = 2 * rows_w // ep_count
        turned = to_place([own_chunk[0, k * cut : (k + 1) * cut] for k in range(4)])
        own_chunk = jnp.concatenate([*turned, own_chunk[0, 4 * cut :]])[None]
        whole = [own_chunk, ep_step(own_chunk, 4)]
        whole = [jnp.concatenate(whole)]
        whole = [jnp.concatenate([whole[0], ep_step(whole[0], 2)])]
        whole = [whole[0], ep_step(whole[0], 1)]
        wide_all, sum_sdown = place_shared(ids, whole, rows_w, width)
    else:
        expert_grads = expert_grads(grads_qkv)
        dense = lax.psum((*to_place(grads_rest[:4]), grads_rest[4]), "ep")
        sum_sdown = dense[4].astype(WIDE)
        wide_rel = jnp.stack([piece.astype(WIDE) for piece in dense[:4]])
        wide_all = jnp.concatenate(
            [
                lax.dynamic_index_in_dim(wide_rel, fs_index ^ k, 0, keepdims=False)
                for k in range(4)
            ],
            2,
        )
    return (
        output,
        grad_tokens,
        sum_gain_one,
        qkv_all[0],
        qkv_all[1],
        qkv_all[2],
        sum_out_w,
        sum_gain_two,
        wide_all[0],
        wide_all[1],
        sum_sdown,
        sum_router,
        *expert_grads,
    )


def solution(mesh):
    ep_count, fs_count = mesh.devices.shape
    cut_mesh = Mesh(mesh.devices.reshape(ep_count, fs_count // 2, 2), ALL)
    tok = P(ALL, None)
    row = P(SEQ, None)
    return jax.shard_map(
        shards,
        mesh=cut_mesh,
        in_specs=(
            tok,
            tok,
            tok,
            P(ALL),
            P(SEQ),
            row,
            row,
            row,
            row,
            P(SEQ),
            row,
            row,
            row,
            row,
            P(None, ALL),
            P(None, ALL),
            tok,
        ),
        out_specs=(
            tok,
            tok,
            P(SEQ),
            row,
            row,
            row,
            row,
            P(SEQ),
            row,
            row,
            row,
            row,
            P(None, ALL),
            P(None, ALL),
            tok,
        ),
        check_vma=False,
    )
```

```python
import jax
import jax.numpy as jnp
import numpy as np
from jax import lax
from jax.experimental import pallas as pl
from jax.experimental.pallas import tpu as pltpu
from jax.sharding import Mesh
from jax.sharding import PartitionSpec as P

HEADS = 12
EXPERTS = 16
MOST = 48
EXTRA = 2 * EXPERTS
LIGHT = 20

EPS = 1e-06
NEG = -1e30
LOW = jnp.bfloat16
WIDE = jnp.float32
ALL = ("ep", "fx", "fc")
SEQ = ("fx", "fc")
SWAP = [(0, 1), (1, 0)]
VMEM = pl.BlockSpec(memory_space=pltpu.VMEM)
SMEM = pl.BlockSpec(memory_space=pltpu.SMEM)


def matmul(left_op, right_op):
    return jnp.dot(left_op, right_op, preferred_element_type=WIDE)


def contract_rows(left_op, right_op):
    return lax.dot_general(left_op, right_op, (((0,), (0,)), ((), ())), preferred_element_type=WIDE)


def contract_cols(left_op, right_op):
    return lax.dot_general(left_op, right_op, (((1,), (1,)), ((), ())), preferred_element_type=WIDE)


def inverse_rms(values):
    return lax.rsqrt(jnp.mean(values * values, -1, keepdims=True) + EPS)


def rms_backward(upstream, values, inverse, gain_vec):
    scaled = upstream * gain_vec
    return inverse * scaled - values * inverse**3 * jnp.mean(scaled * values, -1, keepdims=True)


def silu_grad(gate_val):
    sigma = jax.nn.sigmoid(gate_val)
    return (gate_val * sigma, sigma * (1.0 + gate_val * (1.0 - sigma)))


def far_of(block):
    return lax.ppermute(block, "fx", SWAP)


def near_of(block):
    return lax.ppermute(block, "fc", SWAP)


def after(value, *others):
    return lax.optimization_barrier((value, *others))[0]


def tie(values, *others):
    return lax.optimization_barrier((*values, *others))[: len(values)]


def exchange(blocks, axes):
    return lax.all_to_all(blocks, axes, split_axis=0, concat_axis=0, tiled=True)


def split_part(parts, bit):
    cut = parts.reshape((parts.shape[0] // 2, 2) + parts.shape[1:])
    mine = lax.rem(lax.axis_index("ep") // bit, 2)
    keep = lax.dynamic_index_in_dim(cut, mine, 1, keepdims=False)
    return (keep, lax.dynamic_index_in_dim(cut, 1 - mine, 1, keepdims=False))


def shape_of(dims, kind):
    return jax.ShapeDtypeStruct(dims, kind)


def run_kernel(body, outs, args, specs=None, out_specs=None, scratch=(), grid=None, flops=0, move=0):
    options = {} if grid is None else {"grid": grid}
    return pl.pallas_call(
        body,
        out_shape=outs,
        in_specs=specs if specs is not None else [VMEM] * len(args),
        out_specs=out_specs if out_specs is not None else [VMEM] * len(outs),
        scratch_shapes=list(scratch),
        compiler_params=pltpu.CompilerParams(vmem_limit_bytes=52 * 2**20),
        cost_estimate=pl.CostEstimate(
            flops=flops // LIGHT, bytes_accessed=move // LIGHT, transcendentals=0
        ),
        **options,
    )(*args)


def pick_rows(first_iota, second_iota, source):
    return (first_iota == source(second_iota)).astype(LOW)


def rope_constants(length, half):
    freq = np.exp(-np.log(np.float32(10000.0)) * np.arange(half, dtype=np.float32) / np.float32(half))
    angle = np.arange(length, dtype=np.float32)[:, None] * freq.astype(np.float32)[None, :]
    cosine, sine = (np.cos(angle), np.sin(angle))
    return (
        np.concatenate([cosine, cosine, sine, sine], 1).astype(np.float32),
        np.concatenate([cosine] * 4, 1).astype(np.float32),
        np.concatenate([sine, -sine, sine, -sine], 1).astype(np.float32),
    )


def attention_forward(ids, x_parts, w_parts, table):
    full, width = x_parts[0].shape
    rows = full - EXTRA
    block = w_parts[0].shape[1]
    length = 4 * rows
    heads = block // 64
    size = heads * 128

    def body(ids_ref, *refs):
        x_refs, w_refs, table_ref = (refs[:4], refs[4:8], refs[8])
        ain_ref, own_ref, q_ref, k_ref, v_ref, lse_ref = refs[9:15]
        att_refs, small_ref = (refs[15:19], refs[19])
        att_scr = refs[20]
        first = lax.broadcasted_iota(jnp.int32, (block, width), 0)
        lane = lax.broadcasted_iota(jnp.int32, (block, width), 1)
        small = jnp.zeros((EXTRA, width), WIDE)
        for k in range(4):
            place = jnp.where(lane == first + ids_ref[1 + k] * block, 1.0, 0.0).astype(LOW)
            small = small + matmul(x_refs[k][rows:, :block], place)
        small_ref[...] = small.astype(LOW)
        gain = small[EXPERTS : EXPERTS + 1, :]
        for k in range(4):
            place = ids_ref[1 + k]
            piece = x_refs[k][:rows, :].astype(WIDE)
            ain_ref[pl.ds(place * rows, rows), :] = (piece * inverse_rms(piece) * gain).astype(LOW)
            for m in range(3):
                own_ref[m, pl.ds(place * block, block), :] = w_refs[k][m]
        first = lax.broadcasted_iota(jnp.int32, (block, size), 0)
        lane = lax.broadcasted_iota(jnp.int32, (block, size), 1)
        head, inner = (lane // 128, lane % 128)
        low = inner % 64
        swapped = jnp.where(low < 32, low + 32, low - 32)
        source = 64 * head + jnp.where(inner < 64, low, swapped)
        sign = jnp.where((inner >= 64) & (low < 32), -1.0, 1.0)
        turn = jnp.where(first == source, sign, 0.0).astype(LOW)
        keep = (inner // 64 == head % 2) & (first == 64 * head + low)
        place_v = jnp.where(keep, 1.0, 0.0).astype(LOW)
        w_q = matmul(own_ref[0], turn).astype(LOW)
        w_k = matmul(own_ref[1], turn).astype(LOW)
        w_v = matmul(own_ref[2], place_v).astype(LOW)
        half = lax.broadcasted_iota(jnp.int32, (rows, 128), 1) < 64
        for i in range(4):
            span = slice(i * rows, (i + 1) * rows)
            ain = ain_ref[span, :]
            y_q, y_k, y_v = (matmul(ain, w_q), matmul(ain, w_k), matmul(ain, w_v))
            tab = table_ref[span, :]
            for h in range(heads):
                cols = slice(128 * h, 128 * h + 128)
                turned = y_q[:, cols] * tab
                turned = (turned + pltpu.roll(turned, 64, 1)).astype(LOW).astype(WIDE)
                q_ref[h, span, :] = jnp.where(half, turned * 0.125, 0.0).astype(LOW)
                turned = y_k[:, cols] * tab
                k_ref[h, span, :] = (turned + pltpu.roll(turned, 64, 1)).astype(LOW)
                v_ref[h, span, :] = y_v[:, cols].astype(LOW)
        tri = lax.broadcasted_iota(jnp.int32, (rows, rows), 0) >= lax.broadcasted_iota(
            jnp.int32, (rows, rows), 1
        )
        for i in range(4):
            span = slice(i * rows, (i + 1) * rows)
            done = slice(0, i * rows)
            tiles = []
            for h in range(heads):
                query = q_ref[h, span, :]
                diag = jnp.where(tri, contract_cols(query, k_ref[h, span, :]), NEG)
                top = jnp.max(diag, -1, keepdims=True)
                if i:
                    past = contract_cols(query, k_ref[h, done, :])
                    top = jnp.maximum(top, jnp.max(past, -1, keepdims=True))
                diag = jnp.exp(diag - top)
                total = jnp.sum(diag, -1, keepdims=True)
                if i:
                    past = jnp.exp(past - top)
                    total = total + jnp.sum(past, -1, keepdims=True)
                scale = 1.0 / total
                out = matmul((diag * scale).astype(LOW), v_ref[h, span, :])
                if i:
                    out = out + matmul((past * scale).astype(LOW), v_ref[h, done, :])
                lse_ref[h, span, :] = top + jnp.log(total)
                tiles.append(out)
            for t in range((heads + 1) // 2):
                pair = tiles[2 * t] + (tiles[2 * t + 1] if 2 * t + 1 < heads else 0.0)
                wide = min(128, block - 128 * t)
                att_scr[span, 128 * t : 128 * t + wide] = pair[:, :wide].astype(LOW)
        for k in range(4):
            att_refs[k][...] = att_scr[pl.ds(ids_ref[1 + k] * rows, rows), :]

    outs = (
        [shape_of((length, width), LOW), shape_of((3, width, block), LOW)]
        + [shape_of((heads, length, 128), LOW)] * 3
        + [shape_of((heads, length, 1), WIDE)]
        + [shape_of((rows, block), LOW)] * 4
        + [shape_of((EXTRA, width), LOW)]
    )
    args = [ids, *x_parts, *w_parts, table]
    got = run_kernel(
        body,
        outs,
        args,
        specs=[SMEM] + [VMEM] * (len(args) - 1),
        scratch=[pltpu.VMEM((length, block), LOW)],
        flops=8 * 10**9,
        move=12 * 10**6,
    )
    return (got[0], got[1], got[2:5], got[5], got[6:10], got[10])


def after_attention(att_parts, out_parts, tokens, small):
    rows, width = tokens.shape

    def body(*refs):
        att_refs, out_refs = (refs[:4], refs[4:8])
        tok_ref, small_ref, res_ref, ffn_ref = refs[8:]
        total = tok_ref[...].astype(WIDE)
        for k in range(4):
            total = total + matmul(att_refs[k][...], out_refs[k][...])
        res_ref[...] = total
        gain = small_ref[EXPERTS + 1 : EXPERTS + 2, :].astype(WIDE)
        ffn_ref[...] = (total * inverse_rms(total) * gain).astype(LOW)

    outs = [shape_of((rows, width), WIDE), shape_of((rows, width), LOW)]
    args = [*att_parts, *out_parts, tokens, small]
    return run_kernel(body, outs, args, flops=6 * 10**8, move=4 * 10**6)


def send_pair(ids, hits, blocks):
    rows, width = blocks[0].shape
    groups = hits[0].shape[1] // MOST

    def body(ids_ref, own_hit, far_hit, own_ref, far_ref, out_ref):
        for hit, block, place in (
            (own_hit, own_ref, ids_ref[7]),
            (far_hit, far_ref, 1 - ids_ref[7]),
        ):
            sent = contract_rows(hit[...], block[...]).astype(LOW)
            for g in range(groups):
                out_ref[g, place] = sent[g * MOST : (g + 1) * MOST, :]

    return run_kernel(
        body,
        [shape_of((groups, 2, MOST, width), LOW)],
        [ids, *hits, *blocks],
        specs=[SMEM] + [VMEM] * 4,
        flops=6 * 10**8,
        move=3 * 10**6,
    )[0]


def take_pair(ids, hits, back, sums, near_sum, residual):
    groups, _, _, width = back.shape
    rows = residual.shape[0]

    def body(ids_ref, own_hit, far_hit, back_ref, mine_ref, mid_ref, near_ref, res_ref, own_out, far_out):
        own = res_ref[...] + mine_ref[...].astype(WIDE) + near_ref[0].astype(WIDE)
        far = mid_ref[...].astype(WIDE) + near_ref[1].astype(WIDE)
        for g in range(groups):
            cols = slice(g * MOST, (g + 1) * MOST)
            own = own + matmul(own_hit[:, cols], back_ref[g, ids_ref[7]])
            far = far + matmul(far_hit[:, cols], back_ref[g, 1 - ids_ref[7]])
        own_out[...] = own
        far_out[...] = far.astype(LOW)

    return run_kernel(
        body,
        [shape_of((rows, width), WIDE), shape_of((rows, width), LOW)],
        [ids, *hits, back, sums[0], sums[2], near_sum, residual],
        specs=[SMEM] + [VMEM] * 7,
        flops=6 * 10**8,
        move=5 * 10**6,
    )


def shared_branch(ids, ffn_parts, dy_parts, w_parts, down, chunks):
    rows, width = ffn_parts[0].shape
    block, hidden = w_parts[0].shape[1:]

    def body(ids_ref, *refs):
        ffn_refs, dy_refs, w_refs = (refs[:4], refs[4:8], refs[8:12])
        down_ref = refs[12]
        sum_refs, grad_refs = (refs[13:19], refs[19:-3])
        w_scr, g_scr, d_scr = refs[-3:]
        for k in range(4):
            for m in range(2):
                w_scr[m, pl.ds(ids_ref[1 + k] * block, block), :] = w_refs[k][m]
        for k in range(4):
            ffn, dy = (ffn_refs[k][...], dy_refs[k][...])
            gate, up = (matmul(ffn, w_scr[0]), matmul(ffn, w_scr[1]))
            silu, slope = silu_grad(gate)
            hid = (silu * up).astype(LOW)
            back = contract_cols(dy, down_ref[...])
            d_gate = (back * up * slope).astype(LOW)
            d_up = (back * silu).astype(LOW)
            din = (contract_cols(d_gate, w_scr[0]) + contract_cols(d_up, w_scr[1])).astype(LOW)
            out = matmul(hid, down_ref[...]).astype(LOW)
            for n, value in enumerate((din, out)):
                mine_ref, near_ref, mid_ref = sum_refs[3 * n : 3 * n + 3]
                if k % 2 == 0:
                    target = mine_ref if k == 0 else mid_ref
                    target[...] = value
                else:
                    near_ref[k // 2] = value
            parts = (contract_rows(ffn, d_gate), contract_rows(ffn, d_up), contract_rows(hid, dy))
            if k == 0:
                g_scr[0], g_scr[1], d_scr[...] = parts
            else:
                g_scr[0] += parts[0]
                g_scr[1] += parts[1]
                d_scr[...] += parts[2]
        if chunks:
            per = chunks // 2
            cut, line = (block // per, hidden // chunks)
            for r in range(chunks):
                part = ids_ref[6] ^ r
                target = grad_refs[r % 2]
                which, low = (part // per, part % per)
                for k in range(4):
                    start = ids_ref[1 + k] * block + low * cut
                    target[r // 2, k * cut : (k + 1) * cut, :] = g_scr[
                        which, pl.ds(pl.multiple_of(start, 16), cut), :
                    ].astype(LOW)
                start = pl.multiple_of(part * line, 16)
                piece = d_scr[pl.ds(start, line), :].astype(LOW)
                base = 4 * cut
                target[r // 2, base : base + line, :] = piece[:, :hidden]
                target[r // 2, base + line :, : hidden // 2] = piece[: line // 2, hidden:]
                target[r // 2, base + line :, hidden // 2 :] = piece[line // 2 :, hidden:]
        else:
            for k in range(4):
                for m in range(2):
                    grad_refs[k][m] = g_scr[m, pl.ds(ids_ref[1 + k] * block, block), :].astype(LOW)
            grad_refs[4][...] = d_scr[...].astype(LOW)

    if chunks:
        lines = 4 * block * 2 // chunks + 3 * hidden // chunks // 2
        grad_outs = [shape_of((chunks // 2, lines, hidden), LOW)] * 2
    else:
        grad_outs = [shape_of((2, block, hidden), LOW)] * 4 + [shape_of((hidden, width), LOW)]
    sums = [shape_of((rows, width), LOW), shape_of((2, rows, width), LOW), shape_of((rows, width), LOW)]
    outs = sums * 2 + grad_outs
    args = [ids, *ffn_parts, *dy_parts, *w_parts, down]
    got = run_kernel(
        body,
        outs,
        args,
        specs=[SMEM] + [VMEM] * (len(args) - 1),
        scratch=[
            pltpu.VMEM((2, width, hidden), LOW),
            pltpu.VMEM((2, width, hidden), WIDE),
            pltpu.VMEM((hidden, width), WIDE),
        ],
        flops=7 * 10**9,
        move=14 * 10**6,
    )
    return (got[0:3], got[3:6], got[6:])


def place_shared(ids, groups, block, width):
    per_group, lines, hidden = groups[0].shape
    chunks = per_group * len(groups)
    per = chunks // 2
    cut, line = (block // per, hidden // chunks)
    order = (0, 4, 2, 6, 1, 5, 3, 7)

    def body(ids_ref, *refs):
        gate_ref, up_ref, down_ref = refs[-3:]
        for n in range(chunks):
            part = ids_ref[6] ^ order[n]
            which, low = (part // per, part % per)
            piece = refs[n // per_group][n % per_group].astype(WIDE)
            for k in range(4):
                lane = pl.multiple_of(ids_ref[1 + k] * hidden, 128)
                value = piece[k * cut : (k + 1) * cut, :]
                place = (pl.ds(pl.multiple_of(low * cut, 16), cut), pl.ds(lane, hidden))

                @pl.when(which == 0)
                def to_gate(place=place, value=value):
                    gate_ref[place] = value

                @pl.when(which == 1)
                def to_up(place=place, value=value):
                    up_ref[place] = value

            base = 4 * cut
            start = pl.multiple_of(part * line, 16)
            down_ref[pl.ds(start, line), :hidden] = piece[base : base + line, :]
            tail = piece[base + line :, :]
            down_ref[pl.ds(start, line // 2), hidden:] = tail[:, : hidden // 2]
            down_ref[pl.ds(start + line // 2, line // 2), hidden:] = tail[:, hidden // 2 :]

    return run_kernel(
        body,
        [shape_of((block, 4 * hidden), WIDE)] * 2 + [shape_of((hidden, width), WIDE)],
        [ids, *groups],
        specs=[SMEM] + [VMEM] * len(groups),
        move=8 * 10**6,
    )


def place_dense(sums, w_parts, gain, strip):
    parts, lines, width = sums.shape
    block = parts * strip

    def body(sums_ref, a_ref, b_ref, c_ref, gain_ref, *outs):
        gain_sum = jnp.zeros((block, 1), WIDE)
        for m, w_ref in enumerate((a_ref, b_ref, c_ref)):
            for p in range(parts):
                outs[m][p * strip : (p + 1) * strip, :] = sums_ref[
                    p, m * strip : (m + 1) * strip, :
                ].astype(WIDE)
            gain_sum = gain_sum + jnp.sum(outs[m][...] * w_ref[...].astype(WIDE), -1, keepdims=True)
        for p in range(parts):
            outs[3][p * strip : (p + 1) * strip, :] = sums_ref[
                p, 3 * strip : 4 * strip, :
            ].astype(WIDE)
        outs[4][...] = gain_sum / gain_ref[...].astype(WIDE)

    return run_kernel(
        body,
        [shape_of((block, width), WIDE)] * 4 + [shape_of((block, 1), WIDE)],
        [sums, *w_parts, gain],
        move=5 * 10**6,
    )


def expert_main(ids, rows_in, dy_in, mats, other, router_t):
    count, width = rows_in.shape
    own_hidden = mats[0].shape[1]
    tile = 512
    steps = 2 * own_hidden // tile
    half = steps // 2
    chunk = 256

    def body(ids_ref, rows_ref, dy_ref, *refs):
        own, peer = (refs[0:3], refs[3:6])
        other_ref, router_ref = refs[6:8]
        din_ref, hid_ref, dg_ref, du_ref, dyw_ref, w_ref, part_ref = refs[8:15]
        acc, dot_scr = refs[15:17]
        step = pl.program_id(0)
        expert = ids_ref[5]

        @pl.when(step == 0)
        def start():
            for r in range(0, count, chunk):
                span = slice(r, r + chunk)
                logits = contract_cols(rows_ref[span, :], router_ref[...])
                lane = lax.broadcasted_iota(jnp.int32, logits.shape, 1)
                mine = jnp.sum(jnp.where(lane == expert, logits, 0.0), -1, keepdims=True)
                rest = jnp.sum(jnp.where(lane == other_ref[span, :], logits, 0.0), -1, keepdims=True)
                weight = jax.nn.sigmoid(mine - rest)
                w_ref[span, :] = weight
                dyw_ref[span, :] = (weight * dy_ref[span, :].astype(WIDE)).astype(LOW)
                dot_scr[span, :] = jnp.zeros((chunk, 1), WIDE)
                acc[span, :] = jnp.zeros((chunk, width), WIDE)

        def work(gate_ref, up_ref, down_ref):
            for r in range(0, count, chunk):
                span = slice(r, r + chunk)
                rows = rows_ref[span, :]
                gate, up = (matmul(rows, gate_ref[...]), matmul(rows, up_ref[...]))
                back = contract_cols(dy_ref[span, :], down_ref[...])
                silu, slope = silu_grad(gate)
                hid = (silu * up).astype(LOW)
                hid_ref[span, :] = hid
                dot_scr[span, :] += jnp.sum(hid.astype(WIDE) * back, -1, keepdims=True)
                scaled = w_ref[span, :] * back
                d_gate = (scaled * up * slope).astype(LOW)
                d_up = (scaled * silu).astype(LOW)
                dg_ref[span, :] = d_gate
                du_ref[span, :] = d_up
                acc[span, :] += contract_cols(d_gate, gate_ref[...]) + contract_cols(
                    d_up, up_ref[...]
                )

        @pl.when(step < half)
        def first():
            work(*own)

        @pl.when(step >= half)
        def second():
            work(*peer)

        @pl.when(step == steps - 1)
        def finish():
            for r in range(0, count, chunk):
                span = slice(r, r + chunk)
                weight = w_ref[span, :]
                amount = weight * (1.0 - weight) * dot_scr[span, :]
                lane = lax.broadcasted_iota(jnp.int32, (chunk, EXTRA), 1)
                signs = jnp.where(lane == expert, 1.0, 0.0) - jnp.where(
                    lane == other_ref[span, :], 1.0, 0.0
                )
                d_logit = (amount * signs).astype(LOW)
                din_ref[span, :] = (acc[span, :] + matmul(d_logit, router_ref[...])).astype(LOW)
                part = contract_rows(d_logit, rows_ref[span, :])
                part_ref[...] = part if r == 0 else part_ref[...] + part

    def fixed(dims):
        return pl.BlockSpec(dims, lambda j: (0,) * len(dims))

    def near(j):
        return jnp.minimum(j, half - 1)

    def late(j):
        return jnp.maximum(j - half, 0)

    cols = (width, tile)
    specs = [SMEM, fixed((count, width)), fixed((count, width))]
    for place in (near, late):
        specs += [
            pl.BlockSpec(cols, lambda j, place=place: (0, place(j))),
            pl.BlockSpec(cols, lambda j, place=place: (0, place(j))),
            pl.BlockSpec((tile, width), lambda j, place=place: (place(j), 0)),
        ]
    specs += [fixed((count, 1)), fixed(router_t.shape)]
    tiles = pl.BlockSpec((count, tile), lambda j: (0, j))
    outs = (
        [shape_of((count, width), LOW)]
        + [shape_of((count, 2 * own_hidden), LOW)] * 3
        + [shape_of((count, width), LOW), shape_of((count, 1), WIDE), shape_of(router_t.shape, WIDE)]
    )
    out_specs = [
        fixed((count, width)),
        tiles,
        tiles,
        tiles,
        fixed((count, width)),
        fixed((count, 1)),
        fixed(router_t.shape),
    ]
    return run_kernel(
        body,
        outs,
        [ids, rows_in, dy_in, *mats, other, router_t],
        specs=specs,
        out_specs=out_specs,
        scratch=[pltpu.VMEM((count, width), WIDE), pltpu.VMEM((count, 1), WIDE)],
        grid=(steps,),
        flops=12 * 10**9,
        move=22 * 10**6,
    )


def expert_out(hid, weight, down_own, down_peer):
    count, hidden = hid.shape
    width = down_own.shape[1]
    half = hidden // 2
    chunk = 256

    def body(hid_ref, w_ref, own_ref, peer_ref, out_ref):
        for r in range(0, count, chunk):
            span = slice(r, r + chunk)
            total = matmul(hid_ref[span, :half], own_ref[...])
            total = total + matmul(hid_ref[span, half:], peer_ref[...])
            out_ref[span, :] = (w_ref[span, :] * total).astype(LOW)

    return run_kernel(
        body,
        [shape_of((count, width), LOW)],
        [hid, weight, down_own, down_peer],
        flops=2 * 10**9,
        move=8 * 10**6,
    )[0]


def expert_weight_grads(rows_in, dyw, hid, d_gate, d_up, peer, add=None):
    count, width = rows_in.shape
    half = hid.shape[1] // 2
    tile = 512
    steps = half // tile
    offset = steps if peer else 0
    kind = LOW if add is None else WIDE

    def body(rows_ref, dyw_ref, hid_ref, dg_ref, du_ref, *refs):
        outs = refs[-3:]
        grads = (
            contract_rows(rows_ref[...], dg_ref[...]),
            contract_rows(rows_ref[...], du_ref[...]),
            contract_rows(hid_ref[...], dyw_ref[...]),
        )
        for i in range(3):
            value = grads[i] if add is None else grads[i] + refs[i][...].astype(WIDE)
            outs[i][...] = value.astype(kind)

    def fixed(dims):
        return pl.BlockSpec(dims, lambda j: (0,) * len(dims))

    tiles = pl.BlockSpec((count, tile), lambda j: (0, j + offset))
    cols = pl.BlockSpec((width, tile), lambda j: (0, j))
    lines = pl.BlockSpec((tile, width), lambda j: (j, 0))
    specs = [fixed((count, width)), fixed((count, width)), tiles, tiles, tiles]
    extra = [] if add is None else list(add)
    return run_kernel(
        body,
        [shape_of((width, half), kind), shape_of((width, half), kind), shape_of((half, width), kind)],
        [rows_in, dyw, hid, d_gate, d_up, *extra],
        specs=specs + ([] if add is None else [cols, cols, lines]),
        out_specs=[cols, cols, lines],
        grid=(steps,),
        flops=37 * 10**8,
        move=14 * 10**6,
    )


def back_at_tokens(fold, back_din, dispatch, residual, small, cotangent, router_part):
    rows, width = residual.shape

    def body(one_ref, two_ref, last_ref, back_ref, disp_ref, res_ref, small_ref, dy_ref, part_ref, dres_ref, br_ref):
        d_ffn = one_ref[...].astype(WIDE) + two_ref[0].astype(WIDE) + last_ref[...].astype(WIDE)
        d_ffn = d_ffn + matmul(disp_ref[...], back_ref[...])
        residual_val = res_ref[...]
        inverse = inverse_rms(residual_val)
        gain = small_ref[EXPERTS + 1 : EXPERTS + 2, :].astype(WIDE)
        d_res = dy_ref[...].astype(WIDE) + rms_backward(d_ffn, residual_val, inverse, gain)
        dres_ref[...] = d_res
        br_ref[0:rows, :] = d_res.astype(LOW)
        gain_part = jnp.sum(d_ffn * residual_val * inverse, 0, keepdims=True)
        line = lax.broadcasted_iota(jnp.int32, (EXTRA, width), 0)
        extra = jnp.where(line == EXPERTS, gain_part, part_ref[...])
        br_ref[rows:, :] = extra.astype(LOW)

    return run_kernel(
        body,
        [shape_of((rows, width), WIDE), shape_of((rows + EXTRA, width), LOW)],
        [*fold, back_din, dispatch, residual, small, cotangent, router_part],
        flops=3 * 10**8,
        move=5 * 10**6,
    )


def attention_backward(ids, branch, w_out, queries, keys, values, lse, ain, tables, groups):
    heads, length, _ = queries.shape
    rows = length // 4
    block, width = w_out.shape
    tiles = (heads + 1) // 2
    strip = block // groups

    def body(ids_ref, *refs):
        br_refs = refs[:4]
        wo_ref, q_ref, k_ref, v_ref, lse_ref, ain_ref, cc_ref, ss_ref = refs[4:12]
        d_ref, g_ref = refs[12:14]
        da_scr, dk_scr, dv_scr = refs[14:17]
        zero = jnp.zeros((rows, 128), WIDE)
        for k in range(4):
            d_att = contract_cols(br_refs[k][0:rows, :], wo_ref[...]).astype(LOW)
            place = ids_ref[1 + k] * rows
            for t in range(tiles):
                wide = min(128, block - 128 * t)
                if wide < 128:
                    da_scr[t, pl.ds(place, rows), :] = zero.astype(LOW)
                da_scr[t, pl.ds(place, rows), 0:wide] = d_att[:, 128 * t : 128 * t + wide]
        half = lax.broadcasted_iota(jnp.int32, (rows, 128), 1) < 64
        tri = lax.broadcasted_iota(jnp.int32, (rows, rows), 0) >= lax.broadcasted_iota(
            jnp.int32, (rows, rows), 1
        )

        def place_tile(m, span, h, value):
            t = h // 2
            wide = min(128, block - 128 * t)
            if h % 2 == 0:
                d_ref[m, span, 128 * t : 128 * t + wide] = value[:, :wide].astype(LOW)
            else:
                kept = d_ref[m, span, 128 * t : 128 * t + 128].astype(WIDE)
                d_ref[m, span, 128 * t : 128 * t + 128] = jnp.where(half, kept, value).astype(LOW)

        def unturn(value, span):
            return value * cc_ref[span, :] + pltpu.roll(value, 32, 1) * ss_ref[span, :]

        for h in range(heads):
            for i in range(4):
                span = slice(i * rows, (i + 1) * rows)
                done = slice(0, i * rows)
                query = q_ref[h, span, :]
                d_att = da_scr[h // 2, span, :]
                level = lse_ref[h, span, :]
                diag = contract_cols(query, k_ref[h, span, :]) - level
                diag = jnp.exp(jnp.where(tri, diag, NEG))
                d_diag = contract_cols(d_att, v_ref[h, span, :])
                inner = jnp.sum(diag * d_diag, -1, keepdims=True)
                if i:
                    past = jnp.exp(contract_cols(query, k_ref[h, done, :]) - level)
                    d_past = contract_cols(d_att, v_ref[h, done, :])
                    inner = inner + jnp.sum(past * d_past, -1, keepdims=True)
                d_diag = (diag * (d_diag - inner)).astype(LOW)
                d_query = matmul(d_diag, k_ref[h, span, :])
                dk_scr[span, :] = contract_rows(d_diag, query)
                dv_scr[span, :] = contract_rows(diag.astype(LOW), d_att)
                if i:
                    d_past = (past * (d_past - inner)).astype(LOW)
                    d_query = d_query + matmul(d_past, k_ref[h, done, :])
                    dk_scr[done, :] += contract_rows(d_past, query)
                    dv_scr[done, :] += contract_rows(past.astype(LOW), d_att)
                place_tile(0, span, h, unturn(d_query * 0.125, span))
            for i in range(4):
                span = slice(i * rows, (i + 1) * rows)
                d_key = dk_scr[span, :]
                place_tile(1, span, h, unturn(d_key + pltpu.roll(d_key, 64, 1), span))
                place_tile(2, span, h, dv_scr[span, :])
        for m in range(3):
            grad = contract_rows(ain_ref[...], d_ref[m])
            for f in range(4):
                for e in range(groups):
                    start = f * block + e * strip
                    g_ref[4 * e + f, m] = grad[start : start + strip, :].astype(LOW)

    args = [ids, *branch, w_out, queries, keys, values, lse, ain, *tables]
    return run_kernel(
        body,
        [shape_of((3, length, block), LOW), shape_of((4 * groups, 3, strip, block), LOW)],
        args,
        specs=[SMEM] + [VMEM] * (len(args) - 1),
        scratch=[
            pltpu.VMEM((tiles, length, 128), LOW),
            pltpu.VMEM((length, 128), WIDE),
            pltpu.VMEM((length, 128), WIDE),
        ],
        flops=16 * 10**9,
        move=12 * 10**6,
    )


def late_grads(ids, d_qkv, own_mats, att_parts, branch):
    length, block = d_qkv.shape[1:]
    rows = length // 4
    width = own_mats.shape[1]
    extra = branch[0].shape[0] - rows

    def body(ids_ref, d_ref, w_ref, *refs):
        att_refs, br_refs = (refs[:4], refs[4:8])
        mine_ref, near_ref, mid_ref, gout_ref = refs[8:12]
        for k in range(4):
            span = pl.ds(ids_ref[1 + k] * rows, rows)
            total = contract_cols(d_ref[0, span, :], w_ref[0])
            for m in range(1, 3):
                total = total + contract_cols(d_ref[m, span, :], w_ref[m])
            if k % 2 == 0:
                target = mine_ref if k == 0 else mid_ref
                target[...] = total.astype(LOW)
            else:
                near_ref[k // 2] = total.astype(LOW)
        gout = contract_rows(att_refs[0][...], br_refs[0][0:rows, :])
        small = br_refs[0][rows:, :].astype(WIDE)
        for k in range(1, 4):
            gout = gout + contract_rows(att_refs[k][...], br_refs[k][0:rows, :])
            small = small + br_refs[k][rows:, :].astype(WIDE)
        gout_ref[0:block, :] = gout.astype(LOW)
        gout_ref[block:, :] = small.astype(LOW)

    args = [ids, d_qkv, own_mats, *att_parts, *branch]
    got = run_kernel(
        body,
        [
            shape_of((rows, width), LOW),
            shape_of((2, rows, width), LOW),
            shape_of((rows, width), LOW),
            shape_of((block + extra, width), LOW),
        ],
        args,
        specs=[SMEM] + [VMEM] * (len(args) - 1),
        flops=12 * 10**8,
        move=7 * 10**6,
    )
    return (got[:3], got[3])


def experts_chip(ids, rows_sent, got_dy, other, small, weights, peers, ready):
    width = rows_sent.shape[-1]
    axes = ("ep", "fx")
    own_rows = exchange(rows_sent, "ep").reshape(-1, width)
    own_rows = after(own_rows, *ready)
    din, hid, d_gate, d_up, dyw, weight, part = expert_main(
        ids, own_rows, got_dy, [*weights, *peers], other, small
    )

    def homeward(sent):
        return exchange(sent.reshape(EXPERTS, MOST, width), axes).reshape(-1, width)

    def middle(start):
        return expert_out(after(hid, start), weight, weights[2], peers[2])

    def give(start):
        given = expert_weight_grads(after(own_rows, start), dyw, hid, d_gate, d_up, True)
        return [near_of(piece) for piece in given]

    def outward(out):
        return exchange(out.reshape(EXPERTS // 2, 2, MOST, width), "ep")

    def finish(start, received):
        return expert_weight_grads(
            after(own_rows, start), dyw, hid, d_gate, d_up, False, received
        )

    return (din, part, homeward, middle, outward, give, finish)


def experts_spread(rows_sent, grads_sent, other, router_t, weights):
    ep_count = lax.axis_size("ep")
    weg, weu, wed = weights
    width = rows_sent.shape[1]
    local_count = max(1, EXPERTS // ep_count)
    replicas = max(1, ep_count // EXPERTS)
    groups = EXPERTS // local_count
    gate_cols, up_cols, down_rows = (
        lax.all_gather(weg, SEQ, axis=1, tiled=True),
        lax.all_gather(weu, SEQ, axis=1, tiled=True),
        lax.all_gather(wed, SEQ, axis=0, tiled=True),
    )
    hidden_part = gate_cols.shape[1] // local_count
    gate_local = gate_cols.reshape(width, local_count, hidden_part).transpose(1, 0, 2)
    up_local = up_cols.reshape(width, local_count, hidden_part).transpose(1, 0, 2)
    down_local = down_rows.reshape(local_count, hidden_part, width)

    def spread(buffer):
        last = buffer.shape[-1]
        wide = buffer.reshape(groups, 1, local_count * MOST, last)
        wide = jnp.broadcast_to(wide, (groups, replicas, local_count * MOST, last))
        return exchange(wide.reshape(ep_count, local_count * MOST, last), "ep")

    def collect(buffer):
        last = buffer.shape[-1]
        return jnp.sum(
            exchange(buffer, "ep").astype(WIDE).reshape(groups, replicas, local_count * MOST, last),
            1,
        ).reshape(EXPERTS * MOST, last)

    def owner_layout(received):
        last = received.shape[-1]
        return (
            received.reshape(ep_count, local_count, MOST, last)
            .transpose(1, 0, 2, 3)
            .reshape(local_count, ep_count * MOST, last)
        )

    def source_layout(owned):
        last = owned.shape[-1]
        return (
            owned.reshape(local_count, ep_count, MOST, last)
            .transpose(1, 0, 2, 3)
            .reshape(ep_count, local_count * MOST, last)
        )

    def batched(spec, left_op, right_op):
        return jnp.einsum(spec, left_op, right_op, preferred_element_type=WIDE)

    own_rows = owner_layout(spread(rows_sent))
    got_grads = owner_layout(spread(grads_sent))
    got_other = owner_layout(spread(other[:, None]))
    first = lax.axis_index("ep") // replicas * local_count
    mine = first + jnp.arange(local_count)[:, None, None]
    lane = jnp.arange(EXPERTS)
    logits = batched("lrd,ed->lre", own_rows, router_t)
    hit_mine, hit_other = ((lane == mine).astype(WIDE), (lane == got_other).astype(WIDE))
    got_weight = jax.nn.sigmoid(jnp.sum(logits * (hit_mine - hit_other), -1, keepdims=True))
    gate_val = batched("lrd,ldh->lrh", own_rows, gate_local)
    up_val = batched("lrd,ldh->lrh", own_rows, up_local)
    silu_val, slope_val = silu_grad(gate_val)
    hidden_val = (silu_val * up_val).astype(LOW)
    out_rows = batched("lrh,lhd->lrd", hidden_val, down_local)
    back_out = collect(source_layout((got_weight * out_rows).astype(LOW)))
    grad_hidden = batched("lrd,lhd->lrh", got_grads, down_local)
    row_dot = jnp.sum(hidden_val.astype(WIDE) * grad_hidden, -1, keepdims=True)
    amount = got_weight * (1.0 - got_weight) * row_dot
    d_logits = (amount * (hit_mine - hit_other)).astype(LOW)
    part = jnp.sum(batched("lre,lrd->led", d_logits, own_rows), 0)
    scaled = got_weight * grad_hidden
    own_grads = (got_weight * got_grads.astype(WIDE)).astype(LOW)
    grad_gate = (scaled * up_val * slope_val).astype(LOW)
    grad_up = (scaled * silu_val).astype(LOW)
    din_rows = batched("lrh,ldh->lrd", grad_gate, gate_local)
    din_rows = din_rows + batched("lrh,ldh->lrd", grad_up, up_local)
    din_rows = din_rows + batched("lre,ed->lrd", d_logits, router_t)
    back_din = collect(source_layout(din_rows.astype(LOW)))
    grad_gate_w = batched("lrd,lrh->ldh", own_rows, grad_gate)
    grad_up_w = batched("lrd,lrh->ldh", own_rows, grad_up)
    grad_down_w = batched("lrh,lrd->lhd", hidden_val, own_grads)

    def share(full, axis):
        return lax.psum_scatter(
            full.astype(LOW), SEQ, scatter_dimension=axis, tiled=True
        ).astype(WIDE)

    return (
        back_out.astype(LOW),
        back_din.astype(LOW),
        jnp.pad(part, ((0, EXTRA - EXPERTS), (0, 0))),
        lambda start: (
            share(grad_gate_w.transpose(1, 0, 2).reshape(width, local_count * hidden_part), 1),
            share(grad_up_w.transpose(1, 0, 2).reshape(width, local_count * hidden_part), 1),
            share(grad_down_w.reshape(local_count * hidden_part, width), 0),
        ),
    )


def shards(
    tokens,
    cotangent,
    routes,
    priority,
    gain_attn,
    w_query,
    w_key,
    w_value,
    w_out,
    gain_ffn,
    w_shared_gate,
    w_shared_up,
    w_shared_down,
    w_router,
    w_expert_gate,
    w_expert_up,
    w_expert_down,
):
    tok_rows, width = tokens.shape
    rows_w = w_query.shape[0]
    fs_count = lax.axis_size("fx") * lax.axis_size("fc")
    ep_count = lax.axis_size("ep")
    devices = ep_count * fs_count
    seq_len = tok_rows * fs_count
    head_size = width // HEADS
    side, core = (lax.axis_index("fx"), lax.axis_index("fc"))
    fs_index = side * lax.axis_size("fc") + core
    my_rank = lax.axis_index("ep") * fs_count + fs_index
    my_expert = lax.axis_index("ep") * lax.axis_size("fx") + side
    ids = [core] + [fs_index ^ k for k in range(4)] + [my_expert, lax.axis_index("ep"), side]
    ids = jnp.stack(ids).astype(jnp.int32)

    small_own = jnp.concatenate([w_router.T, gain_attn[None], gain_ffn[None]], 0)
    small_own = jnp.pad(small_own, ((0, EXTRA - EXPERTS - 2), (0, width - rows_w)))
    pack = jnp.concatenate([tokens, small_own])
    pack_far = far_of(pack)
    qkv_stack = jnp.stack([w_query, w_key, w_value])
    qkv_cut = [
        lax.dynamic_slice_in_dim(qkv_stack, (fs_index ^ k) * rows_w, rows_w, 2) for k in range(4)
    ]

    def to_place(parts):
        got = [
            lax.ppermute(parts[k], SEQ, [(i, i ^ k) for i in range(fs_count)]) for k in (2, 3, 1)
        ]
        return (parts[0], got[2], got[0], got[1])

    w_parts = to_place(qkv_cut)
    x_parts = (pack, near_of(pack), pack_far, near_of(pack_far))

    lane = jnp.arange(2 * EXPERTS)
    zero_row = jnp.zeros((EXPERTS,), WIDE)
    lower = (jnp.arange(tok_rows)[:, None] > jnp.arange(tok_rows)[None, :]).astype(LOW)
    slot_iota = jnp.arange(EXPERTS * MOST)
    half_iota = jnp.arange(EXPERTS * MOST // 2)

    def plan(block_routes, block_priority):
        classes = jnp.stack([block_priority, 1 - block_priority], 1)
        named = block_routes + EXPERTS * classes
        hits = [(named[:, j : j + 1] == lane).astype(WIDE) for j in (0, 1)]
        both = hits[0] + hits[1]
        before = matmul(lower, both.astype(LOW))
        counts = jnp.sum(both, 0)
        local_table = before + jnp.concatenate([zero_row, counts[:EXPERTS]])
        ranks = [jnp.sum(local_table * hits[j], -1).astype(jnp.int32) for j in (0, 1)]
        return (hits, before, counts, ranks)

    def keep_of(block_plan, base):
        hits, before = block_plan[:2]
        capacity = 5 * tok_rows * devices // 32
        return [(jnp.sum((before + base) * hits[j], -1) < capacity).astype(LOW) for j in (0, 1)]

    def base_of(all_counts, rank):
        earlier = (jnp.arange(devices) < rank).astype(WIDE)
        base = jnp.sum(all_counts * earlier[:, None], 0)
        return base + jnp.concatenate([zero_row, jnp.sum(all_counts[:, :EXPERTS], 0)])

    own_plan = plan(routes, priority)
    counts, ranks = own_plan[2:]
    slot_hit = [
        ((routes[:, j] * MOST + ranks[j])[:, None] == slot_iota).astype(LOW) for j in (0, 1)
    ]
    dispatch = slot_hit[0] + slot_hit[1]
    others = jnp.stack([routes[:, 1], routes[:, 0]]).astype(LOW)
    other_sent = matmul(others[0:1], slot_hit[0]) + matmul(others[1:2], slot_hit[1])
    other_sent = other_sent.reshape(EXPERTS, MOST)
    pair_of_cores = EXPERTS == ep_count * lax.axis_size("fx")
    if pair_of_cores:
        tiny = jnp.concatenate(
            [jnp.broadcast_to(counts[None], (EXPERTS, 2 * EXPERTS)), other_sent], 1
        )
        tiny = jnp.pad(tiny, ((0, 0), (0, 128 - tiny.shape[1]))).astype(jnp.int32)
        tiny = after(tiny, x_parts[1], w_parts[1])
        tiny = jnp.broadcast_to(tiny[:, None], (EXPERTS, 2, 128)).reshape(devices, 1, 128)
        tiny_got = exchange(tiny, ALL)
        all_counts = tiny_got[:, 0, : 2 * EXPERTS].astype(WIDE)
        other = lax.dynamic_index_in_dim(tiny_got.reshape(EXPERTS, 2, 128), core, 1, keepdims=False)
        other = other[:, 2 * EXPERTS : 2 * EXPERTS + MOST].reshape(EXPERTS * MOST, 1)
        facts_far = far_of(jnp.concatenate([routes.T, priority[None]]))
        far_routes = facts_far[:2].T
        far_plan = plan(far_routes, facts_far[2])
        far_keep = keep_of(far_plan, base_of(all_counts, my_rank ^ 2))
        own_keep = keep_of(own_plan, base_of(all_counts, my_rank))

        def side_hit(block_routes, block_ranks, j):
            place = (block_routes[:, j] >> 1) * MOST + block_ranks[j]
            same = (block_routes[:, j] & 1) == side
            return ((place[:, None] == half_iota) & same[:, None]).astype(LOW)

        own_side = [side_hit(routes, ranks, j) for j in (0, 1)]
        far_side = [side_hit(far_routes, far_plan[3], j) for j in (0, 1)]
        side_hits = (own_side[0] + own_side[1], far_side[0] + far_side[1])
        side_kept = (
            own_side[0] * own_keep[0][:, None] + own_side[1] * own_keep[1][:, None],
            far_side[0] * far_keep[0][:, None] + far_side[1] * far_keep[1][:, None],
        )
    else:
        spread_counts = jnp.broadcast_to(counts.astype(jnp.int32), (devices, 2 * EXPERTS))
        all_counts = exchange(spread_counts, ALL).astype(WIDE)
        kept = keep_of(own_plan, base_of(all_counts, my_rank))
        dispatch_kept = slot_hit[0] * kept[0][:, None] + slot_hit[1] * kept[1][:, None]

    forward_table, cos_table, sin_table = rope_constants(seq_len, head_size // 2)
    weights = (w_expert_gate, w_expert_up, w_expert_down)
    up_stack = jnp.stack([w_shared_gate, w_shared_up])
    ff_part = w_shared_gate.shape[1] // fs_count
    up_own = lax.dynamic_slice_in_dim(up_stack, side * 2 * ff_part, 2 * ff_part, 2)
    up_give = lax.dynamic_slice_in_dim(up_stack, (1 - side) * 2 * ff_part, 2 * ff_part, 2)

    def core_cut(piece, which):
        return lax.dynamic_slice_in_dim(piece, which * ff_part, ff_part, 2)

    up_mine, up_other = (core_cut(up_own, core), core_cut(up_own, 1 - core))
    ready = (*x_parts[1:], *w_parts[1:])
    out_far, dy_far = (far_of(piece) for piece in tie((w_out, cotangent), *ready))
    out_near, dy_near = (near_of(piece) for piece in tie((w_out, cotangent), *ready))
    up_near = near_of(after(up_other, *ready))
    peers = []
    if pair_of_cores:
        peers = [near_of(piece) for piece in tie(weights, tiny_got)]
    ain, own_mats, (queries, keys, values), lse, att_own, small = attention_forward(
        ids, x_parts, w_parts, jnp.asarray(forward_table)
    )
    if pair_of_cores:
        dy_sent = send_pair(ids, side_hits, (cotangent, after(dy_far, att_own[0])))
        got_dy = exchange(dy_sent, "ep").reshape(-1, width)
    out_parts = (w_out, out_near, out_far, near_of(after(out_far, att_own[0])))
    att_parts = tie(to_place(att_own), *out_parts[1:])
    residual, ffn_input = after_attention(att_parts, out_parts, tokens, small)
    ffn_far = far_of(ffn_input)
    dy_parts = (cotangent, dy_near, dy_far, near_of(after(dy_far, ffn_far)))
    ffn_parts = (ffn_input, near_of(ffn_input), ffn_far, near_of(ffn_far))
    up_far = far_of(after(up_give, ffn_far))

    def shared():
        up_last = near_of(core_cut(up_far, 1 - core))
        up_parts = (up_mine, up_near, core_cut(up_far, core), up_last)
        return shared_branch(
            ids,
            ffn_parts,
            dy_parts,
            up_parts,
            w_shared_down,
            ep_count if pair_of_cores else 0,
        )

    def fold(parts):
        mine, give, mid = parts
        got = near_of(give)
        return (mine, got, far_of((mid.astype(WIDE) + got[1].astype(WIDE)).astype(LOW)))

    def ep_step(block, bit):
        return lax.ppermute(block, "ep", [(i, i ^ bit) for i in range(ep_count)])

    def added(first, second):
        return (first.astype(WIDE) + second.astype(WIDE)).astype(LOW)

    if pair_of_cores:
        got_dy = after(got_dy, *peers)
        rows_sent = send_pair(ids, tie(side_kept, got_dy), (ffn_input, ffn_far))
        din_sums, out_sums, (grads_keep, grads_give) = shared()
        grads_got = ep_step(grads_give, 1)
        din_sent, router_part, homeward, middle, outward, give_grads, last = experts_chip(
            ids, rows_sent, got_dy, other, small, weights, peers, (grads_keep,)
        )
        din_fold = fold(din_sums)
        half = added(grads_keep, after(grads_got, din_sent))
        back_din = homeward(after(din_sent, half))
        half_got = ep_step(half[1::2], 2)
        expert_out_rows = middle(half)
        back_din = after(back_din, half_got)
        quarter = added(half[0::2], half_got)
        quarter_got = ep_step(quarter[1:2], 4)
    else:
        dy_sent = contract_rows(dispatch, cotangent).astype(LOW)
        rows_sent = contract_rows(dispatch_kept, ffn_input).astype(LOW)
        back_out, back_din, router_part, expert_grads = experts_spread(
            rows_sent, dy_sent, other_sent.reshape(-1), small[:EXPERTS], weights
        )
        din_sums, out_sums, grads_rest = shared()
        din_fold = fold(din_sums)

    grad_resid, branch = back_at_tokens(
        din_fold, back_din, dispatch, residual, small, cotangent, router_part
    )
    branch_far = far_of(branch)
    branch_pair = (branch, branch_far)
    if pair_of_cores:
        own_chunk = added(quarter[0:1], after(quarter_got, branch))
        branch_pair = tie(branch_pair, own_chunk)
        back_out = outward(after(expert_out_rows, own_chunk, branch_far))
    branch_near, branch_last = (near_of(piece) for piece in branch_pair)
    branch_parts = (branch, branch_near, branch_far, branch_last)
    d_qkv, grads_qkv = attention_backward(
        ids, branch_parts, w_out, queries, keys, values, lse, ain, (cos_table, sin_table), ep_count if pair_of_cores else 1
    )
    strip = rows_w // ep_count
    grads_qkv = after(grads_qkv, back_out)
    if pair_of_cores:
        qkv_blocks = grads_qkv
    else:
        qkv_blocks = grads_qkv.transpose(1, 0, 2, 3).reshape(3, fs_count, ep_count, strip, rows_w)
        qkv_blocks = qkv_blocks.transpose(2, 1, 0, 3, 4).reshape(devices, 3, strip, rows_w)
    qkv_got = exchange(qkv_blocks, ALL)
    din_parts, grad_out_w = late_grads(ids, d_qkv, own_mats, att_own, branch_parts)
    in_fold = fold(din_parts)
    own_float = tokens.astype(WIDE)
    grad_in = in_fold[0].astype(WIDE) + in_fold[1][0].astype(WIDE) + in_fold[2].astype(WIDE)
    gain_one = small[EXPERTS : EXPERTS + 1].astype(WIDE)
    grad_tokens = grad_resid + rms_backward(grad_in, own_float, inverse_rms(own_float), gain_one)

    if pair_of_cores:
        out_near_sum = near_of(after(out_sums[1], qkv_blocks))
        own_total, far_total = take_pair(
            ids, side_hits, back_out, out_sums, out_near_sum, residual
        )
        output = (own_total + far_of(far_total).astype(WIDE)).astype(LOW)
    else:
        out_fold = fold(out_sums)
        total = residual + out_fold[0].astype(WIDE) + out_fold[1][0].astype(WIDE)
        total = total + out_fold[2].astype(WIDE) + matmul(dispatch, back_out)
        output = total.astype(LOW)
    qkv_got = qkv_got.reshape(ep_count, fs_count, 3, strip, rows_w).astype(WIDE)
    qkv_sum = jnp.sum(qkv_got, 0).transpose(1, 2, 0, 3).reshape(3 * strip, width).astype(LOW)
    small_part = lax.dynamic_slice_in_dim(grad_out_w[rows_w:], fs_index * rows_w, rows_w, 1)
    if pair_of_cores:
        lines = EXTRA * rows_w // (ep_count * width)
        parts = jnp.concatenate(
            [
                grad_out_w[:rows_w].reshape(ep_count, strip, width),
                small_part.reshape(ep_count, lines, width),
            ],
            1,
        )
        cut = 2 * rows_w // ep_count
        turned = to_place([own_chunk[0, k * cut : (k + 1) * cut] for k in range(4)])
        whole = jnp.concatenate([*turned, own_chunk[0, 4 * cut :]])[None]
        for bit, far_bit in ((1, 4), (2, 2)):
            keep, give = split_part(parts, bit)
            got, whole_got = (ep_step(give, bit), ep_step(whole, far_bit))
            got, whole_got = lax.optimization_barrier((got, whole_got))
            parts = added(keep, got)
            whole = jnp.concatenate([whole, whole_got])
        keep, give = split_part(parts, 4)
        whole_got = ep_step(whole, 1)
        out_sum = added(keep, ep_step(give, 4))[0]
    else:
        lines = 0
        out_whole = lax.psum((grad_out_w[:rows_w], small_part), "ep")
        out_sum = jnp.zeros((0, width), LOW)
    sums = jnp.concatenate([qkv_sum, out_sum])
    sums = exchange(jnp.broadcast_to(sums[None], (ep_count,) + sums.shape), "ep")
    mats = (w_query, w_key, w_value)
    if pair_of_cores:
        *qkv_all, sum_out_w, gain_col = place_dense(sums, mats, gain_attn[:, None], strip)
        sum_gain_one = gain_col[:, 0]
        sum_small = sums[:, 4 * strip : 4 * strip + lines].astype(WIDE).reshape(EXTRA, rows_w)
    else:
        sums = sums.astype(WIDE)
        qkv_all = sums.reshape(ep_count, 3, strip, width)
        qkv_all = qkv_all.transpose(1, 0, 2, 3).reshape(3, rows_w, width)
        sum_out_w, sum_small = (piece.astype(WIDE) for piece in out_whole)
        sum_gain_one = sum(
            jnp.sum(qkv_all[i] * mat.astype(WIDE), -1) for i, mat in enumerate(mats)
        )
        sum_gain_one = sum_gain_one / gain_attn.astype(WIDE)
    sum_router, sum_gain_two = (sum_small[:EXPERTS].T, sum_small[EXPERTS])
    if pair_of_cores:
        received = give_grads(qkv_blocks)
        expert_grads = last(qkv_blocks, received)
        whole = [whole, after(whole_got, expert_grads[0])]
        sum_sgate, sum_sup, sum_sdown = place_shared(ids, whole, rows_w, width)
    else:
        expert_grads = expert_grads(grads_qkv)
        dense = lax.psum((*to_place(grads_rest[:4]), grads_rest[4]), "ep")
        sum_sdown = dense[4].astype(WIDE)
        wide_rel = jnp.stack([piece.astype(WIDE) for piece in dense[:4]])
        wide_all = jnp.concatenate(
            [
                lax.dynamic_index_in_dim(wide_rel, fs_index ^ k, 0, keepdims=False)
                for k in range(4)
            ],
            2,
        )
        sum_sgate, sum_sup = (wide_all[0], wide_all[1])
    return (
        output,
        grad_tokens,
        sum_gain_one,
        qkv_all[0],
        qkv_all[1],
        qkv_all[2],
        sum_out_w,
        sum_gain_two,
        sum_sgate,
        sum_sup,
        sum_sdown,
        sum_router,
        *expert_grads,
    )


def solution(mesh):
    ep_count, fs_count = mesh.devices.shape
    cut_mesh = Mesh(mesh.devices.reshape(ep_count, fs_count // 2, 2), ALL)
    tok = P(ALL, None)
    row = P(SEQ, None)
    return jax.shard_map(
        shards,
        mesh=cut_mesh,
        in_specs=(
            tok,
            tok,
            tok,
            P(ALL),
            P(SEQ),
            row,
            row,
            row,
            row,
            P(SEQ),
            row,
            row,
            row,
            row,
            P(None, ALL),
            P(None, ALL),
            tok,
        ),
        out_specs=(
            tok,
            tok,
            P(SEQ),
            row,
            row,
            row,
            row,
            P(SEQ),
            row,
            row,
            row,
            row,
            P(None, ALL),
            P(None, ALL),
            tok,
        ),
        check_vma=False,
    )
```

```python
import jax
import jax.numpy as jnp
import numpy as np
from jax import lax
from jax.experimental import pallas as pl
from jax.experimental.pallas import tpu as pltpu
from jax.sharding import Mesh
from jax.sharding import PartitionSpec as P

HEADS = 12
EXPERTS = 16
MOST = 48
EXTRA = 2 * EXPERTS
LIGHT = 20

EPS = 1e-06
NEG = -1e30
LOW = jnp.bfloat16
WIDE = jnp.float32
ALL = ("ep", "fx", "fc")
SEQ = ("fx", "fc")
SWAP = [(0, 1), (1, 0)]
VMEM = pl.BlockSpec(memory_space=pltpu.VMEM)
SMEM = pl.BlockSpec(memory_space=pltpu.SMEM)


def matmul(left_op, right_op):
    return jnp.dot(left_op, right_op, preferred_element_type=WIDE)


def contract_rows(left_op, right_op):
    return lax.dot_general(left_op, right_op, (((0,), (0,)), ((), ())), preferred_element_type=WIDE)


def contract_cols(left_op, right_op):
    return lax.dot_general(left_op, right_op, (((1,), (1,)), ((), ())), preferred_element_type=WIDE)


def inverse_rms(values):
    return lax.rsqrt(jnp.mean(values * values, -1, keepdims=True) + EPS)


def rms_backward(upstream, values, inverse, gain_vec):
    scaled = upstream * gain_vec
    return inverse * scaled - values * inverse**3 * jnp.mean(scaled * values, -1, keepdims=True)


def silu_grad(gate_val):
    sigma = jax.nn.sigmoid(gate_val)
    return (gate_val * sigma, sigma * (1.0 + gate_val * (1.0 - sigma)))


def far_of(block):
    return lax.ppermute(block, "fx", SWAP)


def near_of(block):
    return lax.ppermute(block, "fc", SWAP)


def after(value, *others):
    return lax.optimization_barrier((value, *others))[0]


def tie(values, *others):
    return lax.optimization_barrier((*values, *others))[: len(values)]


def exchange(blocks, axes):
    return lax.all_to_all(blocks, axes, split_axis=0, concat_axis=0, tiled=True)


def split_part(parts, bit):
    cut = parts.reshape((parts.shape[0] // 2, 2) + parts.shape[1:])
    mine = lax.rem(lax.axis_index("ep") // bit, 2)
    keep = lax.dynamic_index_in_dim(cut, mine, 1, keepdims=False)
    return (keep, lax.dynamic_index_in_dim(cut, 1 - mine, 1, keepdims=False))


def shape_of(dims, kind):
    return jax.ShapeDtypeStruct(dims, kind)


def run_kernel(body, outs, args, specs=None, out_specs=None, scratch=(), grid=None, flops=0, move=0):
    options = {} if grid is None else {"grid": grid}
    return pl.pallas_call(
        body,
        out_shape=outs,
        in_specs=specs if specs is not None else [VMEM] * len(args),
        out_specs=out_specs if out_specs is not None else [VMEM] * len(outs),
        scratch_shapes=list(scratch),
        compiler_params=pltpu.CompilerParams(vmem_limit_bytes=52 * 2**20),
        cost_estimate=pl.CostEstimate(
            flops=flops // LIGHT, bytes_accessed=move // LIGHT, transcendentals=0
        ),
        **options,
    )(*args)


def pick_rows(first_iota, second_iota, source):
    return (first_iota == source(second_iota)).astype(LOW)


def rope_constants(length, half):
    freq = np.exp(-np.log(np.float32(10000.0)) * np.arange(half, dtype=np.float32) / np.float32(half))
    angle = np.arange(length, dtype=np.float32)[:, None] * freq.astype(np.float32)[None, :]
    cosine, sine = (np.cos(angle), np.sin(angle))
    return (
        np.concatenate([cosine, cosine, sine, sine], 1).astype(np.float32),
        np.concatenate([cosine] * 4, 1).astype(np.float32),
        np.concatenate([sine, -sine, sine, -sine], 1).astype(np.float32),
    )


def attention_forward(ids, x_parts, w_parts, table):
    full, width = x_parts[0].shape
    rows = full - EXTRA
    block = w_parts[0].shape[1]
    length = 4 * rows
    heads = block // 64
    size = heads * 128

    def body(ids_ref, *refs):
        x_refs, w_refs, table_ref = (refs[:4], refs[4:8], refs[8])
        ain_ref, own_ref, q_ref, k_ref, v_ref, lse_ref = refs[9:15]
        att_refs, small_ref = (refs[15:19], refs[19])
        att_scr = refs[20]
        first = lax.broadcasted_iota(jnp.int32, (block, width), 0)
        lane = lax.broadcasted_iota(jnp.int32, (block, width), 1)
        small = jnp.zeros((EXTRA, width), WIDE)
        for k in range(4):
            place = jnp.where(lane == first + ids_ref[1 + k] * block, 1.0, 0.0).astype(LOW)
            small = small + matmul(x_refs[k][rows:, :block], place)
        small_ref[...] = small.astype(LOW)
        gain = small[EXPERTS : EXPERTS + 1, :]
        for k in range(4):
            place = ids_ref[1 + k]
            piece = x_refs[k][:rows, :].astype(WIDE)
            ain_ref[pl.ds(place * rows, rows), :] = (piece * inverse_rms(piece) * gain).astype(LOW)
            for m in range(3):
                own_ref[m, pl.ds(place * block, block), :] = w_refs[k][m]
        first = lax.broadcasted_iota(jnp.int32, (block, size), 0)
        lane = lax.broadcasted_iota(jnp.int32, (block, size), 1)
        head, inner = (lane // 128, lane % 128)
        low = inner % 64
        swapped = jnp.where(low < 32, low + 32, low - 32)
        source = 64 * head + jnp.where(inner < 64, low, swapped)
        sign = jnp.where((inner >= 64) & (low < 32), -1.0, 1.0)
        turn = jnp.where(first == source, sign, 0.0).astype(LOW)
        keep = (inner // 64 == head % 2) & (first == 64 * head + low)
        place_v = jnp.where(keep, 1.0, 0.0).astype(LOW)
        w_q = matmul(own_ref[0], turn).astype(LOW)
        w_k = matmul(own_ref[1], turn).astype(LOW)
        w_v = matmul(own_ref[2], place_v).astype(LOW)
        half = lax.broadcasted_iota(jnp.int32, (rows, 128), 1) < 64
        for i in range(4):
            span = slice(i * rows, (i + 1) * rows)
            ain = ain_ref[span, :]
            y_q, y_k, y_v = (matmul(ain, w_q), matmul(ain, w_k), matmul(ain, w_v))
            tab = table_ref[span, :]
            for h in range(heads):
                cols = slice(128 * h, 128 * h + 128)
                turned = y_q[:, cols] * tab
                turned = (turned + pltpu.roll(turned, 64, 1)).astype(LOW).astype(WIDE)
                q_ref[h, span, :] = jnp.where(half, turned * 0.125, 0.0).astype(LOW)
                turned = y_k[:, cols] * tab
                k_ref[h, span, :] = (turned + pltpu.roll(turned, 64, 1)).astype(LOW)
                v_ref[h, span, :] = y_v[:, cols].astype(LOW)
        tri = lax.broadcasted_iota(jnp.int32, (rows, rows), 0) >= lax.broadcasted_iota(
            jnp.int32, (rows, rows), 1
        )
        for i in range(4):
            span = slice(i * rows, (i + 1) * rows)
            done = slice(0, i * rows)
            every = range(heads)
            diags = [
                jnp.where(tri, contract_cols(q_ref[h, span, :], k_ref[h, span, :]), NEG)
                for h in every
            ]
            tops = [jnp.max(diag, -1, keepdims=True) for diag in diags]
            if i:
                pasts = [contract_cols(q_ref[h, span, :], k_ref[h, done, :]) for h in every]
                tops = [
                    jnp.maximum(tops[h], jnp.max(pasts[h], -1, keepdims=True)) for h in every
                ]
                pasts = [jnp.exp(pasts[h] - tops[h]) for h in every]
            diags = [jnp.exp(diags[h] - tops[h]) for h in every]
            totals = [jnp.sum(diag, -1, keepdims=True) for diag in diags]
            if i:
                totals = [totals[h] + jnp.sum(pasts[h], -1, keepdims=True) for h in every]
            scales = [1.0 / total for total in totals]
            tiles = [
                matmul((diags[h] * scales[h]).astype(LOW), v_ref[h, span, :]) for h in every
            ]
            if i:
                tiles = [
                    tiles[h] + matmul((pasts[h] * scales[h]).astype(LOW), v_ref[h, done, :])
                    for h in every
                ]
            for h in every:
                lse_ref[h, span, :] = tops[h] + jnp.log(totals[h])
            for t in range((heads + 1) // 2):
                pair = tiles[2 * t] + (tiles[2 * t + 1] if 2 * t + 1 < heads else 0.0)
                wide = min(128, block - 128 * t)
                att_scr[span, 128 * t : 128 * t + wide] = pair[:, :wide].astype(LOW)
        for k in range(4):
            att_refs[k][...] = att_scr[pl.ds(ids_ref[1 + k] * rows, rows), :]

    outs = (
        [shape_of((length, width), LOW), shape_of((3, width, block), LOW)]
        + [shape_of((heads, length, 128), LOW)] * 3
        + [shape_of((heads, length, 1), WIDE)]
        + [shape_of((rows, block), LOW)] * 4
        + [shape_of((EXTRA, width), LOW)]
    )
    args = [ids, *x_parts, *w_parts, table]
    got = run_kernel(
        body,
        outs,
        args,
        specs=[SMEM] + [VMEM] * (len(args) - 1),
        scratch=[pltpu.VMEM((length, block), LOW)],
        flops=8 * 10**9,
        move=12 * 10**6,
    )
    return (got[0], got[1], got[2:5], got[5], got[6:10], got[10])


def after_attention(att_parts, out_parts, tokens, small):
    rows, width = tokens.shape

    def body(*refs):
        att_refs, out_refs = (refs[:4], refs[4:8])
        tok_ref, small_ref, res_ref, ffn_ref = refs[8:]
        total = tok_ref[...].astype(WIDE)
        for k in range(4):
            total = total + matmul(att_refs[k][...], out_refs[k][...])
        res_ref[...] = total
        gain = small_ref[EXPERTS + 1 : EXPERTS + 2, :].astype(WIDE)
        ffn_ref[...] = (total * inverse_rms(total) * gain).astype(LOW)

    outs = [shape_of((rows, width), WIDE), shape_of((rows, width), LOW)]
    args = [*att_parts, *out_parts, tokens, small]
    return run_kernel(body, outs, args, flops=6 * 10**8, move=4 * 10**6)


def send_pair(ids, hits, blocks):
    rows, width = blocks[0].shape
    groups = hits[0].shape[1] // MOST

    def body(ids_ref, own_hit, far_hit, own_ref, far_ref, out_ref):
        for hit, block, place in (
            (own_hit, own_ref, ids_ref[7]),
            (far_hit, far_ref, 1 - ids_ref[7]),
        ):
            sent = contract_rows(hit[...], block[...]).astype(LOW)
            for g in range(groups):
                out_ref[g, place] = sent[g * MOST : (g + 1) * MOST, :]

    return run_kernel(
        body,
        [shape_of((groups, 2, MOST, width), LOW)],
        [ids, *hits, *blocks],
        specs=[SMEM] + [VMEM] * 4,
        flops=6 * 10**8,
        move=3 * 10**6,
    )[0]


def take_pair(ids, hits, back, sums, near_sum, residual):
    groups, _, _, width = back.shape
    rows = residual.shape[0]

    def body(ids_ref, own_hit, far_hit, back_ref, mine_ref, mid_ref, near_ref, res_ref, own_out, far_out):
        own = res_ref[...] + mine_ref[...].astype(WIDE) + near_ref[0].astype(WIDE)
        far = mid_ref[...].astype(WIDE) + near_ref[1].astype(WIDE)
        for g in range(groups):
            cols = slice(g * MOST, (g + 1) * MOST)
            own = own + matmul(own_hit[:, cols], back_ref[g, ids_ref[7]])
            far = far + matmul(far_hit[:, cols], back_ref[g, 1 - ids_ref[7]])
        own_out[...] = own
        far_out[...] = far.astype(LOW)

    return run_kernel(
        body,
        [shape_of((rows, width), WIDE), shape_of((rows, width), LOW)],
        [ids, *hits, back, sums[0], sums[2], near_sum, residual],
        specs=[SMEM] + [VMEM] * 7,
        flops=6 * 10**8,
        move=5 * 10**6,
    )


def shared_branch(ids, ffn_parts, dy_parts, w_parts, down, chunks):
    rows, width = ffn_parts[0].shape
    block, hidden = w_parts[0].shape[1:]

    def body(ids_ref, *refs):
        ffn_refs, dy_refs, w_refs = (refs[:4], refs[4:8], refs[8:12])
        down_ref = refs[12]
        sum_refs, grad_refs = (refs[13:19], refs[19:-3])
        w_scr, g_scr, d_scr = refs[-3:]
        for k in range(4):
            for m in range(2):
                w_scr[m, pl.ds(ids_ref[1 + k] * block, block), :] = w_refs[k][m]
        for k in range(4):
            ffn, dy = (ffn_refs[k][...], dy_refs[k][...])
            gate, up = (matmul(ffn, w_scr[0]), matmul(ffn, w_scr[1]))
            silu, slope = silu_grad(gate)
            hid = (silu * up).astype(LOW)
            back = contract_cols(dy, down_ref[...])
            d_gate = (back * up * slope).astype(LOW)
            d_up = (back * silu).astype(LOW)
            din = (contract_cols(d_gate, w_scr[0]) + contract_cols(d_up, w_scr[1])).astype(LOW)
            out = matmul(hid, down_ref[...]).astype(LOW)
            for n, value in enumerate((din, out)):
                mine_ref, near_ref, mid_ref = sum_refs[3 * n : 3 * n + 3]
                if k % 2 == 0:
                    target = mine_ref if k == 0 else mid_ref
                    target[...] = value
                else:
                    near_ref[k // 2] = value
            parts = (contract_rows(ffn, d_gate), contract_rows(ffn, d_up), contract_rows(hid, dy))
            if k == 0:
                g_scr[0], g_scr[1], d_scr[...] = parts
            else:
                g_scr[0] += parts[0]
                g_scr[1] += parts[1]
                d_scr[...] += parts[2]
        if chunks:
            per = chunks // 2
            cut, line = (block // per, hidden // chunks)
            for r in range(chunks):
                part = ids_ref[6] ^ r
                target = grad_refs[r % 2]
                which, low = (part // per, part % per)
                for k in range(4):
                    start = ids_ref[1 + k] * block + low * cut
                    target[r // 2, k * cut : (k + 1) * cut, :] = g_scr[
                        which, pl.ds(pl.multiple_of(start, 16), cut), :
                    ].astype(LOW)
                start = pl.multiple_of(part * line, 16)
                piece = d_scr[pl.ds(start, line), :].astype(LOW)
                base = 4 * cut
                target[r // 2, base : base + line, :] = piece[:, :hidden]
                target[r // 2, base + line :, : hidden // 2] = piece[: line // 2, hidden:]
                target[r // 2, base + line :, hidden // 2 :] = piece[line // 2 :, hidden:]
        else:
            for k in range(4):
                for m in range(2):
                    grad_refs[k][m] = g_scr[m, pl.ds(ids_ref[1 + k] * block, block), :].astype(LOW)
            grad_refs[4][...] = d_scr[...].astype(LOW)

    if chunks:
        lines = 4 * block * 2 // chunks + 3 * hidden // chunks // 2
        grad_outs = [shape_of((chunks // 2, lines, hidden), LOW)] * 2
    else:
        grad_outs = [shape_of((2, block, hidden), LOW)] * 4 + [shape_of((hidden, width), LOW)]
    sums = [shape_of((rows, width), LOW), shape_of((2, rows, width), LOW), shape_of((rows, width), LOW)]
    outs = sums * 2 + grad_outs
    args = [ids, *ffn_parts, *dy_parts, *w_parts, down]
    got = run_kernel(
        body,
        outs,
        args,
        specs=[SMEM] + [VMEM] * (len(args) - 1),
        scratch=[
            pltpu.VMEM((2, width, hidden), LOW),
            pltpu.VMEM((2, width, hidden), WIDE),
            pltpu.VMEM((hidden, width), WIDE),
        ],
        flops=7 * 10**9,
        move=14 * 10**6,
    )
    return (got[0:3], got[3:6], got[6:])


def place_shared(ids, groups, block, width):
    per_group, lines, hidden = groups[0].shape
    chunks = per_group * len(groups)
    per = chunks // 2
    cut, line = (block // per, hidden // chunks)
    order = (0, 4, 2, 6, 1, 5, 3, 7)

    def body(ids_ref, *refs):
        gate_ref, up_ref, down_ref = refs[-3:]
        for n in range(chunks):
            part = ids_ref[6] ^ order[n]
            which, low = (part // per, part % per)
            piece = refs[n // per_group][n % per_group].astype(WIDE)
            for k in range(4):
                lane = pl.multiple_of(ids_ref[1 + k] * hidden, 128)
                value = piece[k * cut : (k + 1) * cut, :]
                place = (pl.ds(pl.multiple_of(low * cut, 16), cut), pl.ds(lane, hidden))

                @pl.when(which == 0)
                def to_gate(place=place, value=value):
                    gate_ref[place] = value

                @pl.when(which == 1)
                def to_up(place=place, value=value):
                    up_ref[place] = value

            base = 4 * cut
            start = pl.multiple_of(part * line, 16)
            down_ref[pl.ds(start, line), :hidden] = piece[base : base + line, :]
            tail = piece[base + line :, :]
            down_ref[pl.ds(start, line // 2), hidden:] = tail[:, : hidden // 2]
            down_ref[pl.ds(start + line // 2, line // 2), hidden:] = tail[:, hidden // 2 :]

    return run_kernel(
        body,
        [shape_of((block, 4 * hidden), WIDE)] * 2 + [shape_of((hidden, width), WIDE)],
        [ids, *groups],
        specs=[SMEM] + [VMEM] * len(groups),
        move=8 * 10**6,
    )


def place_dense(sums, w_parts, gain, strip):
    parts, lines, width = sums.shape
    block = parts * strip

    def body(sums_ref, a_ref, b_ref, c_ref, gain_ref, *outs):
        gain_sum = jnp.zeros((block, 1), WIDE)
        for m, w_ref in enumerate((a_ref, b_ref, c_ref)):
            for p in range(parts):
                outs[m][p * strip : (p + 1) * strip, :] = sums_ref[
                    p, m * strip : (m + 1) * strip, :
                ].astype(WIDE)
            gain_sum = gain_sum + jnp.sum(outs[m][...] * w_ref[...].astype(WIDE), -1, keepdims=True)
        for p in range(parts):
            outs[3][p * strip : (p + 1) * strip, :] = sums_ref[
                p, 3 * strip : 4 * strip, :
            ].astype(WIDE)
        outs[4][...] = gain_sum / gain_ref[...].astype(WIDE)

    return run_kernel(
        body,
        [shape_of((block, width), WIDE)] * 4 + [shape_of((block, 1), WIDE)],
        [sums, *w_parts, gain],
        move=5 * 10**6,
    )


def expert_main(ids, rows_in, dy_in, mats, other, router_t):
    count, width = rows_in.shape
    own_hidden = mats[0].shape[1]
    tile = 512
    steps = 2 * own_hidden // tile
    half = steps // 2
    chunk = 256

    def body(ids_ref, rows_ref, dy_ref, *refs):
        own, peer = (refs[0:3], refs[3:6])
        other_ref, router_ref = refs[6:8]
        din_ref, hid_ref, dg_ref, du_ref, dyw_ref, w_ref, part_ref = refs[8:15]
        acc, dot_scr = refs[15:17]
        step = pl.program_id(0)
        expert = ids_ref[5]

        @pl.when(step == 0)
        def start():
            for r in range(0, count, chunk):
                span = slice(r, r + chunk)
                logits = contract_cols(rows_ref[span, :], router_ref[...])
                lane = lax.broadcasted_iota(jnp.int32, logits.shape, 1)
                mine = jnp.sum(jnp.where(lane == expert, logits, 0.0), -1, keepdims=True)
                rest = jnp.sum(jnp.where(lane == other_ref[span, :], logits, 0.0), -1, keepdims=True)
                weight = jax.nn.sigmoid(mine - rest)
                w_ref[span, :] = weight
                dyw_ref[span, :] = (weight * dy_ref[span, :].astype(WIDE)).astype(LOW)
                dot_scr[span, :] = jnp.zeros((chunk, 1), WIDE)
                acc[span, :] = jnp.zeros((chunk, width), WIDE)

        def work(gate_ref, up_ref, down_ref):
            for r in range(0, count, chunk):
                span = slice(r, r + chunk)
                rows = rows_ref[span, :]
                gate, up = (matmul(rows, gate_ref[...]), matmul(rows, up_ref[...]))
                back = contract_cols(dy_ref[span, :], down_ref[...])
                silu, slope = silu_grad(gate)
                hid = (silu * up).astype(LOW)
                hid_ref[span, :] = hid
                dot_scr[span, :] += jnp.sum(hid.astype(WIDE) * back, -1, keepdims=True)
                scaled = w_ref[span, :] * back
                d_gate = (scaled * up * slope).astype(LOW)
                d_up = (scaled * silu).astype(LOW)
                dg_ref[span, :] = d_gate
                du_ref[span, :] = d_up
                acc[span, :] += contract_cols(d_gate, gate_ref[...]) + contract_cols(
                    d_up, up_ref[...]
                )

        @pl.when(step < half)
        def first():
            work(*own)

        @pl.when(step >= half)
        def second():
            work(*peer)

        @pl.when(step == steps - 1)
        def finish():
            for r in range(0, count, chunk):
                span = slice(r, r + chunk)
                weight = w_ref[span, :]
                amount = weight * (1.0 - weight) * dot_scr[span, :]
                lane = lax.broadcasted_iota(jnp.int32, (chunk, EXTRA), 1)
                signs = jnp.where(lane == expert, 1.0, 0.0) - jnp.where(
                    lane == other_ref[span, :], 1.0, 0.0
                )
                d_logit = (amount * signs).astype(LOW)
                din_ref[span, :] = (acc[span, :] + matmul(d_logit, router_ref[...])).astype(LOW)
                part = contract_rows(d_logit, rows_ref[span, :])
                part_ref[...] = part if r == 0 else part_ref[...] + part

    def fixed(dims):
        return pl.BlockSpec(dims, lambda j: (0,) * len(dims))

    def near(j):
        return jnp.minimum(j, half - 1)

    def late(j):
        return jnp.maximum(j - half, 0)

    cols = (width, tile)
    specs = [SMEM, fixed((count, width)), fixed((count, width))]
    for place in (near, late):
        specs += [
            pl.BlockSpec(cols, lambda j, place=place: (0, place(j))),
            pl.BlockSpec(cols, lambda j, place=place: (0, place(j))),
            pl.BlockSpec((tile, width), lambda j, place=place: (place(j), 0)),
        ]
    specs += [fixed((count, 1)), fixed(router_t.shape)]
    tiles = pl.BlockSpec((count, tile), lambda j: (0, j))
    outs = (
        [shape_of((count, width), LOW)]
        + [shape_of((count, 2 * own_hidden), LOW)] * 3
        + [shape_of((count, width), LOW), shape_of((count, 1), WIDE), shape_of(router_t.shape, WIDE)]
    )
    out_specs = [
        fixed((count, width)),
        tiles,
        tiles,
        tiles,
        fixed((count, width)),
        fixed((count, 1)),
        fixed(router_t.shape),
    ]
    return run_kernel(
        body,
        outs,
        [ids, rows_in, dy_in, *mats, other, router_t],
        specs=specs,
        out_specs=out_specs,
        scratch=[pltpu.VMEM((count, width), WIDE), pltpu.VMEM((count, 1), WIDE)],
        grid=(steps,),
        flops=12 * 10**9,
        move=22 * 10**6,
    )


def expert_out(hid, weight, down_own, down_peer):
    count, hidden = hid.shape
    width = down_own.shape[1]
    half = hidden // 2
    chunk = 256

    def body(hid_ref, w_ref, own_ref, peer_ref, out_ref):
        for r in range(0, count, chunk):
            span = slice(r, r + chunk)
            total = matmul(hid_ref[span, :half], own_ref[...])
            total = total + matmul(hid_ref[span, half:], peer_ref[...])
            out_ref[span, :] = (w_ref[span, :] * total).astype(LOW)

    return run_kernel(
        body,
        [shape_of((count, width), LOW)],
        [hid, weight, down_own, down_peer],
        flops=2 * 10**9,
        move=8 * 10**6,
    )[0]


def expert_weight_grads(rows_in, dyw, hid, d_gate, d_up, peer, add=None):
    count, width = rows_in.shape
    half = hid.shape[1] // 2
    tile = 512
    steps = half // tile
    offset = steps if peer else 0
    kind = LOW if add is None else WIDE

    def body(rows_ref, dyw_ref, hid_ref, dg_ref, du_ref, *refs):
        outs = refs[-3:]
        grads = (
            contract_rows(rows_ref[...], dg_ref[...]),
            contract_rows(rows_ref[...], du_ref[...]),
            contract_rows(hid_ref[...], dyw_ref[...]),
        )
        for i in range(3):
            value = grads[i] if add is None else grads[i] + refs[i][...].astype(WIDE)
            outs[i][...] = value.astype(kind)

    def fixed(dims):
        return pl.BlockSpec(dims, lambda j: (0,) * len(dims))

    tiles = pl.BlockSpec((count, tile), lambda j: (0, j + offset))
    cols = pl.BlockSpec((width, tile), lambda j: (0, j))
    lines = pl.BlockSpec((tile, width), lambda j: (j, 0))
    specs = [fixed((count, width)), fixed((count, width)), tiles, tiles, tiles]
    extra = [] if add is None else list(add)
    return run_kernel(
        body,
        [shape_of((width, half), kind), shape_of((width, half), kind), shape_of((half, width), kind)],
        [rows_in, dyw, hid, d_gate, d_up, *extra],
        specs=specs + ([] if add is None else [cols, cols, lines]),
        out_specs=[cols, cols, lines],
        grid=(steps,),
        flops=37 * 10**8,
        move=14 * 10**6,
    )


def back_at_tokens(fold, back_din, dispatch, residual, small, cotangent, router_part):
    rows, width = residual.shape

    def body(one_ref, two_ref, last_ref, back_ref, disp_ref, res_ref, small_ref, dy_ref, part_ref, dres_ref, br_ref):
        d_ffn = one_ref[...].astype(WIDE) + two_ref[0].astype(WIDE) + last_ref[...].astype(WIDE)
        d_ffn = d_ffn + matmul(disp_ref[...], back_ref[...])
        residual_val = res_ref[...]
        inverse = inverse_rms(residual_val)
        gain = small_ref[EXPERTS + 1 : EXPERTS + 2, :].astype(WIDE)
        d_res = dy_ref[...].astype(WIDE) + rms_backward(d_ffn, residual_val, inverse, gain)
        dres_ref[...] = d_res
        br_ref[0:rows, :] = d_res.astype(LOW)
        gain_part = jnp.sum(d_ffn * residual_val * inverse, 0, keepdims=True)
        line = lax.broadcasted_iota(jnp.int32, (EXTRA, width), 0)
        extra = jnp.where(line == EXPERTS, gain_part, part_ref[...])
        br_ref[rows:, :] = extra.astype(LOW)

    return run_kernel(
        body,
        [shape_of((rows, width), WIDE), shape_of((rows + EXTRA, width), LOW)],
        [*fold, back_din, dispatch, residual, small, cotangent, router_part],
        flops=3 * 10**8,
        move=5 * 10**6,
    )


def attention_backward(ids, branch, w_out, queries, keys, values, lse, ain, tables, groups):
    heads, length, _ = queries.shape
    rows = length // 4
    block, width = w_out.shape
    tiles = (heads + 1) // 2
    strip = block // groups

    def body(ids_ref, *refs):
        br_refs = refs[:4]
        wo_ref, q_ref, k_ref, v_ref, lse_ref, ain_ref, cc_ref, ss_ref = refs[4:12]
        d_ref, g_ref = refs[12:14]
        da_scr, dk_scr, dv_scr = refs[14:17]
        zero = jnp.zeros((rows, 128), WIDE)
        for k in range(4):
            d_att = contract_cols(br_refs[k][0:rows, :], wo_ref[...]).astype(LOW)
            place = ids_ref[1 + k] * rows
            for t in range(tiles):
                wide = min(128, block - 128 * t)
                if wide < 128:
                    da_scr[t, pl.ds(place, rows), :] = zero.astype(LOW)
                da_scr[t, pl.ds(place, rows), 0:wide] = d_att[:, 128 * t : 128 * t + wide]
        half = lax.broadcasted_iota(jnp.int32, (rows, 128), 1) < 64
        tri = lax.broadcasted_iota(jnp.int32, (rows, rows), 0) >= lax.broadcasted_iota(
            jnp.int32, (rows, rows), 1
        )

        def place_tile(m, span, h, value):
            t = h // 2
            wide = min(128, block - 128 * t)
            if h % 2 == 0:
                d_ref[m, span, 128 * t : 128 * t + wide] = value[:, :wide].astype(LOW)
            else:
                kept = d_ref[m, span, 128 * t : 128 * t + 128].astype(WIDE)
                d_ref[m, span, 128 * t : 128 * t + 128] = jnp.where(half, kept, value).astype(LOW)

        def unturn(value, span):
            return value * cc_ref[span, :] + pltpu.roll(value, 32, 1) * ss_ref[span, :]

        every = range(heads)
        for i in range(4):
            span = slice(i * rows, (i + 1) * rows)
            done = slice(0, i * rows)
            queries_i = [q_ref[h, span, :] for h in every]
            d_atts = [da_scr[h // 2, span, :] for h in every]
            levels = [lse_ref[h, span, :] for h in every]
            diags = [contract_cols(queries_i[h], k_ref[h, span, :]) for h in every]
            d_diags = [contract_cols(d_atts[h], v_ref[h, span, :]) for h in every]
            diags = [jnp.exp(jnp.where(tri, diags[h] - levels[h], NEG)) for h in every]
            inners = [jnp.sum(diags[h] * d_diags[h], -1, keepdims=True) for h in every]
            if i:
                pasts = [contract_cols(queries_i[h], k_ref[h, done, :]) for h in every]
                d_pasts = [contract_cols(d_atts[h], v_ref[h, done, :]) for h in every]
                pasts = [jnp.exp(pasts[h] - levels[h]) for h in every]
                inners = [
                    inners[h] + jnp.sum(pasts[h] * d_pasts[h], -1, keepdims=True) for h in every
                ]
            d_diags = [(diags[h] * (d_diags[h] - inners[h])).astype(LOW) for h in every]
            d_queries = [matmul(d_diags[h], k_ref[h, span, :]) for h in every]
            for h in every:
                dk_scr[h, span, :] = contract_rows(d_diags[h], queries_i[h])
                dv_scr[h, span, :] = contract_rows(diags[h].astype(LOW), d_atts[h])
            if i:
                d_pasts = [(pasts[h] * (d_pasts[h] - inners[h])).astype(LOW) for h in every]
                d_queries = [d_queries[h] + matmul(d_pasts[h], k_ref[h, done, :]) for h in every]
                for h in every:
                    dk_scr[h, done, :] += contract_rows(d_pasts[h], queries_i[h])
                    dv_scr[h, done, :] += contract_rows(pasts[h].astype(LOW), d_atts[h])
            for h in every:
                place_tile(0, span, h, unturn(d_queries[h] * 0.125, span))
        for i in range(4):
            span = slice(i * rows, (i + 1) * rows)
            for h in every:
                d_key = dk_scr[h, span, :]
                place_tile(1, span, h, unturn(d_key + pltpu.roll(d_key, 64, 1), span))
                place_tile(2, span, h, dv_scr[h, span, :])
        for m in range(3):
            grad = contract_rows(ain_ref[...], d_ref[m])
            for f in range(4):
                for e in range(groups):
                    start = f * block + e * strip
                    g_ref[4 * e + f, m] = grad[start : start + strip, :].astype(LOW)

    args = [ids, *branch, w_out, queries, keys, values, lse, ain, *tables]
    return run_kernel(
        body,
        [shape_of((3, length, block), LOW), shape_of((4 * groups, 3, strip, block), LOW)],
        args,
        specs=[SMEM] + [VMEM] * (len(args) - 1),
        scratch=[
            pltpu.VMEM((tiles, length, 128), LOW),
            pltpu.VMEM((heads, length, 128), WIDE),
            pltpu.VMEM((heads, length, 128), WIDE),
        ],
        flops=16 * 10**9,
        move=12 * 10**6,
    )


def late_grads(ids, d_qkv, own_mats, att_parts, branch):
    length, block = d_qkv.shape[1:]
    rows = length // 4
    width = own_mats.shape[1]
    extra = branch[0].shape[0] - rows

    def body(ids_ref, d_ref, w_ref, *refs):
        att_refs, br_refs = (refs[:4], refs[4:8])
        mine_ref, near_ref, mid_ref, gout_ref = refs[8:12]
        for k in range(4):
            span = pl.ds(ids_ref[1 + k] * rows, rows)
            total = contract_cols(d_ref[0, span, :], w_ref[0])
            for m in range(1, 3):
                total = total + contract_cols(d_ref[m, span, :], w_ref[m])
            if k % 2 == 0:
                target = mine_ref if k == 0 else mid_ref
                target[...] = total.astype(LOW)
            else:
                near_ref[k // 2] = total.astype(LOW)
        gout = contract_rows(att_refs[0][...], br_refs[0][0:rows, :])
        small = br_refs[0][rows:, :].astype(WIDE)
        for k in range(1, 4):
            gout = gout + contract_rows(att_refs[k][...], br_refs[k][0:rows, :])
            small = small + br_refs[k][rows:, :].astype(WIDE)
        gout_ref[0:block, :] = gout.astype(LOW)
        gout_ref[block:, :] = small.astype(LOW)

    args = [ids, d_qkv, own_mats, *att_parts, *branch]
    got = run_kernel(
        body,
        [
            shape_of((rows, width), LOW),
            shape_of((2, rows, width), LOW),
            shape_of((rows, width), LOW),
            shape_of((block + extra, width), LOW),
        ],
        args,
        specs=[SMEM] + [VMEM] * (len(args) - 1),
        flops=12 * 10**8,
        move=7 * 10**6,
    )
    return (got[:3], got[3])


def experts_chip(ids, rows_sent, got_dy, other, small, weights, peers, ready):
    width = rows_sent.shape[-1]
    axes = ("ep", "fx")
    own_rows = exchange(rows_sent, "ep").reshape(-1, width)
    own_rows = after(own_rows, *ready)
    din, hid, d_gate, d_up, dyw, weight, part = expert_main(
        ids, own_rows, got_dy, [*weights, *peers], other, small
    )

    def homeward(sent):
        return exchange(sent.reshape(EXPERTS, MOST, width), axes).reshape(-1, width)

    def middle(start):
        return expert_out(after(hid, start), weight, weights[2], peers[2])

    def give(start):
        given = expert_weight_grads(after(own_rows, start), dyw, hid, d_gate, d_up, True)
        return [near_of(piece) for piece in given]

    def outward(out):
        return exchange(out.reshape(EXPERTS // 2, 2, MOST, width), "ep")

    def finish(start, received):
        return expert_weight_grads(
            after(own_rows, start), dyw, hid, d_gate, d_up, False, received
        )

    return (din, part, homeward, middle, outward, give, finish)


def experts_spread(rows_sent, grads_sent, other, router_t, weights):
    ep_count = lax.axis_size("ep")
    weg, weu, wed = weights
    width = rows_sent.shape[1]
    local_count = max(1, EXPERTS // ep_count)
    replicas = max(1, ep_count // EXPERTS)
    groups = EXPERTS // local_count
    gate_cols, up_cols, down_rows = (
        lax.all_gather(weg, SEQ, axis=1, tiled=True),
        lax.all_gather(weu, SEQ, axis=1, tiled=True),
        lax.all_gather(wed, SEQ, axis=0, tiled=True),
    )
    hidden_part = gate_cols.shape[1] // local_count
    gate_local = gate_cols.reshape(width, local_count, hidden_part).transpose(1, 0, 2)
    up_local = up_cols.reshape(width, local_count, hidden_part).transpose(1, 0, 2)
    down_local = down_rows.reshape(local_count, hidden_part, width)

    def spread(buffer):
        last = buffer.shape[-1]
        wide = buffer.reshape(groups, 1, local_count * MOST, last)
        wide = jnp.broadcast_to(wide, (groups, replicas, local_count * MOST, last))
        return exchange(wide.reshape(ep_count, local_count * MOST, last), "ep")

    def collect(buffer):
        last = buffer.shape[-1]
        return jnp.sum(
            exchange(buffer, "ep").astype(WIDE).reshape(groups, replicas, local_count * MOST, last),
            1,
        ).reshape(EXPERTS * MOST, last)

    def owner_layout(received):
        last = received.shape[-1]
        return (
            received.reshape(ep_count, local_count, MOST, last)
            .transpose(1, 0, 2, 3)
            .reshape(local_count, ep_count * MOST, last)
        )

    def source_layout(owned):
        last = owned.shape[-1]
        return (
            owned.reshape(local_count, ep_count, MOST, last)
            .transpose(1, 0, 2, 3)
            .reshape(ep_count, local_count * MOST, last)
        )

    def batched(spec, left_op, right_op):
        return jnp.einsum(spec, left_op, right_op, preferred_element_type=WIDE)

    own_rows = owner_layout(spread(rows_sent))
    got_grads = owner_layout(spread(grads_sent))
    got_other = owner_layout(spread(other[:, None]))
    first = lax.axis_index("ep") // replicas * local_count
    mine = first + jnp.arange(local_count)[:, None, None]
    lane = jnp.arange(EXPERTS)
    logits = batched("lrd,ed->lre", own_rows, router_t)
    hit_mine, hit_other = ((lane == mine).astype(WIDE), (lane == got_other).astype(WIDE))
    got_weight = jax.nn.sigmoid(jnp.sum(logits * (hit_mine - hit_other), -1, keepdims=True))
    gate_val = batched("lrd,ldh->lrh", own_rows, gate_local)
    up_val = batched("lrd,ldh->lrh", own_rows, up_local)
    silu_val, slope_val = silu_grad(gate_val)
    hidden_val = (silu_val * up_val).astype(LOW)
    out_rows = batched("lrh,lhd->lrd", hidden_val, down_local)
    back_out = collect(source_layout((got_weight * out_rows).astype(LOW)))
    grad_hidden = batched("lrd,lhd->lrh", got_grads, down_local)
    row_dot = jnp.sum(hidden_val.astype(WIDE) * grad_hidden, -1, keepdims=True)
    amount = got_weight * (1.0 - got_weight) * row_dot
    d_logits = (amount * (hit_mine - hit_other)).astype(LOW)
    part = jnp.sum(batched("lre,lrd->led", d_logits, own_rows), 0)
    scaled = got_weight * grad_hidden
    own_grads = (got_weight * got_grads.astype(WIDE)).astype(LOW)
    grad_gate = (scaled * up_val * slope_val).astype(LOW)
    grad_up = (scaled * silu_val).astype(LOW)
    din_rows = batched("lrh,ldh->lrd", grad_gate, gate_local)
    din_rows = din_rows + batched("lrh,ldh->lrd", grad_up, up_local)
    din_rows = din_rows + batched("lre,ed->lrd", d_logits, router_t)
    back_din = collect(source_layout(din_rows.astype(LOW)))
    grad_gate_w = batched("lrd,lrh->ldh", own_rows, grad_gate)
    grad_up_w = batched("lrd,lrh->ldh", own_rows, grad_up)
    grad_down_w = batched("lrh,lrd->lhd", hidden_val, own_grads)

    def share(full, axis):
        return lax.psum_scatter(
            full.astype(LOW), SEQ, scatter_dimension=axis, tiled=True
        ).astype(WIDE)

    return (
        back_out.astype(LOW),
        back_din.astype(LOW),
        jnp.pad(part, ((0, EXTRA - EXPERTS), (0, 0))),
        lambda start: (
            share(grad_gate_w.transpose(1, 0, 2).reshape(width, local_count * hidden_part), 1),
            share(grad_up_w.transpose(1, 0, 2).reshape(width, local_count * hidden_part), 1),
            share(grad_down_w.reshape(local_count * hidden_part, width), 0),
        ),
    )


def shards(
    tokens,
    cotangent,
    routes,
    priority,
    gain_attn,
    w_query,
    w_key,
    w_value,
    w_out,
    gain_ffn,
    w_shared_gate,
    w_shared_up,
    w_shared_down,
    w_router,
    w_expert_gate,
    w_expert_up,
    w_expert_down,
):
    tok_rows, width = tokens.shape
    rows_w = w_query.shape[0]
    fs_count = lax.axis_size("fx") * lax.axis_size("fc")
    ep_count = lax.axis_size("ep")
    devices = ep_count * fs_count
    seq_len = tok_rows * fs_count
    head_size = width // HEADS
    side, core = (lax.axis_index("fx"), lax.axis_index("fc"))
    fs_index = side * lax.axis_size("fc") + core
    my_rank = lax.axis_index("ep") * fs_count + fs_index
    my_expert = lax.axis_index("ep") * lax.axis_size("fx") + side
    ids = [core] + [fs_index ^ k for k in range(4)] + [my_expert, lax.axis_index("ep"), side]
    ids = jnp.stack(ids).astype(jnp.int32)

    small_own = jnp.concatenate([w_router.T, gain_attn[None], gain_ffn[None]], 0)
    small_own = jnp.pad(small_own, ((0, EXTRA - EXPERTS - 2), (0, width - rows_w)))
    pack = jnp.concatenate([tokens, small_own])
    pack_far = far_of(pack)
    dy_far = far_of(cotangent)
    qkv_stack = jnp.stack([w_query, w_key, w_value])
    qkv_cut = [
        lax.dynamic_slice_in_dim(qkv_stack, (fs_index ^ k) * rows_w, rows_w, 2) for k in range(4)
    ]

    def to_place(parts):
        got = [
            lax.ppermute(parts[k], SEQ, [(i, i ^ k) for i in range(fs_count)]) for k in (2, 3, 1)
        ]
        return (parts[0], got[2], got[0], got[1])

    w_parts = to_place(qkv_cut)
    x_parts = (pack, near_of(pack), pack_far, near_of(pack_far))

    lane = jnp.arange(2 * EXPERTS)
    zero_row = jnp.zeros((EXPERTS,), WIDE)
    lower = (jnp.arange(tok_rows)[:, None] > jnp.arange(tok_rows)[None, :]).astype(LOW)
    slot_iota = jnp.arange(EXPERTS * MOST)
    half_iota = jnp.arange(EXPERTS * MOST // 2)

    def plan(block_routes, block_priority):
        classes = jnp.stack([block_priority, 1 - block_priority], 1)
        named = block_routes + EXPERTS * classes
        hits = [(named[:, j : j + 1] == lane).astype(WIDE) for j in (0, 1)]
        both = hits[0] + hits[1]
        before = matmul(lower, both.astype(LOW))
        counts = jnp.sum(both, 0)
        local_table = before + jnp.concatenate([zero_row, counts[:EXPERTS]])
        ranks = [jnp.sum(local_table * hits[j], -1).astype(jnp.int32) for j in (0, 1)]
        return (hits, before, counts, ranks)

    def keep_of(block_plan, base):
        hits, before = block_plan[:2]
        capacity = 5 * tok_rows * devices // 32
        return [(jnp.sum((before + base) * hits[j], -1) < capacity).astype(LOW) for j in (0, 1)]

    def base_of(all_counts, rank):
        earlier = (jnp.arange(devices) < rank).astype(WIDE)
        base = jnp.sum(all_counts * earlier[:, None], 0)
        return base + jnp.concatenate([zero_row, jnp.sum(all_counts[:, :EXPERTS], 0)])

    own_plan = plan(routes, priority)
    counts, ranks = own_plan[2:]
    slot_hit = [
        ((routes[:, j] * MOST + ranks[j])[:, None] == slot_iota).astype(LOW) for j in (0, 1)
    ]
    dispatch = slot_hit[0] + slot_hit[1]
    others = jnp.stack([routes[:, 1], routes[:, 0]]).astype(LOW)
    other_sent = matmul(others[0:1], slot_hit[0]) + matmul(others[1:2], slot_hit[1])
    other_sent = other_sent.reshape(EXPERTS, MOST)
    pair_of_cores = EXPERTS == ep_count * lax.axis_size("fx")
    if pair_of_cores:
        tiny = jnp.concatenate(
            [jnp.broadcast_to(counts[None], (EXPERTS, 2 * EXPERTS)), other_sent], 1
        )
        tiny = jnp.pad(tiny, ((0, 0), (0, 128 - tiny.shape[1]))).astype(jnp.int32)
        tiny = jnp.broadcast_to(tiny[:, None], (EXPERTS, 2, 128)).reshape(devices, 1, 128)
        facts_far = far_of(jnp.concatenate([routes.T, priority[None]]))
        far_routes = facts_far[:2].T
        far_plan = plan(far_routes, facts_far[2])

        def side_hit(block_routes, block_ranks, j):
            place = (block_routes[:, j] >> 1) * MOST + block_ranks[j]
            same = (block_routes[:, j] & 1) == side
            return ((place[:, None] == half_iota) & same[:, None]).astype(LOW)

        own_side = [side_hit(routes, ranks, j) for j in (0, 1)]
        far_side = [side_hit(far_routes, far_plan[3], j) for j in (0, 1)]
        side_hits = (own_side[0] + own_side[1], far_side[0] + far_side[1])
        dy_sent = send_pair(ids, side_hits, (cotangent, dy_far))
        got_dy = exchange(dy_sent, "ep").reshape(-1, width)
        tiny_got = exchange(after(tiny, got_dy), ALL)
        all_counts = tiny_got[:, 0, : 2 * EXPERTS].astype(WIDE)
        other = lax.dynamic_index_in_dim(tiny_got.reshape(EXPERTS, 2, 128), core, 1, keepdims=False)
        other = other[:, 2 * EXPERTS : 2 * EXPERTS + MOST].reshape(EXPERTS * MOST, 1)
        far_keep = keep_of(far_plan, base_of(all_counts, my_rank ^ 2))
        own_keep = keep_of(own_plan, base_of(all_counts, my_rank))

        side_kept = (
            own_side[0] * own_keep[0][:, None] + own_side[1] * own_keep[1][:, None],
            far_side[0] * far_keep[0][:, None] + far_side[1] * far_keep[1][:, None],
        )
    else:
        spread_counts = jnp.broadcast_to(counts.astype(jnp.int32), (devices, 2 * EXPERTS))
        all_counts = exchange(spread_counts, ALL).astype(WIDE)
        kept = keep_of(own_plan, base_of(all_counts, my_rank))
        dispatch_kept = slot_hit[0] * kept[0][:, None] + slot_hit[1] * kept[1][:, None]

    forward_table, cos_table, sin_table = rope_constants(seq_len, head_size // 2)
    weights = (w_expert_gate, w_expert_up, w_expert_down)
    up_stack = jnp.stack([w_shared_gate, w_shared_up])
    ff_part = w_shared_gate.shape[1] // fs_count
    up_own = lax.dynamic_slice_in_dim(up_stack, side * 2 * ff_part, 2 * ff_part, 2)
    up_give = lax.dynamic_slice_in_dim(up_stack, (1 - side) * 2 * ff_part, 2 * ff_part, 2)

    def core_cut(piece, which):
        return lax.dynamic_slice_in_dim(piece, which * ff_part, ff_part, 2)

    up_mine, up_other = (core_cut(up_own, core), core_cut(up_own, 1 - core))
    ready = (*x_parts[1:], *w_parts[1:])
    out_far = far_of(after(w_out, *ready))
    out_near, dy_near = (near_of(piece) for piece in tie((w_out, cotangent), *ready))
    up_near = near_of(after(up_other, *ready))
    peers = []
    if pair_of_cores:
        peers = [near_of(piece) for piece in tie(weights, *ready)]
    ain, own_mats, (queries, keys, values), lse, att_own, small = attention_forward(
        ids, x_parts, w_parts, jnp.asarray(forward_table)
    )
    out_parts = (w_out, out_near, out_far, near_of(after(out_far, att_own[0])))
    att_parts = tie(to_place(att_own), *out_parts[1:])
    residual, ffn_input = after_attention(att_parts, out_parts, tokens, small)
    ffn_far = far_of(ffn_input)
    dy_parts = (cotangent, dy_near, dy_far, near_of(after(dy_far, ffn_far)))
    ffn_parts = (ffn_input, near_of(ffn_input), ffn_far, near_of(ffn_far))
    up_far = far_of(after(up_give, ffn_far))

    def shared():
        up_last = near_of(core_cut(up_far, 1 - core))
        up_parts = (up_mine, up_near, core_cut(up_far, core), up_last)
        return shared_branch(
            ids,
            ffn_parts,
            dy_parts,
            up_parts,
            w_shared_down,
            ep_count if pair_of_cores else 0,
        )

    def fold(parts):
        mine, give, mid = parts
        got = near_of(give)
        return (mine, got, far_of((mid.astype(WIDE) + got[1].astype(WIDE)).astype(LOW)))

    def ep_step(block, bit):
        return lax.ppermute(block, "ep", [(i, i ^ bit) for i in range(ep_count)])

    def added(first, second):
        return (first.astype(WIDE) + second.astype(WIDE)).astype(LOW)

    if pair_of_cores:
        got_dy = after(got_dy, *peers)
        rows_sent = send_pair(ids, tie(side_kept, got_dy), (ffn_input, ffn_far))
        din_sums, out_sums, (grads_keep, grads_give) = shared()
        grads_got = ep_step(grads_give, 1)
        din_sent, router_part, homeward, middle, outward, give_grads, last = experts_chip(
            ids, rows_sent, got_dy, other, small, weights, peers, (grads_keep,)
        )
        din_fold = fold(din_sums)
        half = added(grads_keep, after(grads_got, din_sent))
        back_din = homeward(after(din_sent, half))
        half_got = ep_step(half[1::2], 2)
        expert_out_rows = middle(half)
        back_din = after(back_din, half_got)
        quarter = added(half[0::2], half_got)
        quarter_got = ep_step(quarter[1:2], 4)
    else:
        dy_sent = contract_rows(dispatch, cotangent).astype(LOW)
        rows_sent = contract_rows(dispatch_kept, ffn_input).astype(LOW)
        back_out, back_din, router_part, expert_grads = experts_spread(
            rows_sent, dy_sent, other_sent.reshape(-1), small[:EXPERTS], weights
        )
        din_sums, out_sums, grads_rest = shared()
        din_fold = fold(din_sums)

    grad_resid, branch = back_at_tokens(
        din_fold, back_din, dispatch, residual, small, cotangent, router_part
    )
    branch_far = far_of(branch)
    branch_pair = (branch, branch_far)
    if pair_of_cores:
        own_chunk = added(quarter[0:1], after(quarter_got, branch))
        branch_pair = tie(branch_pair, own_chunk)
        back_out = outward(after(expert_out_rows, own_chunk, branch_far))
    branch_near, branch_last = (near_of(piece) for piece in branch_pair)
    branch_parts = (branch, branch_near, branch_far, branch_last)
    d_qkv, grads_qkv = attention_backward(
        ids, branch_parts, w_out, queries, keys, values, lse, ain, (cos_table, sin_table), ep_count if pair_of_cores else 1
    )
    strip = rows_w // ep_count
    grads_qkv = after(grads_qkv, back_out)
    if pair_of_cores:
        qkv_blocks = grads_qkv
    else:
        qkv_blocks = grads_qkv.transpose(1, 0, 2, 3).reshape(3, fs_count, ep_count, strip, rows_w)
        qkv_blocks = qkv_blocks.transpose(2, 1, 0, 3, 4).reshape(devices, 3, strip, rows_w)
    qkv_got = exchange(qkv_blocks, ALL)
    din_parts, grad_out_w = late_grads(ids, d_qkv, own_mats, att_own, branch_parts)
    in_fold = fold(din_parts)
    own_float = tokens.astype(WIDE)
    grad_in = in_fold[0].astype(WIDE) + in_fold[1][0].astype(WIDE) + in_fold[2].astype(WIDE)
    gain_one = small[EXPERTS : EXPERTS + 1].astype(WIDE)
    grad_tokens = grad_resid + rms_backward(grad_in, own_float, inverse_rms(own_float), gain_one)

    if pair_of_cores:
        out_near_sum = near_of(after(out_sums[1], qkv_blocks))
        own_total, far_total = take_pair(
            ids, side_hits, back_out, out_sums, out_near_sum, residual
        )
        output = (own_total + far_of(far_total).astype(WIDE)).astype(LOW)
    else:
        out_fold = fold(out_sums)
        total = residual + out_fold[0].astype(WIDE) + out_fold[1][0].astype(WIDE)
        total = total + out_fold[2].astype(WIDE) + matmul(dispatch, back_out)
        output = total.astype(LOW)
    qkv_got = qkv_got.reshape(ep_count, fs_count, 3, strip, rows_w).astype(WIDE)
    qkv_sum = jnp.sum(qkv_got, 0).transpose(1, 2, 0, 3).reshape(3 * strip, width).astype(LOW)
    small_part = lax.dynamic_slice_in_dim(grad_out_w[rows_w:], fs_index * rows_w, rows_w, 1)
    if pair_of_cores:
        lines = EXTRA * rows_w // (ep_count * width)
        parts = jnp.concatenate(
            [
                grad_out_w[:rows_w].reshape(ep_count, strip, width),
                small_part.reshape(ep_count, lines, width),
            ],
            1,
        )
        cut = 2 * rows_w // ep_count
        turned = to_place([own_chunk[0, k * cut : (k + 1) * cut] for k in range(4)])
        whole = jnp.concatenate([*turned, own_chunk[0, 4 * cut :]])[None]
        for bit, far_bit in ((1, 4), (2, 2)):
            keep, give = split_part(parts, bit)
            got, whole_got = (ep_step(give, bit), ep_step(whole, far_bit))
            got, whole_got = lax.optimization_barrier((got, whole_got))
            parts = added(keep, got)
            whole = jnp.concatenate([whole, whole_got])
        keep, give = split_part(parts, 4)
        whole_got = ep_step(whole, 1)
        out_sum = added(keep, ep_step(give, 4))[0]
    else:
        lines = 0
        out_whole = lax.psum((grad_out_w[:rows_w], small_part), "ep")
        out_sum = jnp.zeros((0, width), LOW)
    sums = jnp.concatenate([qkv_sum, out_sum])
    sums = exchange(jnp.broadcast_to(sums[None], (ep_count,) + sums.shape), "ep")
    mats = (w_query, w_key, w_value)
    if pair_of_cores:
        *qkv_all, sum_out_w, gain_col = place_dense(sums, mats, gain_attn[:, None], strip)
        sum_gain_one = gain_col[:, 0]
        sum_small = sums[:, 4 * strip : 4 * strip + lines].astype(WIDE).reshape(EXTRA, rows_w)
    else:
        sums = sums.astype(WIDE)
        qkv_all = sums.reshape(ep_count, 3, strip, width)
        qkv_all = qkv_all.transpose(1, 0, 2, 3).reshape(3, rows_w, width)
        sum_out_w, sum_small = (piece.astype(WIDE) for piece in out_whole)
        sum_gain_one = sum(
            jnp.sum(qkv_all[i] * mat.astype(WIDE), -1) for i, mat in enumerate(mats)
        )
        sum_gain_one = sum_gain_one / gain_attn.astype(WIDE)
    sum_router, sum_gain_two = (sum_small[:EXPERTS].T, sum_small[EXPERTS])
    if pair_of_cores:
        received = give_grads(qkv_blocks)
        expert_grads = last(qkv_blocks, received)
        whole = [whole, after(whole_got, expert_grads[0])]
        sum_sgate, sum_sup, sum_sdown = place_shared(ids, whole, rows_w, width)
    else:
        expert_grads = expert_grads(grads_qkv)
        dense = lax.psum((*to_place(grads_rest[:4]), grads_rest[4]), "ep")
        sum_sdown = dense[4].astype(WIDE)
        wide_rel = jnp.stack([piece.astype(WIDE) for piece in dense[:4]])
        wide_all = jnp.concatenate(
            [
                lax.dynamic_index_in_dim(wide_rel, fs_index ^ k, 0, keepdims=False)
                for k in range(4)
            ],
            2,
        )
        sum_sgate, sum_sup = (wide_all[0], wide_all[1])
    return (
        output,
        grad_tokens,
        sum_gain_one,
        qkv_all[0],
        qkv_all[1],
        qkv_all[2],
        sum_out_w,
        sum_gain_two,
        sum_sgate,
        sum_sup,
        sum_sdown,
        sum_router,
        *expert_grads,
    )


def solution(mesh):
    ep_count, fs_count = mesh.devices.shape
    cut_mesh = Mesh(mesh.devices.reshape(ep_count, fs_count // 2, 2), ALL)
    tok = P(ALL, None)
    row = P(SEQ, None)
    return jax.shard_map(
        shards,
        mesh=cut_mesh,
        in_specs=(
            tok,
            tok,
            tok,
            P(ALL),
            P(SEQ),
            row,
            row,
            row,
            row,
            P(SEQ),
            row,
            row,
            row,
            row,
            P(None, ALL),
            P(None, ALL),
            tok,
        ),
        out_specs=(
            tok,
            tok,
            P(SEQ),
            row,
            row,
            row,
            row,
            P(SEQ),
            row,
            row,
            row,
            row,
            P(None, ALL),
            P(None, ALL),
            tok,
        ),
        check_vma=False,
    )
```

```python
import jax
import jax.numpy as jnp
import numpy as np
from jax import lax
from jax.experimental import pallas as pl
from jax.experimental.pallas import tpu as pltpu
from jax.sharding import Mesh
from jax.sharding import PartitionSpec as P

HEADS = 12
EXPERTS = 16
MOST = 48
EXTRA = 2 * EXPERTS
LIGHT = 20

EPS = 1e-06
NEG = -1e30
LOW = jnp.bfloat16
WIDE = jnp.float32
ALL = ("ep", "fx", "fc")
SEQ = ("fx", "fc")
SWAP = [(0, 1), (1, 0)]
VMEM = pl.BlockSpec(memory_space=pltpu.VMEM)
SMEM = pl.BlockSpec(memory_space=pltpu.SMEM)


def matmul(left_op, right_op):
    return jnp.dot(left_op, right_op, preferred_element_type=WIDE)


def contract_rows(left_op, right_op):
    return lax.dot_general(left_op, right_op, (((0,), (0,)), ((), ())), preferred_element_type=WIDE)


def contract_cols(left_op, right_op):
    return lax.dot_general(left_op, right_op, (((1,), (1,)), ((), ())), preferred_element_type=WIDE)


def inverse_rms(values):
    return lax.rsqrt(jnp.mean(values * values, -1, keepdims=True) + EPS)


def rms_backward(upstream, values, inverse, gain_vec):
    scaled = upstream * gain_vec
    return inverse * scaled - values * inverse**3 * jnp.mean(scaled * values, -1, keepdims=True)


def silu_grad(gate_val):
    sigma = jax.nn.sigmoid(gate_val)
    return (gate_val * sigma, sigma * (1.0 + gate_val * (1.0 - sigma)))


def far_of(block):
    return lax.ppermute(block, "fx", SWAP)


def near_of(block):
    return lax.ppermute(block, "fc", SWAP)


def after(value, *others):
    return lax.optimization_barrier((value, *others))[0]


def tie(values, *others):
    return lax.optimization_barrier((*values, *others))[: len(values)]


def exchange(blocks, axes):
    return lax.all_to_all(blocks, axes, split_axis=0, concat_axis=0, tiled=True)


def split_part(parts, bit):
    cut = parts.reshape((parts.shape[0] // 2, 2) + parts.shape[1:])
    mine = lax.rem(lax.axis_index("ep") // bit, 2)
    keep = lax.dynamic_index_in_dim(cut, mine, 1, keepdims=False)
    return (keep, lax.dynamic_index_in_dim(cut, 1 - mine, 1, keepdims=False))


def shape_of(dims, kind):
    return jax.ShapeDtypeStruct(dims, kind)


def run_kernel(body, outs, args, specs=None, out_specs=None, scratch=(), grid=None, flops=0, move=0):
    options = {} if grid is None else {"grid": grid}
    return pl.pallas_call(
        body,
        out_shape=outs,
        in_specs=specs if specs is not None else [VMEM] * len(args),
        out_specs=out_specs if out_specs is not None else [VMEM] * len(outs),
        scratch_shapes=list(scratch),
        compiler_params=pltpu.CompilerParams(vmem_limit_bytes=52 * 2**20),
        cost_estimate=pl.CostEstimate(
            flops=flops // LIGHT, bytes_accessed=move // LIGHT, transcendentals=0
        ),
        **options,
    )(*args)


def pick_rows(first_iota, second_iota, source):
    return (first_iota == source(second_iota)).astype(LOW)


def rope_constants(length, half):
    freq = np.exp(-np.log(np.float32(10000.0)) * np.arange(half, dtype=np.float32) / np.float32(half))
    angle = np.arange(length, dtype=np.float32)[:, None] * freq.astype(np.float32)[None, :]
    cosine, sine = (np.cos(angle), np.sin(angle))
    return (
        np.concatenate([cosine, cosine, sine, sine], 1).astype(np.float32),
        np.concatenate([cosine] * 4, 1).astype(np.float32),
        np.concatenate([sine, -sine, sine, -sine], 1).astype(np.float32),
    )


def attention_forward(ids, x_parts, w_parts, table):
    full, width = x_parts[0].shape
    rows = full - EXTRA
    block = w_parts[0].shape[1]
    length = 4 * rows
    heads = block // 64
    size = heads * 128

    def body(ids_ref, *refs):
        x_refs, w_refs, table_ref = (refs[:4], refs[4:8], refs[8])
        ain_ref, own_ref, q_ref, k_ref, v_ref, lse_ref = refs[9:15]
        att_refs, small_ref = (refs[15:19], refs[19])
        att_scr = refs[20]
        first = lax.broadcasted_iota(jnp.int32, (block, width), 0)
        lane = lax.broadcasted_iota(jnp.int32, (block, width), 1)
        small = jnp.zeros((EXTRA, width), WIDE)
        for k in range(4):
            place = jnp.where(lane == first + ids_ref[1 + k] * block, 1.0, 0.0).astype(LOW)
            small = small + matmul(x_refs[k][rows:, :block], place)
        small_ref[...] = small.astype(LOW)
        gain = small[EXPERTS : EXPERTS + 1, :]
        for k in range(4):
            place = ids_ref[1 + k]
            piece = x_refs[k][:rows, :].astype(WIDE)
            ain_ref[pl.ds(place * rows, rows), :] = (piece * inverse_rms(piece) * gain).astype(LOW)
            for m in range(3):
                own_ref[m, pl.ds(place * block, block), :] = w_refs[k][m]
        first = lax.broadcasted_iota(jnp.int32, (block, size), 0)
        lane = lax.broadcasted_iota(jnp.int32, (block, size), 1)
        head, inner = (lane // 128, lane % 128)
        low = inner % 64
        swapped = jnp.where(low < 32, low + 32, low - 32)
        source = 64 * head + jnp.where(inner < 64, low, swapped)
        sign = jnp.where((inner >= 64) & (low < 32), -1.0, 1.0)
        turn = jnp.where(first == source, sign, 0.0).astype(LOW)
        keep = (inner // 64 == head % 2) & (first == 64 * head + low)
        place_v = jnp.where(keep, 1.0, 0.0).astype(LOW)
        w_q = matmul(own_ref[0], turn).astype(LOW)
        w_k = matmul(own_ref[1], turn).astype(LOW)
        w_v = matmul(own_ref[2], place_v).astype(LOW)
        half = lax.broadcasted_iota(jnp.int32, (rows, 128), 1) < 64
        for i in range(4):
            span = slice(i * rows, (i + 1) * rows)
            ain = ain_ref[span, :]
            y_q, y_k, y_v = (matmul(ain, w_q), matmul(ain, w_k), matmul(ain, w_v))
            tab = table_ref[span, :]
            for h in range(heads):
                cols = slice(128 * h, 128 * h + 128)
                turned = y_q[:, cols] * tab
                turned = (turned + pltpu.roll(turned, 64, 1)).astype(LOW).astype(WIDE)
                q_ref[h, span, :] = jnp.where(half, turned * 0.125, 0.0).astype(LOW)
                turned = y_k[:, cols] * tab
                k_ref[h, span, :] = (turned + pltpu.roll(turned, 64, 1)).astype(LOW)
                v_ref[h, span, :] = y_v[:, cols].astype(LOW)
        tri = lax.broadcasted_iota(jnp.int32, (rows, rows), 0) >= lax.broadcasted_iota(
            jnp.int32, (rows, rows), 1
        )
        for i in range(4):
            span = slice(i * rows, (i + 1) * rows)
            done = slice(0, i * rows)
            every = range(heads)
            diags = [
                jnp.where(tri, contract_cols(q_ref[h, span, :], k_ref[h, span, :]), NEG)
                for h in every
            ]
            tops = [jnp.max(diag, -1, keepdims=True) for diag in diags]
            if i:
                pasts = [contract_cols(q_ref[h, span, :], k_ref[h, done, :]) for h in every]
                tops = [
                    jnp.maximum(tops[h], jnp.max(pasts[h], -1, keepdims=True)) for h in every
                ]
                pasts = [jnp.exp(pasts[h] - tops[h]) for h in every]
            diags = [jnp.exp(diags[h] - tops[h]) for h in every]
            totals = [jnp.sum(diag, -1, keepdims=True) for diag in diags]
            if i:
                totals = [totals[h] + jnp.sum(pasts[h], -1, keepdims=True) for h in every]
            scales = [1.0 / total for total in totals]
            tiles = [
                matmul((diags[h] * scales[h]).astype(LOW), v_ref[h, span, :]) for h in every
            ]
            if i:
                tiles = [
                    tiles[h] + matmul((pasts[h] * scales[h]).astype(LOW), v_ref[h, done, :])
                    for h in every
                ]
            for h in every:
                lse_ref[h, span, :] = tops[h] + jnp.log(totals[h])
            for t in range((heads + 1) // 2):
                pair = tiles[2 * t] + (tiles[2 * t + 1] if 2 * t + 1 < heads else 0.0)
                wide = min(128, block - 128 * t)
                att_scr[span, 128 * t : 128 * t + wide] = pair[:, :wide].astype(LOW)
        for k in range(4):
            att_refs[k][...] = att_scr[pl.ds(ids_ref[1 + k] * rows, rows), :]

    outs = (
        [shape_of((length, width), LOW), shape_of((3, width, block), LOW)]
        + [shape_of((heads, length, 128), LOW)] * 3
        + [shape_of((heads, length, 1), WIDE)]
        + [shape_of((rows, block), LOW)] * 4
        + [shape_of((EXTRA, width), LOW)]
    )
    args = [ids, *x_parts, *w_parts, table]
    got = run_kernel(
        body,
        outs,
        args,
        specs=[SMEM] + [VMEM] * (len(args) - 1),
        scratch=[pltpu.VMEM((length, block), LOW)],
        flops=8 * 10**9,
        move=12 * 10**6,
    )
    return (got[0], got[1], got[2:5], got[5], got[6:10], got[10])


def after_attention(att_parts, out_parts, tokens, small):
    rows, width = tokens.shape

    def body(*refs):
        att_refs, out_refs = (refs[:4], refs[4:8])
        tok_ref, small_ref, res_ref, ffn_ref = refs[8:]
        total = tok_ref[...].astype(WIDE)
        for k in range(4):
            total = total + matmul(att_refs[k][...], out_refs[k][...])
        res_ref[...] = total
        gain = small_ref[EXPERTS + 1 : EXPERTS + 2, :].astype(WIDE)
        ffn_ref[...] = (total * inverse_rms(total) * gain).astype(LOW)

    outs = [shape_of((rows, width), WIDE), shape_of((rows, width), LOW)]
    args = [*att_parts, *out_parts, tokens, small]
    return run_kernel(body, outs, args, flops=6 * 10**8, move=4 * 10**6)


def send_pair(ids, hits, blocks):
    rows, width = blocks[0].shape
    groups = hits[0].shape[1] // MOST

    def body(ids_ref, own_hit, far_hit, own_ref, far_ref, out_ref):
        for hit, block, place in (
            (own_hit, own_ref, ids_ref[7]),
            (far_hit, far_ref, 1 - ids_ref[7]),
        ):
            sent = contract_rows(hit[...], block[...]).astype(LOW)
            for g in range(groups):
                out_ref[g, place] = sent[g * MOST : (g + 1) * MOST, :]

    return run_kernel(
        body,
        [shape_of((groups, 2, MOST, width), LOW)],
        [ids, *hits, *blocks],
        specs=[SMEM] + [VMEM] * 4,
        flops=6 * 10**8,
        move=3 * 10**6,
    )[0]


def take_pair(ids, hits, back, sums, near_sum, residual):
    groups, _, _, width = back.shape
    rows = residual.shape[0]

    def body(ids_ref, own_hit, far_hit, back_ref, mine_ref, mid_ref, near_ref, res_ref, own_out, far_out):
        own = res_ref[...] + mine_ref[...].astype(WIDE) + near_ref[0].astype(WIDE)
        far = mid_ref[...].astype(WIDE) + near_ref[1].astype(WIDE)
        for g in range(groups):
            cols = slice(g * MOST, (g + 1) * MOST)
            own = own + matmul(own_hit[:, cols], back_ref[g, ids_ref[7]])
            far = far + matmul(far_hit[:, cols], back_ref[g, 1 - ids_ref[7]])
        own_out[...] = own
        far_out[...] = far.astype(LOW)

    return run_kernel(
        body,
        [shape_of((rows, width), WIDE), shape_of((rows, width), LOW)],
        [ids, *hits, back, sums[0], sums[2], near_sum, residual],
        specs=[SMEM] + [VMEM] * 7,
        flops=6 * 10**8,
        move=5 * 10**6,
    )


def shared_branch(ids, ffn_parts, dy_parts, w_parts, down, chunks):
    rows, width = ffn_parts[0].shape
    block, hidden = w_parts[0].shape[1:]

    def body(ids_ref, *refs):
        ffn_refs, dy_refs, w_refs = (refs[:4], refs[4:8], refs[8:12])
        down_ref = refs[12]
        sum_refs, grad_refs = (refs[13:19], refs[19:-3])
        w_scr, g_scr, d_scr = refs[-3:]
        for k in range(4):
            for m in range(2):
                w_scr[m, pl.ds(ids_ref[1 + k] * block, block), :] = w_refs[k][m]
        for k in range(4):
            ffn, dy = (ffn_refs[k][...], dy_refs[k][...])
            gate, up = (matmul(ffn, w_scr[0]), matmul(ffn, w_scr[1]))
            silu, slope = silu_grad(gate)
            hid = (silu * up).astype(LOW)
            back = contract_cols(dy, down_ref[...])
            d_gate = (back * up * slope).astype(LOW)
            d_up = (back * silu).astype(LOW)
            din = (contract_cols(d_gate, w_scr[0]) + contract_cols(d_up, w_scr[1])).astype(LOW)
            out = matmul(hid, down_ref[...]).astype(LOW)
            for n, value in enumerate((din, out)):
                mine_ref, near_ref, mid_ref = sum_refs[3 * n : 3 * n + 3]
                if k % 2 == 0:
                    target = mine_ref if k == 0 else mid_ref
                    target[...] = value
                else:
                    near_ref[k // 2] = value
            parts = (contract_rows(ffn, d_gate), contract_rows(ffn, d_up), contract_rows(hid, dy))
            if k == 0:
                g_scr[0], g_scr[1], d_scr[...] = parts
            else:
                g_scr[0] += parts[0]
                g_scr[1] += parts[1]
                d_scr[...] += parts[2]
        if chunks:
            per = chunks // 2
            cut, line = (block // per, hidden // chunks)
            for r in range(chunks):
                part = ids_ref[6] ^ r
                target, slot = (grad_refs[(r >> 1) & 1], (r & 1) + 2 * (r >> 2))
                which, low = (part // per, part % per)
                for k in range(4):
                    start = ids_ref[1 + k] * block + low * cut
                    target[slot, k * cut : (k + 1) * cut, :] = g_scr[
                        which, pl.ds(pl.multiple_of(start, 16), cut), :
                    ].astype(LOW)
                start = pl.multiple_of(part * line, 16)
                piece = d_scr[pl.ds(start, line), :].astype(LOW)
                base = 4 * cut
                target[slot, base : base + line, :] = piece[:, :hidden]
                target[slot, base + line :, : hidden // 2] = piece[: line // 2, hidden:]
                target[slot, base + line :, hidden // 2 :] = piece[line // 2 :, hidden:]
        else:
            for k in range(4):
                for m in range(2):
                    grad_refs[k][m] = g_scr[m, pl.ds(ids_ref[1 + k] * block, block), :].astype(LOW)
            grad_refs[4][...] = d_scr[...].astype(LOW)

    if chunks:
        lines = 4 * block * 2 // chunks + 3 * hidden // chunks // 2
        grad_outs = [shape_of((chunks // 2, lines, hidden), LOW)] * 2
    else:
        grad_outs = [shape_of((2, block, hidden), LOW)] * 4 + [shape_of((hidden, width), LOW)]
    sums = [shape_of((rows, width), LOW), shape_of((2, rows, width), LOW), shape_of((rows, width), LOW)]
    outs = sums * 2 + grad_outs
    args = [ids, *ffn_parts, *dy_parts, *w_parts, down]
    got = run_kernel(
        body,
        outs,
        args,
        specs=[SMEM] + [VMEM] * (len(args) - 1),
        scratch=[
            pltpu.VMEM((2, width, hidden), LOW),
            pltpu.VMEM((2, width, hidden), WIDE),
            pltpu.VMEM((hidden, width), WIDE),
        ],
        flops=7 * 10**9,
        move=14 * 10**6,
    )
    return (got[0:3], got[3:6], got[6:])


def place_shared(ids, groups, block, width):
    per_group, lines, hidden = groups[0].shape
    chunks = per_group * len(groups)
    per = chunks // 2
    cut, line = (block // per, hidden // chunks)
    order = (0, 4, 2, 6, 1, 5, 3, 7)

    def body(ids_ref, *refs):
        gate_ref, up_ref, down_ref = refs[-3:]
        for n in range(chunks):
            part = ids_ref[6] ^ order[n]
            which, low = (part // per, part % per)
            piece = refs[n // per_group][n % per_group].astype(WIDE)
            for k in range(4):
                lane = pl.multiple_of(ids_ref[1 + k] * hidden, 128)
                value = piece[k * cut : (k + 1) * cut, :]
                place = (pl.ds(pl.multiple_of(low * cut, 16), cut), pl.ds(lane, hidden))

                @pl.when(which == 0)
                def to_gate(place=place, value=value):
                    gate_ref[place] = value

                @pl.when(which == 1)
                def to_up(place=place, value=value):
                    up_ref[place] = value

            base = 4 * cut
            start = pl.multiple_of(part * line, 16)
            down_ref[pl.ds(start, line), :hidden] = piece[base : base + line, :]
            tail = piece[base + line :, :]
            down_ref[pl.ds(start, line // 2), hidden:] = tail[:, : hidden // 2]
            down_ref[pl.ds(start + line // 2, line // 2), hidden:] = tail[:, hidden // 2 :]

    return run_kernel(
        body,
        [shape_of((block, 4 * hidden), WIDE)] * 2 + [shape_of((hidden, width), WIDE)],
        [ids, *groups],
        specs=[SMEM] + [VMEM] * len(groups),
        move=8 * 10**6,
    )


def place_dense(sums, w_parts, gain, strip):
    parts, lines, width = sums.shape
    block = parts * strip

    def body(sums_ref, a_ref, b_ref, c_ref, gain_ref, *outs):
        gain_sum = jnp.zeros((block, 1), WIDE)
        for m, w_ref in enumerate((a_ref, b_ref, c_ref)):
            for p in range(parts):
                outs[m][p * strip : (p + 1) * strip, :] = sums_ref[
                    p, m * strip : (m + 1) * strip, :
                ].astype(WIDE)
            gain_sum = gain_sum + jnp.sum(outs[m][...] * w_ref[...].astype(WIDE), -1, keepdims=True)
        for p in range(parts):
            outs[3][p * strip : (p + 1) * strip, :] = sums_ref[
                p, 3 * strip : 4 * strip, :
            ].astype(WIDE)
        outs[4][...] = gain_sum / gain_ref[...].astype(WIDE)

    return run_kernel(
        body,
        [shape_of((block, width), WIDE)] * 4 + [shape_of((block, 1), WIDE)],
        [sums, *w_parts, gain],
        move=5 * 10**6,
    )


def expert_main(ids, rows_in, dy_in, mats, other, router_t):
    count, width = rows_in.shape
    own_hidden = mats[0].shape[1]
    tile = 512
    steps = 2 * own_hidden // tile
    half = steps // 2
    chunk = 256

    def body(ids_ref, rows_ref, dy_ref, *refs):
        own, peer = (refs[0:3], refs[3:6])
        other_ref, router_ref = refs[6:8]
        din_ref, hid_ref, dg_ref, du_ref, dyw_ref, w_ref, part_ref = refs[8:15]
        acc, dot_scr = refs[15:17]
        step = pl.program_id(0)
        expert = ids_ref[5]

        @pl.when(step == 0)
        def start():
            for r in range(0, count, chunk):
                span = slice(r, r + chunk)
                logits = contract_cols(rows_ref[span, :], router_ref[...])
                lane = lax.broadcasted_iota(jnp.int32, logits.shape, 1)
                mine = jnp.sum(jnp.where(lane == expert, logits, 0.0), -1, keepdims=True)
                rest = jnp.sum(jnp.where(lane == other_ref[span, :], logits, 0.0), -1, keepdims=True)
                weight = jax.nn.sigmoid(mine - rest)
                w_ref[span, :] = weight
                dyw_ref[span, :] = (weight * dy_ref[span, :].astype(WIDE)).astype(LOW)
                dot_scr[span, :] = jnp.zeros((chunk, 1), WIDE)
                acc[span, :] = jnp.zeros((chunk, width), WIDE)

        def work(gate_ref, up_ref, down_ref):
            for r in range(0, count, chunk):
                span = slice(r, r + chunk)
                rows = rows_ref[span, :]
                gate, up = (matmul(rows, gate_ref[...]), matmul(rows, up_ref[...]))
                back = contract_cols(dy_ref[span, :], down_ref[...])
                silu, slope = silu_grad(gate)
                hid = (silu * up).astype(LOW)
                hid_ref[span, :] = hid
                dot_scr[span, :] += jnp.sum(hid.astype(WIDE) * back, -1, keepdims=True)
                scaled = w_ref[span, :] * back
                d_gate = (scaled * up * slope).astype(LOW)
                d_up = (scaled * silu).astype(LOW)
                dg_ref[span, :] = d_gate
                du_ref[span, :] = d_up
                acc[span, :] += contract_cols(d_gate, gate_ref[...]) + contract_cols(
                    d_up, up_ref[...]
                )

        @pl.when(step < half)
        def first():
            work(*own)

        @pl.when(step >= half)
        def second():
            work(*peer)

        @pl.when(step == steps - 1)
        def finish():
            for r in range(0, count, chunk):
                span = slice(r, r + chunk)
                weight = w_ref[span, :]
                amount = weight * (1.0 - weight) * dot_scr[span, :]
                lane = lax.broadcasted_iota(jnp.int32, (chunk, EXTRA), 1)
                signs = jnp.where(lane == expert, 1.0, 0.0) - jnp.where(
                    lane == other_ref[span, :], 1.0, 0.0
                )
                d_logit = (amount * signs).astype(LOW)
                din_ref[span, :] = (acc[span, :] + matmul(d_logit, router_ref[...])).astype(LOW)
                part = contract_rows(d_logit, rows_ref[span, :])
                part_ref[...] = part if r == 0 else part_ref[...] + part

    def fixed(dims):
        return pl.BlockSpec(dims, lambda j: (0,) * len(dims))

    def near(j):
        return jnp.minimum(j, half - 1)

    def late(j):
        return jnp.maximum(j - half, 0)

    cols = (width, tile)
    specs = [SMEM, fixed((count, width)), fixed((count, width))]
    for place in (near, late):
        specs += [
            pl.BlockSpec(cols, lambda j, place=place: (0, place(j))),
            pl.BlockSpec(cols, lambda j, place=place: (0, place(j))),
            pl.BlockSpec((tile, width), lambda j, place=place: (place(j), 0)),
        ]
    specs += [fixed((count, 1)), fixed(router_t.shape)]
    tiles = pl.BlockSpec((count, tile), lambda j: (0, j))
    outs = (
        [shape_of((count, width), LOW)]
        + [shape_of((count, 2 * own_hidden), LOW)] * 3
        + [shape_of((count, width), LOW), shape_of((count, 1), WIDE), shape_of(router_t.shape, WIDE)]
    )
    out_specs = [
        fixed((count, width)),
        tiles,
        tiles,
        tiles,
        fixed((count, width)),
        fixed((count, 1)),
        fixed(router_t.shape),
    ]
    return run_kernel(
        body,
        outs,
        [ids, rows_in, dy_in, *mats, other, router_t],
        specs=specs,
        out_specs=out_specs,
        scratch=[pltpu.VMEM((count, width), WIDE), pltpu.VMEM((count, 1), WIDE)],
        grid=(steps,),
        flops=12 * 10**9,
        move=22 * 10**6,
    )


def expert_out(hid, weight, down_own, down_peer):
    count, hidden = hid.shape
    width = down_own.shape[1]
    half = hidden // 2
    chunk = 256

    def body(hid_ref, w_ref, own_ref, peer_ref, out_ref):
        for r in range(0, count, chunk):
            span = slice(r, r + chunk)
            total = matmul(hid_ref[span, :half], own_ref[...])
            total = total + matmul(hid_ref[span, half:], peer_ref[...])
            out_ref[span, :] = (w_ref[span, :] * total).astype(LOW)

    return run_kernel(
        body,
        [shape_of((count, width), LOW)],
        [hid, weight, down_own, down_peer],
        flops=2 * 10**9,
        move=8 * 10**6,
    )[0]


def expert_weight_grads(rows_in, dyw, hid, d_gate, d_up, peer, add=None):
    count, width = rows_in.shape
    half = hid.shape[1] // 2
    tile = 512
    steps = half // tile
    offset = steps if peer else 0
    kind = LOW if add is None else WIDE

    def body(rows_ref, dyw_ref, hid_ref, dg_ref, du_ref, *refs):
        outs = refs[-3:]
        grads = (
            contract_rows(rows_ref[...], dg_ref[...]),
            contract_rows(rows_ref[...], du_ref[...]),
            contract_rows(hid_ref[...], dyw_ref[...]),
        )
        for i in range(3):
            value = grads[i] if add is None else grads[i] + refs[i][...].astype(WIDE)
            outs[i][...] = value.astype(kind)

    def fixed(dims):
        return pl.BlockSpec(dims, lambda j: (0,) * len(dims))

    tiles = pl.BlockSpec((count, tile), lambda j: (0, j + offset))
    cols = pl.BlockSpec((width, tile), lambda j: (0, j))
    lines = pl.BlockSpec((tile, width), lambda j: (j, 0))
    specs = [fixed((count, width)), fixed((count, width)), tiles, tiles, tiles]
    extra = [] if add is None else list(add)
    return run_kernel(
        body,
        [shape_of((width, half), kind), shape_of((width, half), kind), shape_of((half, width), kind)],
        [rows_in, dyw, hid, d_gate, d_up, *extra],
        specs=specs + ([] if add is None else [cols, cols, lines]),
        out_specs=[cols, cols, lines],
        grid=(steps,),
        flops=37 * 10**8,
        move=14 * 10**6,
    )


def back_at_tokens(fold, back_din, dispatch, residual, small, cotangent, router_part):
    rows, width = residual.shape

    def body(one_ref, two_ref, last_ref, back_ref, disp_ref, res_ref, small_ref, dy_ref, part_ref, dres_ref, br_ref):
        d_ffn = one_ref[...].astype(WIDE) + two_ref[0].astype(WIDE) + last_ref[...].astype(WIDE)
        d_ffn = d_ffn + matmul(disp_ref[...], back_ref[...])
        residual_val = res_ref[...]
        inverse = inverse_rms(residual_val)
        gain = small_ref[EXPERTS + 1 : EXPERTS + 2, :].astype(WIDE)
        d_res = dy_ref[...].astype(WIDE) + rms_backward(d_ffn, residual_val, inverse, gain)
        dres_ref[...] = d_res
        br_ref[0:rows, :] = d_res.astype(LOW)
        gain_part = jnp.sum(d_ffn * residual_val * inverse, 0, keepdims=True)
        line = lax.broadcasted_iota(jnp.int32, (EXTRA, width), 0)
        extra = jnp.where(line == EXPERTS, gain_part, part_ref[...])
        br_ref[rows:, :] = extra.astype(LOW)

    return run_kernel(
        body,
        [shape_of((rows, width), WIDE), shape_of((rows + EXTRA, width), LOW)],
        [*fold, back_din, dispatch, residual, small, cotangent, router_part],
        flops=3 * 10**8,
        move=5 * 10**6,
    )


def attention_backward(ids, branch, w_out, queries, keys, values, lse, ain, tables, groups):
    heads, length, _ = queries.shape
    rows = length // 4
    block, width = w_out.shape
    tiles = (heads + 1) // 2
    strip = block // groups

    def body(ids_ref, *refs):
        br_refs = refs[:4]
        wo_ref, q_ref, k_ref, v_ref, lse_ref, ain_ref, cc_ref, ss_ref = refs[4:12]
        d_ref, g_ref = refs[12:14]
        da_scr, dk_scr, dv_scr = refs[14:17]
        zero = jnp.zeros((rows, 128), WIDE)
        for k in range(4):
            d_att = contract_cols(br_refs[k][0:rows, :], wo_ref[...]).astype(LOW)
            place = ids_ref[1 + k] * rows
            for t in range(tiles):
                wide = min(128, block - 128 * t)
                if wide < 128:
                    da_scr[t, pl.ds(place, rows), :] = zero.astype(LOW)
                da_scr[t, pl.ds(place, rows), 0:wide] = d_att[:, 128 * t : 128 * t + wide]
        half = lax.broadcasted_iota(jnp.int32, (rows, 128), 1) < 64
        tri = lax.broadcasted_iota(jnp.int32, (rows, rows), 0) >= lax.broadcasted_iota(
            jnp.int32, (rows, rows), 1
        )

        def place_tile(m, span, h, value):
            t = h // 2
            wide = min(128, block - 128 * t)
            if h % 2 == 0:
                d_ref[m, span, 128 * t : 128 * t + wide] = value[:, :wide].astype(LOW)
            else:
                kept = d_ref[m, span, 128 * t : 128 * t + 128].astype(WIDE)
                d_ref[m, span, 128 * t : 128 * t + 128] = jnp.where(half, kept, value).astype(LOW)

        def unturn(value, span):
            return value * cc_ref[span, :] + pltpu.roll(value, 32, 1) * ss_ref[span, :]

        every = range(heads)
        for i in range(4):
            span = slice(i * rows, (i + 1) * rows)
            done = slice(0, i * rows)
            queries_i = [q_ref[h, span, :] for h in every]
            d_atts = [da_scr[h // 2, span, :] for h in every]
            levels = [lse_ref[h, span, :] for h in every]
            diags = [contract_cols(queries_i[h], k_ref[h, span, :]) for h in every]
            d_diags = [contract_cols(d_atts[h], v_ref[h, span, :]) for h in every]
            diags = [jnp.exp(jnp.where(tri, diags[h] - levels[h], NEG)) for h in every]
            inners = [jnp.sum(diags[h] * d_diags[h], -1, keepdims=True) for h in every]
            if i:
                pasts = [contract_cols(queries_i[h], k_ref[h, done, :]) for h in every]
                d_pasts = [contract_cols(d_atts[h], v_ref[h, done, :]) for h in every]
                pasts = [jnp.exp(pasts[h] - levels[h]) for h in every]
                inners = [
                    inners[h] + jnp.sum(pasts[h] * d_pasts[h], -1, keepdims=True) for h in every
                ]
            d_diags = [(diags[h] * (d_diags[h] - inners[h])).astype(LOW) for h in every]
            d_queries = [matmul(d_diags[h], k_ref[h, span, :]) for h in every]
            for h in every:
                dk_scr[h, span, :] = contract_rows(d_diags[h], queries_i[h])
                dv_scr[h, span, :] = contract_rows(diags[h].astype(LOW), d_atts[h])
            if i:
                d_pasts = [(pasts[h] * (d_pasts[h] - inners[h])).astype(LOW) for h in every]
                d_queries = [d_queries[h] + matmul(d_pasts[h], k_ref[h, done, :]) for h in every]
                for h in every:
                    dk_scr[h, done, :] += contract_rows(d_pasts[h], queries_i[h])
                    dv_scr[h, done, :] += contract_rows(pasts[h].astype(LOW), d_atts[h])
            for h in every:
                place_tile(0, span, h, unturn(d_queries[h] * 0.125, span))
        for i in range(4):
            span = slice(i * rows, (i + 1) * rows)
            for h in every:
                d_key = dk_scr[h, span, :]
                place_tile(1, span, h, unturn(d_key + pltpu.roll(d_key, 64, 1), span))
                place_tile(2, span, h, dv_scr[h, span, :])
        for m in range(3):
            grad = contract_rows(ain_ref[...], d_ref[m])
            for f in range(4):
                for e in range(groups):
                    start = f * block + e * strip
                    g_ref[4 * e + f, m] = grad[start : start + strip, :].astype(LOW)

    args = [ids, *branch, w_out, queries, keys, values, lse, ain, *tables]
    return run_kernel(
        body,
        [shape_of((3, length, block), LOW), shape_of((4 * groups, 3, strip, block), LOW)],
        args,
        specs=[SMEM] + [VMEM] * (len(args) - 1),
        scratch=[
            pltpu.VMEM((tiles, length, 128), LOW),
            pltpu.VMEM((heads, length, 128), WIDE),
            pltpu.VMEM((heads, length, 128), WIDE),
        ],
        flops=16 * 10**9,
        move=12 * 10**6,
    )


def late_grads(ids, d_qkv, own_mats, att_parts, branch):
    length, block = d_qkv.shape[1:]
    rows = length // 4
    width = own_mats.shape[1]
    extra = branch[0].shape[0] - rows

    def body(ids_ref, d_ref, w_ref, *refs):
        att_refs, br_refs = (refs[:4], refs[4:8])
        mine_ref, near_ref, mid_ref, gout_ref = refs[8:12]
        for k in range(4):
            span = pl.ds(ids_ref[1 + k] * rows, rows)
            total = contract_cols(d_ref[0, span, :], w_ref[0])
            for m in range(1, 3):
                total = total + contract_cols(d_ref[m, span, :], w_ref[m])
            if k % 2 == 0:
                target = mine_ref if k == 0 else mid_ref
                target[...] = total.astype(LOW)
            else:
                near_ref[k // 2] = total.astype(LOW)
        gout = contract_rows(att_refs[0][...], br_refs[0][0:rows, :])
        small = br_refs[0][rows:, :].astype(WIDE)
        for k in range(1, 4):
            gout = gout + contract_rows(att_refs[k][...], br_refs[k][0:rows, :])
            small = small + br_refs[k][rows:, :].astype(WIDE)
        gout_ref[0:block, :] = gout.astype(LOW)
        gout_ref[block:, :] = small.astype(LOW)

    args = [ids, d_qkv, own_mats, *att_parts, *branch]
    got = run_kernel(
        body,
        [
            shape_of((rows, width), LOW),
            shape_of((2, rows, width), LOW),
            shape_of((rows, width), LOW),
            shape_of((block + extra, width), LOW),
        ],
        args,
        specs=[SMEM] + [VMEM] * (len(args) - 1),
        flops=12 * 10**8,
        move=7 * 10**6,
    )
    return (got[:3], got[3])


def experts_chip(ids, rows_sent, got_dy, other, small, weights, peers, ready):
    width = rows_sent.shape[-1]
    axes = ("ep", "fx")
    own_rows = exchange(rows_sent, "ep").reshape(-1, width)
    own_rows = after(own_rows, *ready)
    din, hid, d_gate, d_up, dyw, weight, part = expert_main(
        ids, own_rows, got_dy, [*weights, *peers], other, small
    )

    def homeward(sent):
        return exchange(sent.reshape(EXPERTS, MOST, width), axes).reshape(-1, width)

    def middle(start):
        return expert_out(after(hid, start), weight, weights[2], peers[2])

    def give(start):
        return expert_weight_grads(after(own_rows, start), dyw, hid, d_gate, d_up, True)

    def outward(out):
        return exchange(out.reshape(EXPERTS // 2, 2, MOST, width), "ep")

    def finish(start, received):
        return expert_weight_grads(
            after(own_rows, start), dyw, hid, d_gate, d_up, False, received
        )

    return (din, part, homeward, middle, outward, give, finish)


def experts_spread(rows_sent, grads_sent, other, router_t, weights):
    ep_count = lax.axis_size("ep")
    weg, weu, wed = weights
    width = rows_sent.shape[1]
    local_count = max(1, EXPERTS // ep_count)
    replicas = max(1, ep_count // EXPERTS)
    groups = EXPERTS // local_count
    gate_cols, up_cols, down_rows = (
        lax.all_gather(weg, SEQ, axis=1, tiled=True),
        lax.all_gather(weu, SEQ, axis=1, tiled=True),
        lax.all_gather(wed, SEQ, axis=0, tiled=True),
    )
    hidden_part = gate_cols.shape[1] // local_count
    gate_local = gate_cols.reshape(width, local_count, hidden_part).transpose(1, 0, 2)
    up_local = up_cols.reshape(width, local_count, hidden_part).transpose(1, 0, 2)
    down_local = down_rows.reshape(local_count, hidden_part, width)

    def spread(buffer):
        last = buffer.shape[-1]
        wide = buffer.reshape(groups, 1, local_count * MOST, last)
        wide = jnp.broadcast_to(wide, (groups, replicas, local_count * MOST, last))
        return exchange(wide.reshape(ep_count, local_count * MOST, last), "ep")

    def collect(buffer):
        last = buffer.shape[-1]
        return jnp.sum(
            exchange(buffer, "ep").astype(WIDE).reshape(groups, replicas, local_count * MOST, last),
            1,
        ).reshape(EXPERTS * MOST, last)

    def owner_layout(received):
        last = received.shape[-1]
        return (
            received.reshape(ep_count, local_count, MOST, last)
            .transpose(1, 0, 2, 3)
            .reshape(local_count, ep_count * MOST, last)
        )

    def source_layout(owned):
        last = owned.shape[-1]
        return (
            owned.reshape(local_count, ep_count, MOST, last)
            .transpose(1, 0, 2, 3)
            .reshape(ep_count, local_count * MOST, last)
        )

    def batched(spec, left_op, right_op):
        return jnp.einsum(spec, left_op, right_op, preferred_element_type=WIDE)

    own_rows = owner_layout(spread(rows_sent))
    got_grads = owner_layout(spread(grads_sent))
    got_other = owner_layout(spread(other[:, None]))
    first = lax.axis_index("ep") // replicas * local_count
    mine = first + jnp.arange(local_count)[:, None, None]
    lane = jnp.arange(EXPERTS)
    logits = batched("lrd,ed->lre", own_rows, router_t)
    hit_mine, hit_other = ((lane == mine).astype(WIDE), (lane == got_other).astype(WIDE))
    got_weight = jax.nn.sigmoid(jnp.sum(logits * (hit_mine - hit_other), -1, keepdims=True))
    gate_val = batched("lrd,ldh->lrh", own_rows, gate_local)
    up_val = batched("lrd,ldh->lrh", own_rows, up_local)
    silu_val, slope_val = silu_grad(gate_val)
    hidden_val = (silu_val * up_val).astype(LOW)
    out_rows = batched("lrh,lhd->lrd", hidden_val, down_local)
    back_out = collect(source_layout((got_weight * out_rows).astype(LOW)))
    grad_hidden = batched("lrd,lhd->lrh", got_grads, down_local)
    row_dot = jnp.sum(hidden_val.astype(WIDE) * grad_hidden, -1, keepdims=True)
    amount = got_weight * (1.0 - got_weight) * row_dot
    d_logits = (amount * (hit_mine - hit_other)).astype(LOW)
    part = jnp.sum(batched("lre,lrd->led", d_logits, own_rows), 0)
    scaled = got_weight * grad_hidden
    own_grads = (got_weight * got_grads.astype(WIDE)).astype(LOW)
    grad_gate = (scaled * up_val * slope_val).astype(LOW)
    grad_up = (scaled * silu_val).astype(LOW)
    din_rows = batched("lrh,ldh->lrd", grad_gate, gate_local)
    din_rows = din_rows + batched("lrh,ldh->lrd", grad_up, up_local)
    din_rows = din_rows + batched("lre,ed->lrd", d_logits, router_t)
    back_din = collect(source_layout(din_rows.astype(LOW)))
    grad_gate_w = batched("lrd,lrh->ldh", own_rows, grad_gate)
    grad_up_w = batched("lrd,lrh->ldh", own_rows, grad_up)
    grad_down_w = batched("lrh,lrd->lhd", hidden_val, own_grads)

    def share(full, axis):
        return lax.psum_scatter(
            full.astype(LOW), SEQ, scatter_dimension=axis, tiled=True
        ).astype(WIDE)

    return (
        back_out.astype(LOW),
        back_din.astype(LOW),
        jnp.pad(part, ((0, EXTRA - EXPERTS), (0, 0))),
        lambda start: (
            share(grad_gate_w.transpose(1, 0, 2).reshape(width, local_count * hidden_part), 1),
            share(grad_up_w.transpose(1, 0, 2).reshape(width, local_count * hidden_part), 1),
            share(grad_down_w.reshape(local_count * hidden_part, width), 0),
        ),
    )


def shards(
    tokens,
    cotangent,
    routes,
    priority,
    gain_attn,
    w_query,
    w_key,
    w_value,
    w_out,
    gain_ffn,
    w_shared_gate,
    w_shared_up,
    w_shared_down,
    w_router,
    w_expert_gate,
    w_expert_up,
    w_expert_down,
):
    tok_rows, width = tokens.shape
    rows_w = w_query.shape[0]
    fs_count = lax.axis_size("fx") * lax.axis_size("fc")
    ep_count = lax.axis_size("ep")
    devices = ep_count * fs_count
    seq_len = tok_rows * fs_count
    head_size = width // HEADS
    side, core = (lax.axis_index("fx"), lax.axis_index("fc"))
    fs_index = side * lax.axis_size("fc") + core
    my_rank = lax.axis_index("ep") * fs_count + fs_index
    my_expert = lax.axis_index("ep") * lax.axis_size("fx") + side
    ids = [core] + [fs_index ^ k for k in range(4)] + [my_expert, lax.axis_index("ep"), side]
    ids = jnp.stack(ids).astype(jnp.int32)

    small_own = jnp.concatenate([w_router.T, gain_attn[None], gain_ffn[None]], 0)
    small_own = jnp.pad(small_own, ((0, EXTRA - EXPERTS - 2), (0, width - rows_w)))
    pack = jnp.concatenate([tokens, small_own])
    facts_far = far_of(jnp.concatenate([routes.T, priority[None]]))
    dy_far = far_of(cotangent)
    pack_far = far_of(after(pack, facts_far))
    qkv_stack = jnp.stack([w_query, w_key, w_value])
    qkv_cut = [
        lax.dynamic_slice_in_dim(qkv_stack, (fs_index ^ k) * rows_w, rows_w, 2) for k in range(4)
    ]

    def to_place(parts):
        got = [
            lax.ppermute(parts[k], SEQ, [(i, i ^ k) for i in range(fs_count)]) for k in (2, 3, 1)
        ]
        return (parts[0], got[2], got[0], got[1])

    w_parts = to_place(qkv_cut)
    x_parts = (pack, near_of(pack), pack_far, near_of(pack_far))

    lane = jnp.arange(2 * EXPERTS)
    zero_row = jnp.zeros((EXPERTS,), WIDE)
    lower = (jnp.arange(tok_rows)[:, None] > jnp.arange(tok_rows)[None, :]).astype(LOW)
    slot_iota = jnp.arange(EXPERTS * MOST)
    half_iota = jnp.arange(EXPERTS * MOST // 2)

    def plan(block_routes, block_priority):
        classes = jnp.stack([block_priority, 1 - block_priority], 1)
        named = block_routes + EXPERTS * classes
        hits = [(named[:, j : j + 1] == lane).astype(WIDE) for j in (0, 1)]
        both = hits[0] + hits[1]
        before = matmul(lower, both.astype(LOW))
        counts = jnp.sum(both, 0)
        local_table = before + jnp.concatenate([zero_row, counts[:EXPERTS]])
        ranks = [jnp.sum(local_table * hits[j], -1).astype(jnp.int32) for j in (0, 1)]
        return (hits, before, counts, ranks)

    def keep_of(block_plan, base):
        hits, before = block_plan[:2]
        capacity = 5 * tok_rows * devices // 32
        return [(jnp.sum((before + base) * hits[j], -1) < capacity).astype(LOW) for j in (0, 1)]

    def base_of(all_counts, rank):
        earlier = (jnp.arange(devices) < rank).astype(WIDE)
        base = jnp.sum(all_counts * earlier[:, None], 0)
        return base + jnp.concatenate([zero_row, jnp.sum(all_counts[:, :EXPERTS], 0)])

    own_plan = plan(routes, priority)
    counts, ranks = own_plan[2:]
    slot_hit = [
        ((routes[:, j] * MOST + ranks[j])[:, None] == slot_iota).astype(LOW) for j in (0, 1)
    ]
    dispatch = slot_hit[0] + slot_hit[1]
    others = jnp.stack([routes[:, 1], routes[:, 0]]).astype(LOW)
    other_sent = matmul(others[0:1], slot_hit[0]) + matmul(others[1:2], slot_hit[1])
    other_sent = other_sent.reshape(EXPERTS, MOST)
    pair_of_cores = EXPERTS == ep_count * lax.axis_size("fx")
    if pair_of_cores:
        tiny = jnp.concatenate(
            [jnp.broadcast_to(counts[None], (EXPERTS, 2 * EXPERTS)), other_sent], 1
        )
        tiny = jnp.pad(tiny, ((0, 0), (0, 128 - tiny.shape[1]))).astype(jnp.int32)
        tiny = jnp.broadcast_to(tiny[:, None], (EXPERTS, 2, 128)).reshape(devices, 1, 128)
        far_routes = facts_far[:2].T
        far_plan = plan(far_routes, facts_far[2])

        def side_hit(block_routes, block_ranks, j):
            place = (block_routes[:, j] >> 1) * MOST + block_ranks[j]
            same = (block_routes[:, j] & 1) == side
            return ((place[:, None] == half_iota) & same[:, None]).astype(LOW)

        own_side = [side_hit(routes, ranks, j) for j in (0, 1)]
        far_side = [side_hit(far_routes, far_plan[3], j) for j in (0, 1)]
        side_hits = (own_side[0] + own_side[1], far_side[0] + far_side[1])
        dy_sent = send_pair(ids, side_hits, (cotangent, dy_far))
        got_dy = exchange(dy_sent, "ep").reshape(-1, width)
        tiny_got = exchange(after(tiny, got_dy), ALL)
        all_counts = tiny_got[:, 0, : 2 * EXPERTS].astype(WIDE)
        other = lax.dynamic_index_in_dim(tiny_got.reshape(EXPERTS, 2, 128), core, 1, keepdims=False)
        other = other[:, 2 * EXPERTS : 2 * EXPERTS + MOST].reshape(EXPERTS * MOST, 1)
        far_keep = keep_of(far_plan, base_of(all_counts, my_rank ^ 2))
        own_keep = keep_of(own_plan, base_of(all_counts, my_rank))

        side_kept = (
            own_side[0] * own_keep[0][:, None] + own_side[1] * own_keep[1][:, None],
            far_side[0] * far_keep[0][:, None] + far_side[1] * far_keep[1][:, None],
        )
    else:
        spread_counts = jnp.broadcast_to(counts.astype(jnp.int32), (devices, 2 * EXPERTS))
        all_counts = exchange(spread_counts, ALL).astype(WIDE)
        kept = keep_of(own_plan, base_of(all_counts, my_rank))
        dispatch_kept = slot_hit[0] * kept[0][:, None] + slot_hit[1] * kept[1][:, None]

    forward_table, cos_table, sin_table = rope_constants(seq_len, head_size // 2)
    weights = (w_expert_gate, w_expert_up, w_expert_down)
    up_stack = jnp.stack([w_shared_gate, w_shared_up])
    ff_part = w_shared_gate.shape[1] // fs_count
    up_own = lax.dynamic_slice_in_dim(up_stack, side * 2 * ff_part, 2 * ff_part, 2)
    up_give = lax.dynamic_slice_in_dim(up_stack, (1 - side) * 2 * ff_part, 2 * ff_part, 2)

    def core_cut(piece, which):
        return lax.dynamic_slice_in_dim(piece, which * ff_part, ff_part, 2)

    up_mine, up_other = (core_cut(up_own, core), core_cut(up_own, 1 - core))
    ready = (*x_parts[1:], *w_parts[1:])
    out_far = far_of(after(w_out, *ready))
    out_near, dy_near = (near_of(piece) for piece in tie((w_out, cotangent), *ready))
    up_near = near_of(after(up_other, *ready))
    peers = []
    if pair_of_cores:
        peers = [near_of(piece) for piece in tie(weights, *ready)]
    ain, own_mats, (queries, keys, values), lse, att_own, small = attention_forward(
        ids, x_parts, w_parts, jnp.asarray(forward_table)
    )
    out_parts = (w_out, out_near, out_far, near_of(after(out_far, att_own[0])))
    att_parts = tie(to_place(att_own), *out_parts[1:])
    residual, ffn_input = after_attention(att_parts, out_parts, tokens, small)
    ffn_far = far_of(ffn_input)
    dy_parts = (cotangent, dy_near, dy_far, near_of(after(dy_far, ffn_far)))
    ffn_parts = (ffn_input, near_of(ffn_input), ffn_far, near_of(ffn_far))
    up_far = far_of(after(up_give, ffn_far))

    def shared():
        up_last = near_of(core_cut(up_far, 1 - core))
        up_parts = (up_mine, up_near, core_cut(up_far, core), up_last)
        return shared_branch(
            ids,
            ffn_parts,
            dy_parts,
            up_parts,
            w_shared_down,
            ep_count if pair_of_cores else 0,
        )

    def fold(parts):
        mine, give, mid = parts
        got = near_of(give)
        return (mine, got, far_of((mid.astype(WIDE) + got[1].astype(WIDE)).astype(LOW)))

    def ep_step(block, bit):
        return lax.ppermute(block, "ep", [(i, i ^ bit) for i in range(ep_count)])

    def added(first, second):
        return (first.astype(WIDE) + second.astype(WIDE)).astype(LOW)

    if pair_of_cores:
        got_dy = after(got_dy, *peers)
        rows_sent = send_pair(ids, tie(side_kept, got_dy), (ffn_input, ffn_far))
        din_sums, out_sums, (grads_keep, grads_give) = shared()
        grads_got = ep_step(grads_give, 2)
        din_sent, router_part, homeward, middle, outward, give_grads, last = experts_chip(
            ids, rows_sent, got_dy, other, small, weights, peers, (grads_keep,)
        )
        din_fold = fold(din_sums)
        half = added(grads_keep, after(grads_got, din_sent))
        back_din = homeward(after(din_sent, half))
        half_got = ep_step(half[1::2], 1)
        expert_out_rows = middle(half)
        out_near_sum = near_of(after(out_sums[1], half))
        back_din = after(back_din, out_near_sum)
        back_din = after(back_din, half_got)
        quarter = added(half[0::2], half_got)
        quarter_got = ep_step(quarter[1:2], 4)
    else:
        dy_sent = contract_rows(dispatch, cotangent).astype(LOW)
        rows_sent = contract_rows(dispatch_kept, ffn_input).astype(LOW)
        back_out, back_din, router_part, expert_grads = experts_spread(
            rows_sent, dy_sent, other_sent.reshape(-1), small[:EXPERTS], weights
        )
        din_sums, out_sums, grads_rest = shared()
        din_fold = fold(din_sums)

    grad_resid, branch = back_at_tokens(
        din_fold, back_din, dispatch, residual, small, cotangent, router_part
    )
    branch_far = far_of(branch)
    branch_pair = (branch, branch_far)
    if pair_of_cores:
        own_chunk = added(quarter[0:1], after(quarter_got, branch))
        branch_pair = tie(branch_pair, own_chunk)
        back_out = outward(after(expert_out_rows, own_chunk, branch_far))
    branch_near, branch_last = (near_of(piece) for piece in branch_pair)
    branch_parts = (branch, branch_near, branch_far, branch_last)
    d_qkv, grads_qkv = attention_backward(
        ids, branch_parts, w_out, queries, keys, values, lse, ain, (cos_table, sin_table), ep_count if pair_of_cores else 1
    )
    strip = rows_w // ep_count
    grads_qkv = after(grads_qkv, back_out)
    if pair_of_cores:
        qkv_blocks = grads_qkv
    else:
        qkv_blocks = grads_qkv.transpose(1, 0, 2, 3).reshape(3, fs_count, ep_count, strip, rows_w)
        qkv_blocks = qkv_blocks.transpose(2, 1, 0, 3, 4).reshape(devices, 3, strip, rows_w)
    qkv_got = exchange(qkv_blocks, ALL)
    din_parts, grad_out_w = late_grads(ids, d_qkv, own_mats, att_own, branch_parts)
    in_fold = fold(din_parts)
    own_float = tokens.astype(WIDE)
    grad_in = in_fold[0].astype(WIDE) + in_fold[1][0].astype(WIDE) + in_fold[2].astype(WIDE)
    gain_one = small[EXPERTS : EXPERTS + 1].astype(WIDE)
    grad_tokens = grad_resid + rms_backward(grad_in, own_float, inverse_rms(own_float), gain_one)

    if not pair_of_cores:
        out_fold = fold(out_sums)
        total = residual + out_fold[0].astype(WIDE) + out_fold[1][0].astype(WIDE)
        total = total + out_fold[2].astype(WIDE) + matmul(dispatch, back_out)
        output = total.astype(LOW)
    qkv_got = qkv_got.reshape(ep_count, fs_count, 3, strip, rows_w).astype(WIDE)
    qkv_sum = jnp.sum(qkv_got, 0).transpose(1, 2, 0, 3).reshape(3 * strip, width).astype(LOW)
    small_part = lax.dynamic_slice_in_dim(grad_out_w[rows_w:], fs_index * rows_w, rows_w, 1)
    if pair_of_cores:
        lines = EXTRA * rows_w // (ep_count * width)
        parts = jnp.concatenate(
            [
                grad_out_w[:rows_w].reshape(ep_count, strip, width),
                small_part.reshape(ep_count, lines, width),
            ],
            1,
        )
        cut = 2 * rows_w // ep_count
        turned = to_place([own_chunk[0, k * cut : (k + 1) * cut] for k in range(4)])
        whole = jnp.concatenate([*turned, own_chunk[0, 4 * cut :]])[None]
        for bit, far_bit in ((1, 4), (2, 2)):
            keep, give = split_part(parts, bit)
            got, whole_got = (ep_step(give, bit), ep_step(whole, far_bit))
            if bit == 1:
                got, whole_got, in_last = lax.optimization_barrier((got, whole_got, in_fold[2]))
                own_total, far_total = take_pair(
                    ids, side_hits, after(back_out, got), out_sums, out_near_sum, residual
                )
                out_got = far_of(far_total)
            else:
                got, whole_got, out_got = lax.optimization_barrier((got, whole_got, out_got))
            parts = added(keep, got)
            whole = jnp.concatenate([whole, whole_got])
        keep, give = split_part(parts, 4)
        whole_got = ep_step(whole, 1)
        out_sum = added(keep, ep_step(give, 4))[0]
        output = (own_total + out_got.astype(WIDE)).astype(LOW)
    else:
        lines = 0
        out_whole = lax.psum((grad_out_w[:rows_w], small_part), "ep")
        out_sum = jnp.zeros((0, width), LOW)
    sums = jnp.concatenate([qkv_sum, out_sum])
    sums_sent = jnp.broadcast_to(sums[None], (ep_count,) + sums.shape)
    sums = exchange(sums_sent, "ep")
    mats = (w_query, w_key, w_value)
    if pair_of_cores:
        *qkv_all, sum_out_w, gain_col = place_dense(sums, mats, gain_attn[:, None], strip)
        sum_gain_one = gain_col[:, 0]
        sum_small = sums[:, 4 * strip : 4 * strip + lines].astype(WIDE).reshape(EXTRA, rows_w)
    else:
        sums = sums.astype(WIDE)
        qkv_all = sums.reshape(ep_count, 3, strip, width)
        qkv_all = qkv_all.transpose(1, 0, 2, 3).reshape(3, rows_w, width)
        sum_out_w, sum_small = (piece.astype(WIDE) for piece in out_whole)
        sum_gain_one = sum(
            jnp.sum(qkv_all[i] * mat.astype(WIDE), -1) for i, mat in enumerate(mats)
        )
        sum_gain_one = sum_gain_one / gain_attn.astype(WIDE)
    sum_router, sum_gain_two = (sum_small[:EXPERTS].T, sum_small[EXPERTS])
    if pair_of_cores:
        whole_got, *given = lax.optimization_barrier((whole_got, *give_grads(sums_sent)))
        expert_grads = last(qkv_blocks, [near_of(piece) for piece in given])
        whole = [whole, whole_got]
        sum_sgate, sum_sup, sum_sdown = place_shared(ids, whole, rows_w, width)
    else:
        expert_grads = expert_grads(grads_qkv)
        dense = lax.psum((*to_place(grads_rest[:4]), grads_rest[4]), "ep")
        sum_sdown = dense[4].astype(WIDE)
        wide_rel = jnp.stack([piece.astype(WIDE) for piece in dense[:4]])
        wide_all = jnp.concatenate(
            [
                lax.dynamic_index_in_dim(wide_rel, fs_index ^ k, 0, keepdims=False)
                for k in range(4)
            ],
            2,
        )
        sum_sgate, sum_sup = (wide_all[0], wide_all[1])
    return (
        output,
        grad_tokens,
        sum_gain_one,
        qkv_all[0],
        qkv_all[1],
        qkv_all[2],
        sum_out_w,
        sum_gain_two,
        sum_sgate,
        sum_sup,
        sum_sdown,
        sum_router,
        *expert_grads,
    )


def solution(mesh):
    ep_count, fs_count = mesh.devices.shape
    cut_mesh = Mesh(mesh.devices.reshape(ep_count, fs_count // 2, 2), ALL)
    tok = P(ALL, None)
    row = P(SEQ, None)
    return jax.shard_map(
        shards,
        mesh=cut_mesh,
        in_specs=(
            tok,
            tok,
            tok,
            P(ALL),
            P(SEQ),
            row,
            row,
            row,
            row,
            P(SEQ),
            row,
            row,
            row,
            row,
            P(None, ALL),
            P(None, ALL),
            tok,
        ),
        out_specs=(
            tok,
            tok,
            P(SEQ),
            row,
            row,
            row,
            row,
            P(SEQ),
            row,
            row,
            row,
            row,
            P(None, ALL),
            P(None, ALL),
            tok,
        ),
        check_vma=False,
    )
```

```python
import jax
import jax.numpy as jnp
import numpy as np
from jax import lax
from jax.experimental import pallas as pl
from jax.experimental.pallas import tpu as pltpu
from jax.sharding import Mesh
from jax.sharding import PartitionSpec as P

HEADS = 12
EXPERTS = 16
MOST = 48
EXTRA = 2 * EXPERTS
LIGHT = 20

EPS = 1e-06
NEG = -1e30
LOW = jnp.bfloat16
WIDE = jnp.float32
ALL = ("ep", "fx", "fc")
SEQ = ("fx", "fc")
SWAP = [(0, 1), (1, 0)]
VMEM = pl.BlockSpec(memory_space=pltpu.VMEM)
SMEM = pl.BlockSpec(memory_space=pltpu.SMEM)


def matmul(left_op, right_op):
    return jnp.dot(left_op, right_op, preferred_element_type=WIDE)


def contract_rows(left_op, right_op):
    return lax.dot_general(left_op, right_op, (((0,), (0,)), ((), ())), preferred_element_type=WIDE)


def contract_cols(left_op, right_op):
    return lax.dot_general(left_op, right_op, (((1,), (1,)), ((), ())), preferred_element_type=WIDE)


def inverse_rms(values):
    return lax.rsqrt(jnp.mean(values * values, -1, keepdims=True) + EPS)


def rms_backward(upstream, values, inverse, gain_vec):
    scaled = upstream * gain_vec
    return inverse * scaled - values * inverse**3 * jnp.mean(scaled * values, -1, keepdims=True)


def silu_grad(gate_val):
    sigma = jax.nn.sigmoid(gate_val)
    return (gate_val * sigma, sigma * (1.0 + gate_val * (1.0 - sigma)))


def far_of(block):
    return lax.ppermute(block, "fx", SWAP)


def near_of(block):
    return lax.ppermute(block, "fc", SWAP)


def after(value, *others):
    return lax.optimization_barrier((value, *others))[0]


def tie(values, *others):
    return lax.optimization_barrier((*values, *others))[: len(values)]


def exchange(blocks, axes):
    return lax.all_to_all(blocks, axes, split_axis=0, concat_axis=0, tiled=True)


def split_part(parts, bit):
    cut = parts.reshape((parts.shape[0] // 2, 2) + parts.shape[1:])
    mine = lax.rem(lax.axis_index("ep") // bit, 2)
    keep = lax.dynamic_index_in_dim(cut, mine, 1, keepdims=False)
    return (keep, lax.dynamic_index_in_dim(cut, 1 - mine, 1, keepdims=False))


def shape_of(dims, kind):
    return jax.ShapeDtypeStruct(dims, kind)


def run_kernel(body, outs, args, specs=None, out_specs=None, scratch=(), grid=None, flops=0, move=0):
    options = {} if grid is None else {"grid": grid}
    return pl.pallas_call(
        body,
        out_shape=outs,
        in_specs=specs if specs is not None else [VMEM] * len(args),
        out_specs=out_specs if out_specs is not None else [VMEM] * len(outs),
        scratch_shapes=list(scratch),
        compiler_params=pltpu.CompilerParams(vmem_limit_bytes=52 * 2**20),
        cost_estimate=pl.CostEstimate(
            flops=flops // LIGHT, bytes_accessed=move // LIGHT, transcendentals=0
        ),
        **options,
    )(*args)


def pick_rows(first_iota, second_iota, source):
    return (first_iota == source(second_iota)).astype(LOW)


def rope_constants(length, half):
    freq = np.exp(-np.log(np.float32(10000.0)) * np.arange(half, dtype=np.float32) / np.float32(half))
    angle = np.arange(length, dtype=np.float32)[:, None] * freq.astype(np.float32)[None, :]
    cosine, sine = (np.cos(angle), np.sin(angle))
    return (
        np.concatenate([cosine, cosine, sine, sine], 1).astype(np.float32),
        np.concatenate([cosine] * 4, 1).astype(np.float32),
        np.concatenate([sine, -sine, sine, -sine], 1).astype(np.float32),
    )


def attention_forward(ids, x_parts, w_parts, table):
    full, width = x_parts[0].shape
    rows = full - EXTRA
    block = w_parts[0].shape[1]
    length = 4 * rows
    heads = block // 64
    size = heads * 128

    def body(ids_ref, *refs):
        x_refs, w_refs, table_ref = (refs[:4], refs[4:8], refs[8])
        ain_ref, own_ref, q_ref, k_ref, v_ref, lse_ref = refs[9:15]
        att_refs, small_ref = (refs[15:19], refs[19])
        att_scr = refs[20]
        first = lax.broadcasted_iota(jnp.int32, (block, width), 0)
        lane = lax.broadcasted_iota(jnp.int32, (block, width), 1)
        small = jnp.zeros((EXTRA, width), WIDE)
        for k in range(4):
            place = jnp.where(lane == first + ids_ref[1 + k] * block, 1.0, 0.0).astype(LOW)
            small = small + matmul(x_refs[k][rows:, :block], place)
        small_ref[...] = small.astype(LOW)
        gain = small[EXPERTS : EXPERTS + 1, :]
        for k in range(4):
            place = ids_ref[1 + k]
            piece = x_refs[k][:rows, :].astype(WIDE)
            ain_ref[pl.ds(place * rows, rows), :] = (piece * inverse_rms(piece) * gain).astype(LOW)
            for m in range(3):
                own_ref[m, pl.ds(place * block, block), :] = w_refs[k][m]
        first = lax.broadcasted_iota(jnp.int32, (block, size), 0)
        lane = lax.broadcasted_iota(jnp.int32, (block, size), 1)
        head, inner = (lane // 128, lane % 128)
        low = inner % 64
        swapped = jnp.where(low < 32, low + 32, low - 32)
        source = 64 * head + jnp.where(inner < 64, low, swapped)
        sign = jnp.where((inner >= 64) & (low < 32), -1.0, 1.0)
        turn = jnp.where(first == source, sign, 0.0).astype(LOW)
        keep = (inner // 64 == head % 2) & (first == 64 * head + low)
        place_v = jnp.where(keep, 1.0, 0.0).astype(LOW)
        w_q = matmul(own_ref[0], turn).astype(LOW)
        w_k = matmul(own_ref[1], turn).astype(LOW)
        w_v = matmul(own_ref[2], place_v).astype(LOW)
        half = lax.broadcasted_iota(jnp.int32, (rows, 128), 1) < 64
        for i in range(4):
            span = slice(i * rows, (i + 1) * rows)
            ain = ain_ref[span, :]
            y_q, y_k, y_v = (matmul(ain, w_q), matmul(ain, w_k), matmul(ain, w_v))
            tab = table_ref[span, :]
            for h in range(heads):
                cols = slice(128 * h, 128 * h + 128)
                turned = y_q[:, cols] * tab
                turned = (turned + pltpu.roll(turned, 64, 1)).astype(LOW).astype(WIDE)
                q_ref[h, span, :] = jnp.where(half, turned * 0.125, 0.0).astype(LOW)
                turned = y_k[:, cols] * tab
                k_ref[h, span, :] = (turned + pltpu.roll(turned, 64, 1)).astype(LOW)
                v_ref[h, span, :] = y_v[:, cols].astype(LOW)
        tri = lax.broadcasted_iota(jnp.int32, (rows, rows), 0) >= lax.broadcasted_iota(
            jnp.int32, (rows, rows), 1
        )
        for i in range(4):
            span = slice(i * rows, (i + 1) * rows)
            done = slice(0, i * rows)
            every = range(heads)
            diags = [
                jnp.where(tri, contract_cols(q_ref[h, span, :], k_ref[h, span, :]), NEG)
                for h in every
            ]
            tops = [jnp.max(diag, -1, keepdims=True) for diag in diags]
            if i:
                pasts = [contract_cols(q_ref[h, span, :], k_ref[h, done, :]) for h in every]
                tops = [
                    jnp.maximum(tops[h], jnp.max(pasts[h], -1, keepdims=True)) for h in every
                ]
                pasts = [jnp.exp(pasts[h] - tops[h]) for h in every]
            diags = [jnp.exp(diags[h] - tops[h]) for h in every]
            totals = [jnp.sum(diag, -1, keepdims=True) for diag in diags]
            if i:
                totals = [totals[h] + jnp.sum(pasts[h], -1, keepdims=True) for h in every]
            scales = [1.0 / total for total in totals]
            tiles = [
                matmul((diags[h] * scales[h]).astype(LOW), v_ref[h, span, :]) for h in every
            ]
            if i:
                tiles = [
                    tiles[h] + matmul((pasts[h] * scales[h]).astype(LOW), v_ref[h, done, :])
                    for h in every
                ]
            for h in every:
                lse_ref[h, span, :] = tops[h] + jnp.log(totals[h])
            for t in range((heads + 1) // 2):
                pair = tiles[2 * t] + (tiles[2 * t + 1] if 2 * t + 1 < heads else 0.0)
                wide = min(128, block - 128 * t)
                att_scr[span, 128 * t : 128 * t + wide] = pair[:, :wide].astype(LOW)
        for k in range(4):
            att_refs[k][...] = att_scr[pl.ds(ids_ref[1 + k] * rows, rows), :]

    outs = (
        [shape_of((length, width), LOW), shape_of((3, width, block), LOW)]
        + [shape_of((heads, length, 128), LOW)] * 3
        + [shape_of((heads, length, 1), WIDE)]
        + [shape_of((rows, block), LOW)] * 4
        + [shape_of((EXTRA, width), LOW)]
    )
    args = [ids, *x_parts, *w_parts, table]
    got = run_kernel(
        body,
        outs,
        args,
        specs=[SMEM] + [VMEM] * (len(args) - 1),
        scratch=[pltpu.VMEM((length, block), LOW)],
        flops=8 * 10**9,
        move=12 * 10**6,
    )
    return (got[0], got[1], got[2:5], got[5], got[6:10], got[10])


def after_attention(att_parts, out_parts, tokens, small):
    rows, width = tokens.shape

    def body(*refs):
        att_refs, out_refs = (refs[:4], refs[4:8])
        tok_ref, small_ref, res_ref, ffn_ref = refs[8:]
        total = tok_ref[...].astype(WIDE)
        for k in range(4):
            total = total + matmul(att_refs[k][...], out_refs[k][...])
        res_ref[...] = total
        gain = small_ref[EXPERTS + 1 : EXPERTS + 2, :].astype(WIDE)
        ffn_ref[...] = (total * inverse_rms(total) * gain).astype(LOW)

    outs = [shape_of((rows, width), WIDE), shape_of((rows, width), LOW)]
    args = [*att_parts, *out_parts, tokens, small]
    return run_kernel(body, outs, args, flops=6 * 10**8, move=4 * 10**6)


def send_pair(ids, hits, blocks):
    rows, width = blocks[0].shape
    groups = hits[0].shape[1] // MOST

    def body(ids_ref, own_hit, far_hit, own_ref, far_ref, out_ref):
        for hit, block, place in (
            (own_hit, own_ref, ids_ref[7]),
            (far_hit, far_ref, 1 - ids_ref[7]),
        ):
            sent = contract_rows(hit[...], block[...]).astype(LOW)
            for g in range(groups):
                out_ref[g, place] = sent[g * MOST : (g + 1) * MOST, :]

    return run_kernel(
        body,
        [shape_of((groups, 2, MOST, width), LOW)],
        [ids, *hits, *blocks],
        specs=[SMEM] + [VMEM] * 4,
        flops=6 * 10**8,
        move=3 * 10**6,
    )[0]


def take_pair(ids, hits, back, sums, near_sum, residual):
    groups, _, _, width = back.shape
    rows = residual.shape[0]

    def body(ids_ref, own_hit, far_hit, back_ref, mine_ref, mid_ref, near_ref, res_ref, own_out, far_out):
        own = res_ref[...] + mine_ref[...].astype(WIDE) + near_ref[0].astype(WIDE)
        far = mid_ref[...].astype(WIDE) + near_ref[1].astype(WIDE)
        for g in range(groups):
            cols = slice(g * MOST, (g + 1) * MOST)
            own = own + matmul(own_hit[:, cols], back_ref[g, ids_ref[7]])
            far = far + matmul(far_hit[:, cols], back_ref[g, 1 - ids_ref[7]])
        own_out[...] = own
        far_out[...] = far.astype(LOW)

    return run_kernel(
        body,
        [shape_of((rows, width), WIDE), shape_of((rows, width), LOW)],
        [ids, *hits, back, sums[0], sums[2], near_sum, residual],
        specs=[SMEM] + [VMEM] * 7,
        flops=6 * 10**8,
        move=5 * 10**6,
    )


def shared_branch(ids, ffn_parts, dy_parts, w_parts, down, chunks):
    rows, width = ffn_parts[0].shape
    block, hidden = w_parts[0].shape[1:]

    def body(ids_ref, *refs):
        ffn_refs, dy_refs, w_refs = (refs[:4], refs[4:8], refs[8:12])
        down_ref = refs[12]
        sum_refs, grad_refs = (refs[13:19], refs[19:-3])
        w_scr, g_scr, d_scr = refs[-3:]
        for k in range(4):
            for m in range(2):
                w_scr[m, pl.ds(ids_ref[1 + k] * block, block), :] = w_refs[k][m]
        for k in range(4):
            ffn, dy = (ffn_refs[k][...], dy_refs[k][...])
            gate, up = (matmul(ffn, w_scr[0]), matmul(ffn, w_scr[1]))
            silu, slope = silu_grad(gate)
            hid = (silu * up).astype(LOW)
            back = contract_cols(dy, down_ref[...])
            d_gate = (back * up * slope).astype(LOW)
            d_up = (back * silu).astype(LOW)
            din = (contract_cols(d_gate, w_scr[0]) + contract_cols(d_up, w_scr[1])).astype(LOW)
            out = matmul(hid, down_ref[...]).astype(LOW)
            for n, value in enumerate((din, out)):
                mine_ref, near_ref, mid_ref = sum_refs[3 * n : 3 * n + 3]
                if k % 2 == 0:
                    target = mine_ref if k == 0 else mid_ref
                    target[...] = value
                else:
                    near_ref[k // 2] = value
            parts = (contract_rows(ffn, d_gate), contract_rows(ffn, d_up), contract_rows(hid, dy))
            if k == 0:
                g_scr[0], g_scr[1], d_scr[...] = parts
            else:
                g_scr[0] += parts[0]
                g_scr[1] += parts[1]
                d_scr[...] += parts[2]
        if chunks:
            per = chunks // 2
            cut, line = (block // per, hidden // chunks)
            for r in range(chunks):
                part = ids_ref[6] ^ r
                target, slot = (grad_refs[(r >> 1) & 1], (r & 1) + 2 * (r >> 2))
                which, low = (part // per, part % per)
                for k in range(4):
                    start = ids_ref[1 + k] * block + low * cut
                    target[slot, k * cut : (k + 1) * cut, :] = g_scr[
                        which, pl.ds(pl.multiple_of(start, 16), cut), :
                    ].astype(LOW)
                start = pl.multiple_of(part * line, 16)
                piece = d_scr[pl.ds(start, line), :].astype(LOW)
                base = 4 * cut
                target[slot, base : base + line, :] = piece[:, :hidden]
                target[slot, base + line :, : hidden // 2] = piece[: line // 2, hidden:]
                target[slot, base + line :, hidden // 2 :] = piece[line // 2 :, hidden:]
        else:
            for k in range(4):
                for m in range(2):
                    grad_refs[k][m] = g_scr[m, pl.ds(ids_ref[1 + k] * block, block), :].astype(LOW)
            grad_refs[4][...] = d_scr[...].astype(LOW)

    if chunks:
        lines = 4 * block * 2 // chunks + 3 * hidden // chunks // 2
        grad_outs = [shape_of((chunks // 2, lines, hidden), LOW)] * 2
    else:
        grad_outs = [shape_of((2, block, hidden), LOW)] * 4 + [shape_of((hidden, width), LOW)]
    sums = [shape_of((rows, width), LOW), shape_of((2, rows, width), LOW), shape_of((rows, width), LOW)]
    outs = sums * 2 + grad_outs
    args = [ids, *ffn_parts, *dy_parts, *w_parts, down]
    got = run_kernel(
        body,
        outs,
        args,
        specs=[SMEM] + [VMEM] * (len(args) - 1),
        scratch=[
            pltpu.VMEM((2, width, hidden), LOW),
            pltpu.VMEM((2, width, hidden), WIDE),
            pltpu.VMEM((hidden, width), WIDE),
        ],
        flops=7 * 10**9,
        move=14 * 10**6,
    )
    return (got[0:3], got[3:6], got[6:])


def place_shared(ids, groups, block, width):
    per_group, lines, hidden = groups[0].shape
    chunks = per_group * len(groups)
    per = chunks // 2
    cut, line = (block // per, hidden // chunks)
    order = (0, 4, 2, 6, 1, 5, 3, 7)

    def body(ids_ref, *refs):
        gate_ref, up_ref, down_ref = refs[-3:]
        for n in range(chunks):
            part = ids_ref[6] ^ order[n]
            which, low = (part // per, part % per)
            piece = refs[n // per_group][n % per_group].astype(WIDE)
            for k in range(4):
                lane = pl.multiple_of(ids_ref[1 + k] * hidden, 128)
                value = piece[k * cut : (k + 1) * cut, :]
                place = (pl.ds(pl.multiple_of(low * cut, 16), cut), pl.ds(lane, hidden))

                @pl.when(which == 0)
                def to_gate(place=place, value=value):
                    gate_ref[place] = value

                @pl.when(which == 1)
                def to_up(place=place, value=value):
                    up_ref[place] = value

            base = 4 * cut
            start = pl.multiple_of(part * line, 16)
            down_ref[pl.ds(start, line), :hidden] = piece[base : base + line, :]
            tail = piece[base + line :, :]
            down_ref[pl.ds(start, line // 2), hidden:] = tail[:, : hidden // 2]
            down_ref[pl.ds(start + line // 2, line // 2), hidden:] = tail[:, hidden // 2 :]

    return run_kernel(
        body,
        [shape_of((block, 4 * hidden), WIDE)] * 2 + [shape_of((hidden, width), WIDE)],
        [ids, *groups],
        specs=[SMEM] + [VMEM] * len(groups),
        move=8 * 10**6,
    )


def place_dense(sums, w_parts, gain, strip):
    parts, lines, width = sums.shape
    block = parts * strip

    def body(sums_ref, a_ref, b_ref, c_ref, gain_ref, *outs):
        for p in range(parts):
            piece = sums_ref[p].astype(WIDE)
            for m in range(4):
                outs[m][p * strip : (p + 1) * strip, :] = piece[m * strip : (m + 1) * strip, :]
        gain_sum = jnp.zeros((block, 1), WIDE)
        for m, w_ref in enumerate((a_ref, b_ref, c_ref)):
            gain_sum = gain_sum + jnp.sum(outs[m][...] * w_ref[...].astype(WIDE), -1, keepdims=True)
        outs[4][...] = gain_sum / gain_ref[...].astype(WIDE)

    return run_kernel(
        body,
        [shape_of((block, width), WIDE)] * 4 + [shape_of((block, 1), WIDE)],
        [sums, *w_parts, gain],
        move=5 * 10**6,
    )


def expert_main(ids, rows_in, dy_in, mats, other, router_t):
    count, width = rows_in.shape
    own_hidden = mats[0].shape[1]
    tile = 512
    steps = 2 * own_hidden // tile
    half = steps // 2
    chunk = 256

    def body(ids_ref, rows_ref, dy_ref, *refs):
        own, peer = (refs[0:3], refs[3:6])
        other_ref, router_ref = refs[6:8]
        din_ref, hid_ref, dg_ref, du_ref, dyw_ref, w_ref, part_ref = refs[8:15]
        acc, dot_scr = refs[15:17]
        step = pl.program_id(0)
        expert = ids_ref[5]

        @pl.when(step == 0)
        def start():
            for r in range(0, count, chunk):
                span = slice(r, r + chunk)
                logits = contract_cols(rows_ref[span, :], router_ref[...])
                lane = lax.broadcasted_iota(jnp.int32, logits.shape, 1)
                mine = jnp.sum(jnp.where(lane == expert, logits, 0.0), -1, keepdims=True)
                rest = jnp.sum(jnp.where(lane == other_ref[span, :], logits, 0.0), -1, keepdims=True)
                weight = jax.nn.sigmoid(mine - rest)
                w_ref[span, :] = weight
                dyw_ref[span, :] = (weight * dy_ref[span, :].astype(WIDE)).astype(LOW)
                dot_scr[span, :] = jnp.zeros((chunk, 1), WIDE)
                acc[span, :] = jnp.zeros((chunk, width), WIDE)

        def work(gate_ref, up_ref, down_ref):
            for r in range(0, count, chunk):
                span = slice(r, r + chunk)
                rows = rows_ref[span, :]
                gate, up = (matmul(rows, gate_ref[...]), matmul(rows, up_ref[...]))
                back = contract_cols(dy_ref[span, :], down_ref[...])
                silu, slope = silu_grad(gate)
                hid = (silu * up).astype(LOW)
                hid_ref[span, :] = hid
                dot_scr[span, :] += jnp.sum(hid.astype(WIDE) * back, -1, keepdims=True)
                scaled = w_ref[span, :] * back
                d_gate = (scaled * up * slope).astype(LOW)
                d_up = (scaled * silu).astype(LOW)
                dg_ref[span, :] = d_gate
                du_ref[span, :] = d_up
                acc[span, :] += contract_cols(d_gate, gate_ref[...]) + contract_cols(
                    d_up, up_ref[...]
                )

        @pl.when(step < half)
        def first():
            work(*own)

        @pl.when(step >= half)
        def second():
            work(*peer)

        @pl.when(step == steps - 1)
        def finish():
            for r in range(0, count, chunk):
                span = slice(r, r + chunk)
                weight = w_ref[span, :]
                amount = weight * (1.0 - weight) * dot_scr[span, :]
                lane = lax.broadcasted_iota(jnp.int32, (chunk, EXTRA), 1)
                signs = jnp.where(lane == expert, 1.0, 0.0) - jnp.where(
                    lane == other_ref[span, :], 1.0, 0.0
                )
                d_logit = (amount * signs).astype(LOW)
                din_ref[span, :] = (acc[span, :] + matmul(d_logit, router_ref[...])).astype(LOW)
                part = contract_rows(d_logit, rows_ref[span, :])
                part_ref[...] = part if r == 0 else part_ref[...] + part

    def fixed(dims):
        return pl.BlockSpec(dims, lambda j: (0,) * len(dims))

    def near(j):
        return jnp.minimum(j, half - 1)

    def late(j):
        return jnp.maximum(j - half, 0)

    cols = (width, tile)
    specs = [SMEM, fixed((count, width)), fixed((count, width))]
    for place in (near, late):
        specs += [
            pl.BlockSpec(cols, lambda j, place=place: (0, place(j))),
            pl.BlockSpec(cols, lambda j, place=place: (0, place(j))),
            pl.BlockSpec((tile, width), lambda j, place=place: (place(j), 0)),
        ]
    specs += [fixed((count, 1)), fixed(router_t.shape)]
    tiles = pl.BlockSpec((count, tile), lambda j: (0, j))
    outs = (
        [shape_of((count, width), LOW)]
        + [shape_of((count, 2 * own_hidden), LOW)] * 3
        + [shape_of((count, width), LOW), shape_of((count, 1), WIDE), shape_of(router_t.shape, WIDE)]
    )
    out_specs = [
        fixed((count, width)),
        tiles,
        tiles,
        tiles,
        fixed((count, width)),
        fixed((count, 1)),
        fixed(router_t.shape),
    ]
    return run_kernel(
        body,
        outs,
        [ids, rows_in, dy_in, *mats, other, router_t],
        specs=specs,
        out_specs=out_specs,
        scratch=[pltpu.VMEM((count, width), WIDE), pltpu.VMEM((count, 1), WIDE)],
        grid=(steps,),
        flops=12 * 10**9,
        move=22 * 10**6,
    )


def expert_out(hid, weight, down_own, down_peer):
    count, hidden = hid.shape
    width = down_own.shape[1]
    half = hidden // 2
    chunk = 256

    def body(hid_ref, w_ref, own_ref, peer_ref, out_ref):
        for r in range(0, count, chunk):
            span = slice(r, r + chunk)
            total = matmul(hid_ref[span, :half], own_ref[...])
            total = total + matmul(hid_ref[span, half:], peer_ref[...])
            out_ref[span, :] = (w_ref[span, :] * total).astype(LOW)

    return run_kernel(
        body,
        [shape_of((count, width), LOW)],
        [hid, weight, down_own, down_peer],
        flops=2 * 10**9,
        move=8 * 10**6,
    )[0]


def expert_weight_grads(rows_in, dyw, hid, d_gate, d_up, peer, add=None):
    count, width = rows_in.shape
    half = hid.shape[1] // 2
    tile = 512
    steps = half // tile
    offset = steps if peer else 0
    kind = LOW if add is None else WIDE

    def body(rows_ref, dyw_ref, hid_ref, dg_ref, du_ref, *refs):
        outs = refs[-3:]
        grads = (
            contract_rows(rows_ref[...], dg_ref[...]),
            contract_rows(rows_ref[...], du_ref[...]),
            contract_rows(hid_ref[...], dyw_ref[...]),
        )
        for i in range(3):
            value = grads[i] if add is None else grads[i] + refs[i][...].astype(WIDE)
            outs[i][...] = value.astype(kind)

    def fixed(dims):
        return pl.BlockSpec(dims, lambda j: (0,) * len(dims))

    tiles = pl.BlockSpec((count, tile), lambda j: (0, j + offset))
    cols = pl.BlockSpec((width, tile), lambda j: (0, j))
    lines = pl.BlockSpec((tile, width), lambda j: (j, 0))
    specs = [fixed((count, width)), fixed((count, width)), tiles, tiles, tiles]
    extra = [] if add is None else list(add)
    return run_kernel(
        body,
        [shape_of((width, half), kind), shape_of((width, half), kind), shape_of((half, width), kind)],
        [rows_in, dyw, hid, d_gate, d_up, *extra],
        specs=specs + ([] if add is None else [cols, cols, lines]),
        out_specs=[cols, cols, lines],
        grid=(steps,),
        flops=37 * 10**8,
        move=14 * 10**6,
    )


def back_at_tokens(fold, back_din, dispatch, residual, small, cotangent, router_part):
    rows, width = residual.shape

    def body(one_ref, two_ref, last_ref, back_ref, disp_ref, res_ref, small_ref, dy_ref, part_ref, dres_ref, br_ref):
        d_ffn = one_ref[...].astype(WIDE) + two_ref[0].astype(WIDE) + last_ref[...].astype(WIDE)
        d_ffn = d_ffn + matmul(disp_ref[...], back_ref[...])
        residual_val = res_ref[...]
        inverse = inverse_rms(residual_val)
        gain = small_ref[EXPERTS + 1 : EXPERTS + 2, :].astype(WIDE)
        d_res = dy_ref[...].astype(WIDE) + rms_backward(d_ffn, residual_val, inverse, gain)
        dres_ref[...] = d_res
        br_ref[0:rows, :] = d_res.astype(LOW)
        gain_part = jnp.sum(d_ffn * residual_val * inverse, 0, keepdims=True)
        line = lax.broadcasted_iota(jnp.int32, (EXTRA, width), 0)
        extra = jnp.where(line == EXPERTS, gain_part, part_ref[...])
        br_ref[rows:, :] = extra.astype(LOW)

    return run_kernel(
        body,
        [shape_of((rows, width), WIDE), shape_of((rows + EXTRA, width), LOW)],
        [*fold, back_din, dispatch, residual, small, cotangent, router_part],
        flops=3 * 10**8,
        move=5 * 10**6,
    )


def attention_backward(ids, branch, w_out, queries, keys, values, lse, ain, tables, groups):
    heads, length, _ = queries.shape
    rows = length // 4
    block, width = w_out.shape
    tiles = (heads + 1) // 2
    strip = block // groups

    def body(ids_ref, *refs):
        br_refs = refs[:4]
        wo_ref, q_ref, k_ref, v_ref, lse_ref, ain_ref, cc_ref, ss_ref = refs[4:12]
        d_ref, g_ref = refs[12:14]
        da_scr, dk_scr, dv_scr = refs[14:17]
        zero = jnp.zeros((rows, 128), WIDE)
        for k in range(4):
            d_att = contract_cols(br_refs[k][0:rows, :], wo_ref[...]).astype(LOW)
            place = ids_ref[1 + k] * rows
            for t in range(tiles):
                wide = min(128, block - 128 * t)
                if wide < 128:
                    da_scr[t, pl.ds(place, rows), :] = zero.astype(LOW)
                da_scr[t, pl.ds(place, rows), 0:wide] = d_att[:, 128 * t : 128 * t + wide]
        half = lax.broadcasted_iota(jnp.int32, (rows, 128), 1) < 64
        tri = lax.broadcasted_iota(jnp.int32, (rows, rows), 0) >= lax.broadcasted_iota(
            jnp.int32, (rows, rows), 1
        )

        def place_tile(m, span, h, value):
            t = h // 2
            wide = min(128, block - 128 * t)
            if h % 2 == 0:
                d_ref[m, span, 128 * t : 128 * t + wide] = value[:, :wide].astype(LOW)
            else:
                kept = d_ref[m, span, 128 * t : 128 * t + 128].astype(WIDE)
                d_ref[m, span, 128 * t : 128 * t + 128] = jnp.where(half, kept, value).astype(LOW)

        def unturn(value, span):
            return value * cc_ref[span, :] + pltpu.roll(value, 32, 1) * ss_ref[span, :]

        every = range(heads)
        for i in range(4):
            span = slice(i * rows, (i + 1) * rows)
            done = slice(0, i * rows)
            queries_i = [q_ref[h, span, :] for h in every]
            d_atts = [da_scr[h // 2, span, :] for h in every]
            levels = [lse_ref[h, span, :] for h in every]
            diags = [contract_cols(queries_i[h], k_ref[h, span, :]) for h in every]
            d_diags = [contract_cols(d_atts[h], v_ref[h, span, :]) for h in every]
            diags = [jnp.exp(jnp.where(tri, diags[h] - levels[h], NEG)) for h in every]
            inners = [jnp.sum(diags[h] * d_diags[h], -1, keepdims=True) for h in every]
            if i:
                pasts = [contract_cols(queries_i[h], k_ref[h, done, :]) for h in every]
                d_pasts = [contract_cols(d_atts[h], v_ref[h, done, :]) for h in every]
                pasts = [jnp.exp(pasts[h] - levels[h]) for h in every]
                inners = [
                    inners[h] + jnp.sum(pasts[h] * d_pasts[h], -1, keepdims=True) for h in every
                ]
            d_diags = [(diags[h] * (d_diags[h] - inners[h])).astype(LOW) for h in every]
            d_queries = [matmul(d_diags[h], k_ref[h, span, :]) for h in every]
            for h in every:
                dk_scr[h, span, :] = contract_rows(d_diags[h], queries_i[h])
                dv_scr[h, span, :] = contract_rows(diags[h].astype(LOW), d_atts[h])
            if i:
                d_pasts = [(pasts[h] * (d_pasts[h] - inners[h])).astype(LOW) for h in every]
                d_queries = [d_queries[h] + matmul(d_pasts[h], k_ref[h, done, :]) for h in every]
                for h in every:
                    dk_scr[h, done, :] += contract_rows(d_pasts[h], queries_i[h])
                    dv_scr[h, done, :] += contract_rows(pasts[h].astype(LOW), d_atts[h])
            for h in every:
                place_tile(0, span, h, unturn(d_queries[h] * 0.125, span))
        for i in range(4):
            span = slice(i * rows, (i + 1) * rows)
            for h in every:
                d_key = dk_scr[h, span, :]
                place_tile(1, span, h, unturn(d_key + pltpu.roll(d_key, 64, 1), span))
                place_tile(2, span, h, dv_scr[h, span, :])
        for m in range(3):
            grad = contract_rows(ain_ref[...], d_ref[m])
            for f in range(4):
                for e in range(groups):
                    start = f * block + e * strip
                    g_ref[4 * e + f, m] = grad[start : start + strip, :].astype(LOW)

    args = [ids, *branch, w_out, queries, keys, values, lse, ain, *tables]
    return run_kernel(
        body,
        [shape_of((3, length, block), LOW), shape_of((4 * groups, 3, strip, block), LOW)],
        args,
        specs=[SMEM] + [VMEM] * (len(args) - 1),
        scratch=[
            pltpu.VMEM((tiles, length, 128), LOW),
            pltpu.VMEM((heads, length, 128), WIDE),
            pltpu.VMEM((heads, length, 128), WIDE),
        ],
        flops=16 * 10**9,
        move=12 * 10**6,
    )


def late_grads(ids, d_qkv, own_mats, att_parts, branch):
    length, block = d_qkv.shape[1:]
    rows = length // 4
    width = own_mats.shape[1]
    extra = branch[0].shape[0] - rows

    def body(ids_ref, d_ref, w_ref, *refs):
        att_refs, br_refs = (refs[:4], refs[4:8])
        mine_ref, near_ref, mid_ref, gout_ref = refs[8:12]
        for k in range(4):
            span = pl.ds(ids_ref[1 + k] * rows, rows)
            total = contract_cols(d_ref[0, span, :], w_ref[0])
            for m in range(1, 3):
                total = total + contract_cols(d_ref[m, span, :], w_ref[m])
            if k % 2 == 0:
                target = mine_ref if k == 0 else mid_ref
                target[...] = total.astype(LOW)
            else:
                near_ref[k // 2] = total.astype(LOW)
        gout = contract_rows(att_refs[0][...], br_refs[0][0:rows, :])
        small = br_refs[0][rows:, :].astype(WIDE)
        for k in range(1, 4):
            gout = gout + contract_rows(att_refs[k][...], br_refs[k][0:rows, :])
            small = small + br_refs[k][rows:, :].astype(WIDE)
        gout_ref[0:block, :] = gout.astype(LOW)
        gout_ref[block:, :] = small.astype(LOW)

    args = [ids, d_qkv, own_mats, *att_parts, *branch]
    got = run_kernel(
        body,
        [
            shape_of((rows, width), LOW),
            shape_of((2, rows, width), LOW),
            shape_of((rows, width), LOW),
            shape_of((block + extra, width), LOW),
        ],
        args,
        specs=[SMEM] + [VMEM] * (len(args) - 1),
        flops=12 * 10**8,
        move=7 * 10**6,
    )
    return (got[:3], got[3])


def experts_chip(ids, rows_sent, got_dy, other, small, weights, peers, ready):
    width = rows_sent.shape[-1]
    axes = ("ep", "fx")
    own_rows = exchange(rows_sent, "ep").reshape(-1, width)
    own_rows = after(own_rows, *ready)
    din, hid, d_gate, d_up, dyw, weight, part = expert_main(
        ids, own_rows, got_dy, [*weights, *peers], other, small
    )

    def homeward(sent):
        return exchange(sent.reshape(EXPERTS, MOST, width), axes).reshape(-1, width)

    def middle(start):
        return expert_out(after(hid, start), weight, weights[2], peers[2])

    def give(start):
        return expert_weight_grads(after(own_rows, start), dyw, hid, d_gate, d_up, True)

    def outward(out):
        return exchange(out.reshape(EXPERTS // 2, 2, MOST, width), "ep")

    def finish(start, received):
        return expert_weight_grads(
            after(own_rows, start), dyw, hid, d_gate, d_up, False, received
        )

    return (din, part, homeward, middle, outward, give, finish)


def experts_spread(rows_sent, grads_sent, other, router_t, weights):
    ep_count = lax.axis_size("ep")
    weg, weu, wed = weights
    width = rows_sent.shape[1]
    local_count = max(1, EXPERTS // ep_count)
    replicas = max(1, ep_count // EXPERTS)
    groups = EXPERTS // local_count
    gate_cols, up_cols, down_rows = (
        lax.all_gather(weg, SEQ, axis=1, tiled=True),
        lax.all_gather(weu, SEQ, axis=1, tiled=True),
        lax.all_gather(wed, SEQ, axis=0, tiled=True),
    )
    hidden_part = gate_cols.shape[1] // local_count
    gate_local = gate_cols.reshape(width, local_count, hidden_part).transpose(1, 0, 2)
    up_local = up_cols.reshape(width, local_count, hidden_part).transpose(1, 0, 2)
    down_local = down_rows.reshape(local_count, hidden_part, width)

    def spread(buffer):
        last = buffer.shape[-1]
        wide = buffer.reshape(groups, 1, local_count * MOST, last)
        wide = jnp.broadcast_to(wide, (groups, replicas, local_count * MOST, last))
        return exchange(wide.reshape(ep_count, local_count * MOST, last), "ep")

    def collect(buffer):
        last = buffer.shape[-1]
        return jnp.sum(
            exchange(buffer, "ep").astype(WIDE).reshape(groups, replicas, local_count * MOST, last),
            1,
        ).reshape(EXPERTS * MOST, last)

    def owner_layout(received):
        last = received.shape[-1]
        return (
            received.reshape(ep_count, local_count, MOST, last)
            .transpose(1, 0, 2, 3)
            .reshape(local_count, ep_count * MOST, last)
        )

    def source_layout(owned):
        last = owned.shape[-1]
        return (
            owned.reshape(local_count, ep_count, MOST, last)
            .transpose(1, 0, 2, 3)
            .reshape(ep_count, local_count * MOST, last)
        )

    def batched(spec, left_op, right_op):
        return jnp.einsum(spec, left_op, right_op, preferred_element_type=WIDE)

    own_rows = owner_layout(spread(rows_sent))
    got_grads = owner_layout(spread(grads_sent))
    got_other = owner_layout(spread(other[:, None]))
    first = lax.axis_index("ep") // replicas * local_count
    mine = first + jnp.arange(local_count)[:, None, None]
    lane = jnp.arange(EXPERTS)
    logits = batched("lrd,ed->lre", own_rows, router_t)
    hit_mine, hit_other = ((lane == mine).astype(WIDE), (lane == got_other).astype(WIDE))
    got_weight = jax.nn.sigmoid(jnp.sum(logits * (hit_mine - hit_other), -1, keepdims=True))
    gate_val = batched("lrd,ldh->lrh", own_rows, gate_local)
    up_val = batched("lrd,ldh->lrh", own_rows, up_local)
    silu_val, slope_val = silu_grad(gate_val)
    hidden_val = (silu_val * up_val).astype(LOW)
    out_rows = batched("lrh,lhd->lrd", hidden_val, down_local)
    back_out = collect(source_layout((got_weight * out_rows).astype(LOW)))
    grad_hidden = batched("lrd,lhd->lrh", got_grads, down_local)
    row_dot = jnp.sum(hidden_val.astype(WIDE) * grad_hidden, -1, keepdims=True)
    amount = got_weight * (1.0 - got_weight) * row_dot
    d_logits = (amount * (hit_mine - hit_other)).astype(LOW)
    part = jnp.sum(batched("lre,lrd->led", d_logits, own_rows), 0)
    scaled = got_weight * grad_hidden
    own_grads = (got_weight * got_grads.astype(WIDE)).astype(LOW)
    grad_gate = (scaled * up_val * slope_val).astype(LOW)
    grad_up = (scaled * silu_val).astype(LOW)
    din_rows = batched("lrh,ldh->lrd", grad_gate, gate_local)
    din_rows = din_rows + batched("lrh,ldh->lrd", grad_up, up_local)
    din_rows = din_rows + batched("lre,ed->lrd", d_logits, router_t)
    back_din = collect(source_layout(din_rows.astype(LOW)))
    grad_gate_w = batched("lrd,lrh->ldh", own_rows, grad_gate)
    grad_up_w = batched("lrd,lrh->ldh", own_rows, grad_up)
    grad_down_w = batched("lrh,lrd->lhd", hidden_val, own_grads)

    def share(full, axis):
        return lax.psum_scatter(
            full.astype(LOW), SEQ, scatter_dimension=axis, tiled=True
        ).astype(WIDE)

    return (
        back_out.astype(LOW),
        back_din.astype(LOW),
        jnp.pad(part, ((0, EXTRA - EXPERTS), (0, 0))),
        lambda start: (
            share(grad_gate_w.transpose(1, 0, 2).reshape(width, local_count * hidden_part), 1),
            share(grad_up_w.transpose(1, 0, 2).reshape(width, local_count * hidden_part), 1),
            share(grad_down_w.reshape(local_count * hidden_part, width), 0),
        ),
    )


def shards(
    tokens,
    cotangent,
    routes,
    priority,
    gain_attn,
    w_query,
    w_key,
    w_value,
    w_out,
    gain_ffn,
    w_shared_gate,
    w_shared_up,
    w_shared_down,
    w_router,
    w_expert_gate,
    w_expert_up,
    w_expert_down,
):
    tok_rows, width = tokens.shape
    rows_w = w_query.shape[0]
    fs_count = lax.axis_size("fx") * lax.axis_size("fc")
    ep_count = lax.axis_size("ep")
    devices = ep_count * fs_count
    seq_len = tok_rows * fs_count
    head_size = width // HEADS
    side, core = (lax.axis_index("fx"), lax.axis_index("fc"))
    fs_index = side * lax.axis_size("fc") + core
    my_rank = lax.axis_index("ep") * fs_count + fs_index
    my_expert = lax.axis_index("ep") * lax.axis_size("fx") + side
    ids = [core] + [fs_index ^ k for k in range(4)] + [my_expert, lax.axis_index("ep"), side]
    ids = jnp.stack(ids).astype(jnp.int32)

    small_own = jnp.concatenate([w_router.T, gain_attn[None], gain_ffn[None]], 0)
    small_own = jnp.pad(small_own, ((0, EXTRA - EXPERTS - 2), (0, width - rows_w)))
    pack = jnp.concatenate([tokens, small_own])
    facts_far = far_of(jnp.concatenate([routes.T, priority[None]]))
    dy_far = far_of(cotangent)
    pack_far = far_of(after(pack, facts_far))
    qkv_stack = jnp.stack([w_query, w_key, w_value])
    qkv_cut = [
        lax.dynamic_slice_in_dim(qkv_stack, (fs_index ^ k) * rows_w, rows_w, 2) for k in range(4)
    ]

    def to_place(parts):
        got = [
            lax.ppermute(parts[k], SEQ, [(i, i ^ k) for i in range(fs_count)]) for k in (2, 3, 1)
        ]
        return (parts[0], got[2], got[0], got[1])

    w_parts = to_place(qkv_cut)
    x_parts = (pack, near_of(pack), pack_far, near_of(pack_far))

    lane = jnp.arange(2 * EXPERTS)
    zero_row = jnp.zeros((EXPERTS,), WIDE)
    lower = (jnp.arange(tok_rows)[:, None] > jnp.arange(tok_rows)[None, :]).astype(LOW)
    slot_iota = jnp.arange(EXPERTS * MOST)
    half_iota = jnp.arange(EXPERTS * MOST // 2)

    def plan(block_routes, block_priority):
        classes = jnp.stack([block_priority, 1 - block_priority], 1)
        named = block_routes + EXPERTS * classes
        hits = [(named[:, j : j + 1] == lane).astype(WIDE) for j in (0, 1)]
        both = hits[0] + hits[1]
        before = matmul(lower, both.astype(LOW))
        counts = jnp.sum(both, 0)
        local_table = before + jnp.concatenate([zero_row, counts[:EXPERTS]])
        ranks = [jnp.sum(local_table * hits[j], -1).astype(jnp.int32) for j in (0, 1)]
        return (hits, before, counts, ranks)

    def keep_of(block_plan, base):
        hits, before = block_plan[:2]
        capacity = 5 * tok_rows * devices // 32
        return [(jnp.sum((before + base) * hits[j], -1) < capacity).astype(LOW) for j in (0, 1)]

    def base_of(all_counts, rank):
        earlier = (jnp.arange(devices) < rank).astype(WIDE)
        base = jnp.sum(all_counts * earlier[:, None], 0)
        return base + jnp.concatenate([zero_row, jnp.sum(all_counts[:, :EXPERTS], 0)])

    own_plan = plan(routes, priority)
    counts, ranks = own_plan[2:]
    slot_hit = [
        ((routes[:, j] * MOST + ranks[j])[:, None] == slot_iota).astype(LOW) for j in (0, 1)
    ]
    dispatch = slot_hit[0] + slot_hit[1]
    others = jnp.stack([routes[:, 1], routes[:, 0]]).astype(LOW)
    other_sent = matmul(others[0:1], slot_hit[0]) + matmul(others[1:2], slot_hit[1])
    other_sent = other_sent.reshape(EXPERTS, MOST)
    pair_of_cores = EXPERTS == ep_count * lax.axis_size("fx")
    if pair_of_cores:
        tiny = jnp.concatenate(
            [jnp.broadcast_to(counts[None], (EXPERTS, 2 * EXPERTS)), other_sent], 1
        )
        tiny = jnp.pad(tiny, ((0, 0), (0, 128 - tiny.shape[1]))).astype(jnp.int32)
        tiny = jnp.broadcast_to(tiny[:, None], (EXPERTS, 2, 128)).reshape(devices, 1, 128)
        far_routes = facts_far[:2].T
        far_plan = plan(far_routes, facts_far[2])

        def side_hit(block_routes, block_ranks, j):
            place = (block_routes[:, j] >> 1) * MOST + block_ranks[j]
            same = (block_routes[:, j] & 1) == side
            return ((place[:, None] == half_iota) & same[:, None]).astype(LOW)

        own_side = [side_hit(routes, ranks, j) for j in (0, 1)]
        far_side = [side_hit(far_routes, far_plan[3], j) for j in (0, 1)]
        side_hits = (own_side[0] + own_side[1], far_side[0] + far_side[1])
        dy_sent = send_pair(ids, side_hits, (cotangent, dy_far))
        got_dy = exchange(dy_sent, "ep").reshape(-1, width)
        tiny_got = exchange(after(tiny, got_dy), ALL)
        all_counts = tiny_got[:, 0, : 2 * EXPERTS].astype(WIDE)
        other = lax.dynamic_index_in_dim(tiny_got.reshape(EXPERTS, 2, 128), core, 1, keepdims=False)
        other = other[:, 2 * EXPERTS : 2 * EXPERTS + MOST].reshape(EXPERTS * MOST, 1)
        far_keep = keep_of(far_plan, base_of(all_counts, my_rank ^ 2))
        own_keep = keep_of(own_plan, base_of(all_counts, my_rank))

        side_kept = (
            own_side[0] * own_keep[0][:, None] + own_side[1] * own_keep[1][:, None],
            far_side[0] * far_keep[0][:, None] + far_side[1] * far_keep[1][:, None],
        )
    else:
        spread_counts = jnp.broadcast_to(counts.astype(jnp.int32), (devices, 2 * EXPERTS))
        all_counts = exchange(spread_counts, ALL).astype(WIDE)
        kept = keep_of(own_plan, base_of(all_counts, my_rank))
        dispatch_kept = slot_hit[0] * kept[0][:, None] + slot_hit[1] * kept[1][:, None]

    forward_table, cos_table, sin_table = rope_constants(seq_len, head_size // 2)
    weights = (w_expert_gate, w_expert_up, w_expert_down)
    up_stack = jnp.stack([w_shared_gate, w_shared_up])
    ff_part = w_shared_gate.shape[1] // fs_count
    up_own = lax.dynamic_slice_in_dim(up_stack, side * 2 * ff_part, 2 * ff_part, 2)
    up_give = lax.dynamic_slice_in_dim(up_stack, (1 - side) * 2 * ff_part, 2 * ff_part, 2)

    def core_cut(piece, which):
        return lax.dynamic_slice_in_dim(piece, which * ff_part, ff_part, 2)

    up_mine, up_other = (core_cut(up_own, core), core_cut(up_own, 1 - core))
    ready = (*x_parts[1:], *w_parts[1:])
    out_far = far_of(after(w_out, *ready))
    out_near, dy_near = (near_of(piece) for piece in tie((w_out, cotangent), *ready))
    up_near = near_of(after(up_other, *ready))
    peers = []
    if pair_of_cores:
        peers = [near_of(piece) for piece in tie(weights, *ready)]
    ain, own_mats, (queries, keys, values), lse, att_own, small = attention_forward(
        ids, x_parts, w_parts, jnp.asarray(forward_table)
    )
    out_parts = (w_out, out_near, out_far, near_of(after(out_far, att_own[0])))
    att_parts = tie(to_place(att_own), *out_parts[1:])
    residual, ffn_input = after_attention(att_parts, out_parts, tokens, small)
    ffn_far = far_of(ffn_input)
    dy_parts = (cotangent, dy_near, dy_far, near_of(after(dy_far, ffn_far)))
    ffn_parts = (ffn_input, near_of(ffn_input), ffn_far, near_of(ffn_far))
    up_far = far_of(after(up_give, ffn_far))

    def shared():
        up_last = near_of(core_cut(up_far, 1 - core))
        up_parts = (up_mine, up_near, core_cut(up_far, core), up_last)
        return shared_branch(
            ids,
            ffn_parts,
            dy_parts,
            up_parts,
            w_shared_down,
            ep_count if pair_of_cores else 0,
        )

    def fold(parts):
        mine, give, mid = parts
        got = near_of(give)
        return (mine, got, far_of((mid.astype(WIDE) + got[1].astype(WIDE)).astype(LOW)))

    def ep_step(block, bit):
        return lax.ppermute(block, "ep", [(i, i ^ bit) for i in range(ep_count)])

    def added(first, second):
        return (first.astype(WIDE) + second.astype(WIDE)).astype(LOW)

    if pair_of_cores:
        got_dy = after(got_dy, *peers)
        rows_sent = send_pair(ids, tie(side_kept, got_dy), (ffn_input, ffn_far))
        din_sums, out_sums, (grads_keep, grads_give) = shared()
        grads_got = ep_step(grads_give, 2)
        din_sent, router_part, homeward, middle, outward, give_grads, last = experts_chip(
            ids, rows_sent, got_dy, other, small, weights, peers, (grads_keep,)
        )
        din_fold = fold(din_sums)
        half = added(grads_keep, after(grads_got, din_sent))
        back_din = homeward(after(din_sent, half))
        half_got = ep_step(half[1::2], 1)
        expert_out_rows = middle(half)
        out_near_sum = near_of(after(out_sums[1], half))
        back_din = after(back_din, out_near_sum)
        back_din = after(back_din, half_got)
        quarter = added(half[0::2], half_got)
        quarter_got = ep_step(quarter[1:2], 4)
    else:
        dy_sent = contract_rows(dispatch, cotangent).astype(LOW)
        rows_sent = contract_rows(dispatch_kept, ffn_input).astype(LOW)
        back_out, back_din, router_part, expert_grads = experts_spread(
            rows_sent, dy_sent, other_sent.reshape(-1), small[:EXPERTS], weights
        )
        din_sums, out_sums, grads_rest = shared()
        din_fold = fold(din_sums)

    grad_resid, branch = back_at_tokens(
        din_fold, back_din, dispatch, residual, small, cotangent, router_part
    )
    branch_far = far_of(branch)
    branch_pair = (branch, branch_far)
    if pair_of_cores:
        own_chunk = added(quarter[0:1], after(quarter_got, branch))
        branch_pair = tie(branch_pair, own_chunk)
        back_out = outward(after(expert_out_rows, own_chunk, branch_far))
    branch_near, branch_last = (near_of(piece) for piece in branch_pair)
    branch_parts = (branch, branch_near, branch_far, branch_last)
    d_qkv, grads_qkv = attention_backward(
        ids, branch_parts, w_out, queries, keys, values, lse, ain, (cos_table, sin_table), ep_count if pair_of_cores else 1
    )
    strip = rows_w // ep_count
    grads_qkv = after(grads_qkv, back_out)
    if pair_of_cores:
        qkv_blocks = grads_qkv
    else:
        qkv_blocks = grads_qkv.transpose(1, 0, 2, 3).reshape(3, fs_count, ep_count, strip, rows_w)
        qkv_blocks = qkv_blocks.transpose(2, 1, 0, 3, 4).reshape(devices, 3, strip, rows_w)
    qkv_got = exchange(qkv_blocks, ALL)
    din_parts, grad_out_w = late_grads(ids, d_qkv, own_mats, att_own, branch_parts)
    in_fold = fold(din_parts)
    own_float = tokens.astype(WIDE)
    grad_in = in_fold[0].astype(WIDE) + in_fold[1][0].astype(WIDE) + in_fold[2].astype(WIDE)
    gain_one = small[EXPERTS : EXPERTS + 1].astype(WIDE)
    grad_tokens = grad_resid + rms_backward(grad_in, own_float, inverse_rms(own_float), gain_one)

    if not pair_of_cores:
        out_fold = fold(out_sums)
        total = residual + out_fold[0].astype(WIDE) + out_fold[1][0].astype(WIDE)
        total = total + out_fold[2].astype(WIDE) + matmul(dispatch, back_out)
        output = total.astype(LOW)
    qkv_got = qkv_got.reshape(ep_count, fs_count, 3, strip, rows_w).astype(WIDE)
    qkv_sum = jnp.sum(qkv_got, 0).transpose(1, 2, 0, 3).reshape(3 * strip, width).astype(LOW)
    small_part = lax.dynamic_slice_in_dim(grad_out_w[rows_w:], fs_index * rows_w, rows_w, 1)
    if pair_of_cores:
        lines = EXTRA * rows_w // (ep_count * width)
        parts = jnp.concatenate(
            [
                grad_out_w[:rows_w].reshape(ep_count, strip, width),
                small_part.reshape(ep_count, lines, width),
            ],
            1,
        )
        cut = 2 * rows_w // ep_count
        turned = to_place([own_chunk[0, k * cut : (k + 1) * cut] for k in range(4)])
        whole = jnp.concatenate([*turned, own_chunk[0, 4 * cut :]])[None]
        for bit, far_bit in ((1, 4), (2, 2)):
            keep, give = split_part(parts, bit)
            got, whole_got = (ep_step(give, bit), ep_step(whole, far_bit))
            if bit == 1:
                got, whole_got, in_last = lax.optimization_barrier((got, whole_got, in_fold[2]))
                own_total, far_total = take_pair(
                    ids, side_hits, after(back_out, got), out_sums, out_near_sum, residual
                )
                out_got = far_of(far_total)
            else:
                got, whole_got, out_got = lax.optimization_barrier((got, whole_got, out_got))
            parts = added(keep, got)
            whole = jnp.concatenate([whole, whole_got])
        keep, give = split_part(parts, 4)
        whole_got = ep_step(whole, 1)
        out_sum = added(keep, ep_step(give, 4))[0]
        output = (own_total + out_got.astype(WIDE)).astype(LOW)
    else:
        lines = 0
        out_whole = lax.psum((grad_out_w[:rows_w], small_part), "ep")
        out_sum = jnp.zeros((0, width), LOW)
    sums = jnp.concatenate([qkv_sum, out_sum])
    sums_sent = jnp.broadcast_to(sums[None], (ep_count,) + sums.shape)
    sums = exchange(sums_sent, "ep")
    mats = (w_query, w_key, w_value)
    if pair_of_cores:
        *qkv_all, sum_out_w, gain_col = place_dense(sums, mats, gain_attn[:, None], strip)
        sum_gain_one = gain_col[:, 0]
        sum_small = sums[:, 4 * strip : 4 * strip + lines].astype(WIDE).reshape(EXTRA, rows_w)
    else:
        sums = sums.astype(WIDE)
        qkv_all = sums.reshape(ep_count, 3, strip, width)
        qkv_all = qkv_all.transpose(1, 0, 2, 3).reshape(3, rows_w, width)
        sum_out_w, sum_small = (piece.astype(WIDE) for piece in out_whole)
        sum_gain_one = sum(
            jnp.sum(qkv_all[i] * mat.astype(WIDE), -1) for i, mat in enumerate(mats)
        )
        sum_gain_one = sum_gain_one / gain_attn.astype(WIDE)
    sum_router, sum_gain_two = (sum_small[:EXPERTS].T, sum_small[EXPERTS])
    if pair_of_cores:
        whole_got, *given = lax.optimization_barrier((whole_got, *give_grads(sums_sent)))
        expert_grads = last(qkv_blocks, [near_of(piece) for piece in given])
        whole = [whole, whole_got]
        sum_sgate, sum_sup, sum_sdown = place_shared(ids, whole, rows_w, width)
    else:
        expert_grads = expert_grads(grads_qkv)
        dense = lax.psum((*to_place(grads_rest[:4]), grads_rest[4]), "ep")
        sum_sdown = dense[4].astype(WIDE)
        wide_rel = jnp.stack([piece.astype(WIDE) for piece in dense[:4]])
        wide_all = jnp.concatenate(
            [
                lax.dynamic_index_in_dim(wide_rel, fs_index ^ k, 0, keepdims=False)
                for k in range(4)
            ],
            2,
        )
        sum_sgate, sum_sup = (wide_all[0], wide_all[1])
    return (
        output,
        grad_tokens,
        sum_gain_one,
        qkv_all[0],
        qkv_all[1],
        qkv_all[2],
        sum_out_w,
        sum_gain_two,
        sum_sgate,
        sum_sup,
        sum_sdown,
        sum_router,
        *expert_grads,
    )


def solution(mesh):
    ep_count, fs_count = mesh.devices.shape
    cut_mesh = Mesh(mesh.devices.reshape(ep_count, fs_count // 2, 2), ALL)
    tok = P(ALL, None)
    row = P(SEQ, None)
    return jax.shard_map(
        shards,
        mesh=cut_mesh,
        in_specs=(
            tok,
            tok,
            tok,
            P(ALL),
            P(SEQ),
            row,
            row,
            row,
            row,
            P(SEQ),
            row,
            row,
            row,
            row,
            P(None, ALL),
            P(None, ALL),
            tok,
        ),
        out_specs=(
            tok,
            tok,
            P(SEQ),
            row,
            row,
            row,
            row,
            P(SEQ),
            row,
            row,
            row,
            row,
            P(None, ALL),
            P(None, ALL),
            tok,
        ),
        check_vma=False,
    )
```
